128 devices in a mesh: leaf: 32 (over x, z, y_lo), grid: 4 (over y_hi, core).
Axes of the slice: x: 4, y: 4 (y_hi: 2, y_lo: 2; y = y_hi * 2 + y_lo), z: 4, core: 2. Of those that a mesh axis runs over, the one named last changes fastest.
Arguments:
- rhs_rows: float32 [65536, 256], P(('leaf', 'grid')), may hold values from -6 to 6
- order: int32 [65536], P(('leaf', 'grid')), may hold values from 0 to 511, as said below
- leaf_inverse: float32 [65536, 2048], P('leaf', 'grid'), as said below
- leaf_panels: float32 [32, 6, 1024, 2048], P('leaf', None, None, 'grid'), may hold values from -0.0234375 to 0.0234375
- panel_mask: int32 [32, 6, 16], P('leaf', None, 'grid'), may hold values 0 or 1
- sep_rhs: float32 [32, 1024, 256], P('leaf', None, 'grid'), may hold values from -6 to 6
- sep_inverse: float32 [32, 1024, 1024], P('leaf'), as said below
- sep_panels: float32 [32, 5, 1024, 1024], P('leaf'), may hold values from -0.03125 to 0.03125
Outputs:
- leaf_solution: float32 [65536, 256], P(('leaf', 'grid'))
- sep_solution: float32 [32, 1024, 256], P('leaf', None, 'grid')
- widths: float32 [256], P('grid')
The draws below stay inside these ranges and needn't reach their ends.
Inputs may be any that keep to these rules, and one draw needn't show every extreme that they name: Each row block of 512 entries of order is a permutation of 0 .. 511. Each leaf's block of leaf_inverse is lower triangular. Each separator's block of sep_inverse is lower triangular.
All inputs are finite; a program needn't handle non-finite values. No bound on the sum of `panel_mask` on one device may be relied on, other than what follows from the above.
Results may differ from the reference program's by a relative error of at most 0.0001.
Values sent between devices are 32-bit elements; how exact they have to be, the bound alone decides.
A program may use at most 192 MiB of HBM per device.

```python
import jax
import jax.numpy as jnp
import numpy as np
from jax import lax

COLUMNS = 256
LEAF_ROWS = 2048
SEP_ROWS = 1024
LEVELS = 5
TIERS = 6
BLOCKS = 128
BLOCK_ROWS = 512
SLOTS = 4
ALL_LEAF_ROWS = 65536
MASK_BLOCKS = 16
N_LEAF = 32


def lower_block(noise, diagonal, rows_total, order_size):
    local = jax.lax.broadcasted_iota(jnp.int32, (rows_total, order_size), 0) % order_size
    column = jax.lax.broadcasted_iota(jnp.int32, (rows_total, order_size), 1)
    return jnp.where(column < local, noise, jnp.where(column == local, diagonal, 0.0))


def draw_order(key, part):
    key = jax.random.fold_in(key, 3)
    keys = jax.random.split(key, BLOCKS)
    shuffled = jax.vmap(lambda single: jax.random.permutation(single, BLOCK_ROWS))(keys)
    return shuffled.reshape(-1).astype(jnp.int32)


def draw_leaf_inverse(key, part):
    key = jax.random.fold_in(key, 5)
    first, second = jax.random.split(key)
    shape = (ALL_LEAF_ROWS, LEAF_ROWS)
    noise = jax.random.normal(first, shape, jnp.float32) * (0.8 / LEAF_ROWS ** 0.5)
    diagonal = jax.random.uniform(second, shape, jnp.float32, 0.6, 1.4)
    return lower_block(noise, diagonal, ALL_LEAF_ROWS, LEAF_ROWS)


def draw_sep_inverse(key, part):
    key = jax.random.fold_in(key, 7)
    first, second = jax.random.split(key)
    shape = (N_LEAF * SEP_ROWS, SEP_ROWS)
    noise = jax.random.normal(first, shape, jnp.float32) * (0.8 / SEP_ROWS ** 0.5)
    diagonal = jax.random.uniform(second, shape, jnp.float32, 0.6, 1.4)
    return lower_block(noise, diagonal, N_LEAF * SEP_ROWS, SEP_ROWS).reshape(N_LEAF, SEP_ROWS, SEP_ROWS)


def set_ends(entries, own_key, smallest, top_value):
    index_at = [jax.random.randint(jax.random.fold_in(own_key, axis), (), 0, length) for axis, length in enumerate(entries.shape)]
    widest = entries.shape.index(max(entries.shape))
    beside = index_at[:widest] + [(index_at[widest] + 1) % entries.shape[widest]] + index_at[widest + 1:]
    return entries.at[tuple(index_at)].set(smallest).at[tuple(beside)].set(top_value)


def level_of(rng, dims, cuts, smallest, largest):
    level, own = 1.0, jax.random.fold_in(rng, 6)
    for axis_at, shards_of in cuts:
        heights = jnp.exp(jax.random.uniform(jax.random.fold_in(own, axis_at), (shards_of,), jnp.float32, smallest / len(cuts), largest / len(cuts)))
        level = level * jnp.repeat(heights, dims[axis_at] // shards_of).reshape([-1 if axis == axis_at else 1 for axis in range(len(dims))])
    return level


def gaussian(rng, dims, scale, reach, cuts=(), held_as=jnp.bfloat16):
    values = scale * jax.random.normal(rng, dims, jnp.float32)
    if cuts:
        values = values * level_of(rng, dims, cuts, -0.22, 0.18)
    return jnp.clip(values, -reach, reach).astype(held_as)


def setup_inputs(seed: int = 0) -> dict:
    seeds = jax.random.split(jax.random.key(seed), 9)
    rhs_rows = gaussian(seeds[0], (ALL_LEAF_ROWS, COLUMNS), 1.0, 6.0, ((0, 128),), jnp.float32)
    order = draw_order(jax.random.fold_in(seeds[8], 71), 0)
    leaf_inverse = draw_leaf_inverse(jax.random.fold_in(seeds[8], 71), 0)
    leaf_panels = gaussian(seeds[3], (N_LEAF, TIERS, SEP_ROWS, LEAF_ROWS), (LEAF_ROWS * N_LEAF) ** -0.5, 0.0234375, ((0, 32), (3, 4)), jnp.float32)
    panel_mask = set_ends((jax.random.randint(seeds[4], (N_LEAF, TIERS, MASK_BLOCKS), 0, 4) < 3).astype(jnp.int32), jax.random.fold_in(seeds[4], 1), 0, 1)
    sep_rhs = gaussian(seeds[5], (N_LEAF, SEP_ROWS, COLUMNS), 1.0, 6.0, ((0, 32), (2, 4)), jnp.float32)
    sep_inverse = draw_sep_inverse(jax.random.fold_in(seeds[8], 71), 0)
    sep_panels = gaussian(seeds[7], (N_LEAF, LEVELS, SEP_ROWS, SEP_ROWS), (SEP_ROWS * N_LEAF) ** -0.5, 0.03125, ((0, 32),), jnp.float32)
    return {"rhs_rows": rhs_rows, "order": order, "leaf_inverse": leaf_inverse, "leaf_panels": leaf_panels, "panel_mask": panel_mask, "sep_rhs": sep_rhs, "sep_inverse": sep_inverse, "sep_panels": sep_panels}


def host_of(index, tier):
    return index // 2 ** tier * 2 ** tier + 2 ** (tier - 1) - 1

def reference(rhs_rows, order, leaf_inverse, leaf_panels, panel_mask, sep_rhs, sep_inverse, sep_panels):
    highest = lax.Precision.HIGHEST
    source = jnp.arange(BLOCKS, dtype=jnp.int32)[:, None] * BLOCK_ROWS + order.reshape(BLOCKS, BLOCK_ROWS).astype(jnp.int32)
    source = source.reshape(BLOCKS, BLOCKS, SLOTS).transpose(1, 0, 2).reshape(-1)
    permuted = rhs_rows[source]
    blocks = permuted.reshape(N_LEAF, LEAF_ROWS, COLUMNS)
    inverse = leaf_inverse.reshape(N_LEAF, LEAF_ROWS, LEAF_ROWS)
    leaf_y = jnp.einsum('nij,njk->nik', inverse, blocks, precision=highest)
    column_mask = jnp.repeat(panel_mask.astype(jnp.float32), 128, axis=2)
    leaves = np.arange(N_LEAF)
    update = jnp.zeros((N_LEAF, SEP_ROWS, COLUMNS), jnp.float32)
    for tier in range(1, TIERS + 1):
        masked = leaf_panels[:, tier - 1] * column_mask[:, tier - 1, None, :]
        contrib = jnp.einsum('nsj,njk->nsk', masked, leaf_y, precision=highest)
        update = update.at[host_of(leaves, tier)].add(contrib)
    level = np.ones(N_LEAF, dtype=np.int64)
    for bit in range(1, TIERS):
        level = level + ((leaves + 1) % 2 ** bit == 0)
    sep_y = jnp.zeros((N_LEAF, SEP_ROWS, COLUMNS), jnp.float32)
    for tier in range(1, TIERS + 1):
        hosts = leaves[level == tier]
        rhs = sep_rhs[hosts] - update[hosts]
        solved = jnp.einsum('hij,hjk->hik', sep_inverse[hosts], rhs, precision=highest)
        sep_y = sep_y.at[hosts].set(solved)
        for step in range(TIERS - tier):
            target = host_of(hosts, tier + 1 + step)
            term = jnp.einsum('hij,hjk->hik', sep_panels[hosts, step], solved, precision=highest)
            update = update.at[target].add(term)
    total = lax.optimization_barrier(jnp.sum(leaf_y * leaf_y, axis=(0, 1))) + lax.optimization_barrier(jnp.sum(sep_y * sep_y, axis=(0, 1)))
    widths = jnp.sqrt(total / (N_LEAF * (LEAF_ROWS + SEP_ROWS)) + 1e-06)
    return (leaf_y.reshape(ALL_LEAF_ROWS, COLUMNS), sep_y, widths)
```

```python
import jax
import jax.numpy as jnp
from jax import lax
from jax.experimental import pallas as pl
from jax.experimental.pallas import tpu as pltpu
from jax.sharding import PartitionSpec as P

F32, BF16 = jnp.float32, jnp.bfloat16
MESH = pl.DeviceIdType.MESH
DMA = pltpu.SemaphoreType.DMA


def split(value):
    high = value.astype(BF16)
    return high, (value - high.astype(F32)).astype(BF16)


def dot(a, b):
    return jnp.dot(a, b, preferred_element_type=F32)


def dot3(a, b_high, b_low):
    high, low = split(a)
    return dot(high, b_high) + dot(high, b_low) + dot(low, b_high)


def lane_left(shape):
    return lax.broadcasted_iota(jnp.int32, shape, 1) < 64


def turned(value):
    return pltpu.roll(value, 64, 1)


def packed_pair(top, bottom):
    left = lane_left(top.shape)
    return jnp.where(left, top, turned(bottom)), jnp.where(left, turned(top), bottom)


def unpacked(value):
    left = lane_left(value.shape)
    other = turned(value)
    return jnp.where(left, value, other), jnp.where(left, other, value)


def rows(start, size, unit=8):
    if isinstance(start, int):
        return pl.ds(start, size)
    return pl.ds(pl.multiple_of(start, unit), size)


def kernel(order_ref, mask_ref, rhs_ref, linv_hbm, lpan_hbm, srhs_hbm, sinv_hbm, span_hbm,
           leafy_hbm, sol_hbm, width_ref,
           abuf, xbuf, xh, xl, lbuf, zs, zr, za, ybuf, yh_s, yl_s, pbuf, own, snd, rcv, zrs,
           pk12, pk3, ubuf, accp, pend, rhsv, rhsp, vcat, vh0, solv, invb, spb, csend, crecv, wsend, wrecv,
           ld_sem, lp_sem, sp_sem, a2a_sem, zs_sem, zr_sem, za_sem, us_sem, ur_sem, rs_sem, rr_sem,
           ps_sem, p3_sem, u_sem, cs_sem, cr_sem, w_sem, out_sem):
    leaf = lax.axis_index("leaf")
    grid = lax.axis_index("grid")
    me = leaf * 4 + grid
    yl = lax.rem(leaf, 2)
    z = lax.rem(lax.div(leaf, 2), 4)
    x = lax.div(leaf, 8)
    yh = lax.div(grid, 2)
    c = lax.rem(grid, 2)
    sib = yh * 2 + 1 - c

    level = jnp.int32(1)
    for bit in range(1, 6):
        level = level + (lax.rem(leaf + 1, 2 ** bit) == 0).astype(jnp.int32)
    parent = jnp.int32(0)
    for tier in range(1, 6):
        size = 2 ** (tier + 1)
        parent = jnp.where(level == tier, lax.div(leaf, size) * size + 2 ** tier - 1, parent)
    side = (leaf > parent).astype(jnp.int32)
    n_pan = 6 - level

    l_copy = pltpu.make_async_copy(linv_hbm, lbuf, ld_sem.at[0])
    l_copy.start()
    inv_copy = pltpu.make_async_copy(sinv_hbm, invb, ld_sem.at[1])
    srhs_copy = pltpu.make_async_copy(srhs_hbm, rhsv, ld_sem.at[2])

    def lp_copy(t):
        return pltpu.make_async_copy(lpan_hbm.at[t], pbuf.at[t % 3], lp_sem.at[t % 3])

    def sp_copy(m):
        slot = lax.rem(m, 3)
        return pltpu.make_async_copy(span_hbm.at[m], spb.at[slot], sp_sem.at[slot])

    rh, rl = split(rhs_ref[...])
    for part in range(4):
        index = order_ref[rows(part * 256, 256), :]
        hot = (lax.broadcasted_iota(jnp.int32, (256, 512), 1) == index).astype(BF16)
        got = dot(hot, rh) + dot(hot, rl)
        upper = lax.rem(lax.broadcasted_iota(jnp.int32, (256, 128), 0), 8) < 4
        abuf[rows(part * 256, 256), :] = jnp.where(upper, got[:, :128], got[:, 128:])

    barrier = pltpu.get_barrier_semaphore()

    def greet(k, carry):
        d = lax.rem(me + k, 128)
        pl.semaphore_signal(barrier, inc=1, device_id=(lax.div(d, 4), lax.rem(d, 4)), device_id_type=MESH)
        return carry

    lax.fori_loop(1, 128, greet, 0)
    for t in range(3):
        lp_copy(t).start()
    srhs_copy.start()
    pl.semaphore_wait(barrier, 127)

    def a2a(k, carry):
        d = lax.rem(me + k, 128)
        pltpu.make_async_remote_copy(
            src_ref=abuf.at[rows(d * 8, 8)], dst_ref=xbuf.at[rows(me * 8, 8)],
            send_sem=a2a_sem.at[0], recv_sem=a2a_sem.at[1],
            device_id=(lax.div(d, 4), lax.rem(d, 4)), device_id_type=MESH).start()
        return carry

    lax.fori_loop(1, 128, a2a, 0)
    xbuf[rows(me * 8, 8), :] = abuf[rows(me * 8, 8), :]
    inv_copy.start()
    for m in range(3):
        @pl.when(m < n_pan)
        def _():
            sp_copy(jnp.int32(m)).start()
    pltpu.make_async_copy(xbuf.at[pl.ds(0, 1016)], xbuf.at[pl.ds(0, 1016)], a2a_sem.at[1]).wait()

    raw = xbuf[...].reshape(64, 2, 8, 128)
    first, second = raw[:, 0], raw[:, 1]
    upper = lax.broadcasted_iota(jnp.int32, (64, 8, 128), 1) < 4
    left = jnp.where(upper, first, pltpu.roll(second, 4, 1)).reshape(512, 128)
    right = jnp.where(upper, pltpu.roll(first, 4, 1), second).reshape(512, 128)
    for half, value in enumerate((left, right)):
        high, low = split(value)
        xh[:, half * 128:(half + 1) * 128] = high
        xl[:, half * 128:(half + 1) * 128] = low

    l_copy.wait()

    def leaf_block(r, dst):
        def body(i, carry):
            dst[rows(i * 256, 256), :] = dot3(lbuf[rows(r * 512 + i * 256, 256), :], xh[...], xl[...])
            return carry
        lax.fori_loop(0, 2, body, 0)

    def to_sibling(slot):
        return pltpu.make_async_remote_copy(
            src_ref=zs.at[slot], dst_ref=zr.at[slot], send_sem=zs_sem.at[slot], recv_sem=zr_sem.at[slot],
            device_id=(leaf, sib), device_id_type=MESH)

    def across():
        return pltpu.make_async_remote_copy(
            src_ref=zs.at[2], dst_ref=za, send_sem=zs_sem.at[2], recv_sem=za_sem,
            device_id=(leaf, 2 + c), device_id_type=MESH)

    @pl.when(yh == 0)
    def _():
        leaf_block(3 - c, zs.at[0])
        to_sibling(0).start()
        leaf_block(2 + c, zs.at[2])
        to_sibling(0).wait_recv()
        zs[2] = zs[2] + zr[0]
        across().start()

        @pl.when(c == 0)
        def _():
            leaf_block(1, zs.at[1])
            to_sibling(1).start()

    @pl.when((yh == 1) & (c == 0))
    def _():
        leaf_block(3, zs.at[1])
        to_sibling(1).start()

    leaf_block(grid, ybuf)

    @pl.when(c == 1)
    def _():
        to_sibling(1).wait_recv()
        ybuf[...] = ybuf[...] + zr[1]

    @pl.when(yh == 1)
    def _():
        across().wait_recv()
        ybuf[...] = ybuf[...] + za[...]

    y_out = pltpu.make_async_copy(ybuf, leafy_hbm, out_sem.at[0])
    y_out.start()

    y_left, y_right = ybuf[:, :128], ybuf[:, 128:]
    for_0, for_1 = packed_pair(y_left, y_right)
    mine = jnp.where(c == 0, for_0, for_1)
    other = jnp.where(c == 0, for_1, for_0)
    own[0, pl.ds(1024, 8), :] = jnp.broadcast_to(jnp.sum(mine * mine, axis=0, keepdims=True), (8, 128))
    snd[0, pl.ds(1024, 8), :] = jnp.broadcast_to(jnp.sum(other * other, axis=0, keepdims=True), (8, 128))
    for half, value in enumerate((mine, other)):
        high, low = split(value)
        yh_s[:, half * 128:(half + 1) * 128] = high
        yl_s[:, half * 128:(half + 1) * 128] = low

    def u_copy(t):
        size = 1032 if t == 0 else 1024
        return pltpu.make_async_remote_copy(
            src_ref=snd.at[t, pl.ds(0, size)], dst_ref=rcv.at[t, pl.ds(0, size)],
            send_sem=us_sem.at[t], recv_sem=ur_sem.at[t], device_id=(leaf, sib), device_id_type=MESH)

    def send_pieces(src, base, size, to_leaf, sems, recv_sem):
        for to_yh in range(2):
            to_me = (to_leaf == leaf) & (yh == to_yh)

            @pl.when(to_me)
            def _():
                ubuf[rows(base, size), :] = src[to_yh]

            @pl.when(jnp.logical_not(to_me))
            def _():
                pltpu.make_async_remote_copy(
                    src_ref=src.at[to_yh], dst_ref=ubuf.at[rows(base, size)],
                    send_sem=sems.at[to_yh], recv_sem=recv_sem,
                    device_id=(to_leaf, to_yh * 2 + c), device_id_type=MESH).start()

    def wait_pieces(src, base, size, to_leaf, sems):
        for to_yh in range(2):
            @pl.when(jnp.logical_not((to_leaf == leaf) & (yh == to_yh)))
            def _():
                pltpu.make_async_copy(src.at[to_yh], src.at[to_yh], sems.at[to_yh]).wait()

    y_src = yl * 2 + yh
    leaf_1 = leaf - yl
    leaf_2 = (x * 4 + z - lax.rem(z, 2)) * 2 + 1
    leaf_3 = x * 8 + 3
    piece_1 = (pk12.at[0], y_src * 520, 520, leaf_1, ps_sem.at[0])
    piece_2 = (pk12.at[1, :, pl.ds(0, 512)], (lax.rem(z, 2) * 4 + y_src) * 512, 512, leaf_2, ps_sem.at[1])

    def piece_3(t):
        return (pk3.at[t - 2], ((t - 2) * 16 + y_src * 4 + z) * 128, 128, leaf_3, p3_sem.at[t - 2])

    def rs_copy(t, k):
        q = lax.rem(z + k, 4)
        return pltpu.make_async_remote_copy(
            src_ref=own.at[t, rows(q * 256, 256)], dst_ref=zrs.at[t - 2, 3 - k],
            send_sem=rs_sem.at[t - 2, k - 1], recv_sem=rr_sem.at[t - 2, 3 - k],
            device_id=((x * 4 + q) * 2 + yl, grid), device_id_type=MESH)

    def spread(t):
        u_copy(t).wait_recv()
        if t < 2:
            def body(i, carry):
                base = i * 256
                top = own[t, rows(base, 128), :] + rcv[t, rows(base, 128), :]
                bottom = own[t, rows(base + 128, 128), :] + rcv[t, rows(base + 128, 128), :]
                p0, p1 = packed_pair(top, bottom)
                pk12[t, 0, rows(i * 128, 128), :] = p0
                pk12[t, 1, rows(i * 128, 128), :] = p1
                return carry
            lax.fori_loop(0, 4, body, 0)
            if t == 0:
                squares = own[0, pl.ds(1024, 8), :] + rcv[0, pl.ds(1024, 8), :]
                pk12[0, 0, pl.ds(512, 8), :] = squares
                pk12[0, 1, pl.ds(512, 8), :] = turned(squares)
            send_pieces(*(piece_1 if t == 0 else piece_2), u_sem.at[0])
        else:
            def body(i, carry):
                part = rows(i * 256, 256)
                own[t, part, :] = own[t, part, :] + rcv[t, part, :]
                return carry
            lax.fori_loop(0, 4, body, 0)
            for k in range(1, 4):
                rs_copy(t, k).start()

    for t in range(6):
        lp_copy(t).wait()
        masks = [mask_ref[pl.ds(t * 4 + b, 1), :] for b in range(4)]
        masked = lambda ref: jnp.concatenate(
            [ref[b * 128:(b + 1) * 128, :] * jnp.concatenate([masks[b]] * 2, axis=1) for b in range(4)], axis=0)
        y_high, y_low = masked(yh_s), masked(yl_s)
        xh[...] = y_high
        xl[...] = y_low

        def body(i, carry):
            part = rows(i * 256, 256)
            product = dot3(pbuf[t % 3, part, :], xh[...], xl[...])
            own[t, part, :] = product[:, :128]
            snd[t, part, :] = product[:, 128:]
            return carry
        lax.fori_loop(0, 4, body, 0)
        if t + 3 < 6:
            lp_copy(t + 3).start()
        u_copy(t).start()
        if t > 0:
            spread(t - 1)
    spread(5)

    def gather_rs(t):
        for k in range(1, 4):
            rs_copy(t, k).wait_recv()
        base = z * 256

        def total(start):
            value = own[t, rows(base + start, 128), :]
            for k in range(3):
                value = value + zrs[t - 2, k, pl.ds(start, 128), :]
            return value
        p0, p1 = packed_pair(total(0), total(128))
        pk3[t - 2, 0] = p0
        pk3[t - 2, 1] = p1
        send_pieces(*piece_3(t), u_sem.at[t - 2])

    def up_copy(m, size):
        return pltpu.make_async_remote_copy(
            src_ref=csend.at[m, pl.ds(0, size)], dst_ref=crecv.at[side, m, pl.ds(0, size)],
            send_sem=cs_sem.at[m], recv_sem=cr_sem.at[side, m], device_id=(parent, grid), device_id_type=MESH)

    def wait_child(s, m, size):
        pltpu.make_async_copy(csend.at[m, pl.ds(0, size)], crecv.at[s, m, pl.ds(0, size)], cr_sem.at[s, m]).wait()

    def take_3(k, dst):
        start = k * 2048
        pltpu.make_async_copy(ubuf.at[pl.ds(0, 1920)], ubuf.at[pl.ds(0, 1920)], u_sem.at[k]).wait()
        value = ubuf[rows(start, 512), :]
        for s in range(1, 4):
            value = value + ubuf[rows(start + s * 512, 512), :]
        dst[pl.ds(0, 512), :] = dst[pl.ds(0, 512), :] + value

    def chain():
        accp[...] = jnp.zeros_like(accp)

        @pl.when(level == 1)
        def _():
            pltpu.make_async_copy(ubuf.at[pl.ds(0, 1560)], ubuf.at[pl.ds(0, 1560)], u_sem.at[0]).wait()
            accp[...] = ubuf[0:520, :] + ubuf[520:1040, :] + ubuf[1040:1560, :] + ubuf[1560:2080, :]

        @pl.when(level == 2)
        def _():
            pltpu.make_async_copy(ubuf.at[pl.ds(0, 3584)], ubuf.at[pl.ds(0, 3584)], u_sem.at[0]).wait()
            value = ubuf[0:512, :]
            for s in range(1, 8):
                value = value + ubuf[s * 512:(s + 1) * 512, :]
            accp[0:512, :] = value

        @pl.when(level == 3)
        def _():
            take_3(0, accp)

        @pl.when(level > 1)
        def _():
            wait_child(0, 0, 520)
            accp[...] = accp[...] + crecv[0, 0]

        @pl.when((level > 1) & (level < 6))
        def _():
            wait_child(1, 0, 520)
            accp[...] = accp[...] + crecv[1, 0]

        for i in range(4):
            left = lane_left((128, 128))
            for j, value in enumerate(unpacked(accp[i * 128:(i + 1) * 128, :])):
                part = pl.ds(i * 256 + j * 128, 128)
                right_side = rhsp[part, :]
                v = jnp.where(left, right_side, turned(right_side)) - value
                high, low = split(v)
                vcat[0, part, :] = jnp.where(left, high.astype(F32), low.astype(F32)).astype(BF16)
                vh0[0, part, :] = jnp.where(left, high.astype(F32), 0.0).astype(BF16)
        squares = accp[512:520, :]
        for r in range(4):
            part = pl.ds(r * 256, 256)
            depth = (r + 1) * 256
            high, low = split(invb[part, 0:depth])
            product = dot(high, vcat[0, 0:depth, :]) + dot(low, vh0[0, 0:depth, :])
            s_value = product + turned(product)
            solv[part, :] = s_value[:, :64]
            left = lane_left((256, 128))
            high, low = split(s_value)
            vcat[1, part, :] = jnp.where(left, high.astype(F32), low.astype(F32)).astype(BF16)
            vh0[1, part, :] = jnp.where(left, high.astype(F32), 0.0).astype(BF16)
            squares = squares + jnp.sum(s_value * s_value, axis=0, keepdims=True)
        csend[0, pl.ds(512, 8), :] = squares
        pltpu.make_async_copy(solv, sol_hbm, out_sem.at[1]).start()

        def panel(m, carry):
            sp_copy(m).wait()
            pend[...] = jnp.zeros_like(pend)

            @pl.when(level > 1)
            def _():
                wait_child(0, m + 1, 512)
                wait_child(1, m + 1, 512)
                pend[...] = crecv[0, m + 1, 0:512, :] + crecv[1, m + 1, 0:512, :]

            @pl.when(level == 3)
            def _():
                take_3(m + 1, pend)

            slot = lax.rem(m, 3)

            def body(i, inner):
                high, low = split(spb[slot, rows(i * 256, 256), :])
                product = dot(high, vcat[1]) + dot(low, vh0[1])
                total = product + turned(product)
                left = lane_left((128, 128))
                part = rows(i * 128, 128)
                csend[m, part, :] = jnp.where(left, total[:128], total[128:]) + pend[part, :]
                return inner
            lax.fori_loop(0, 4, body, 0)

            @pl.when(m == 0)
            def _():
                up_copy(m, 520).start()

            @pl.when(m > 0)
            def _():
                up_copy(m, 512).start()

            @pl.when(m + 3 < n_pan)
            def _():
                sp_copy(m + 3).start()
            return carry
        lax.fori_loop(0, n_pan, panel, 0)

    srhs_copy.wait()
    rhsp[...] = jnp.zeros_like(rhsp)
    rhsp[:, :64] = rhsv[...]
    inv_copy.wait()

    turn = jnp.minimum(level, 3) - 1

    def phase(p, carry):
        @pl.when(p == turn)
        def _():
            chain()

        @pl.when(p == 0)
        def _():
            gather_rs(2)
            gather_rs(3)

        @pl.when(p == 1)
        def _():
            gather_rs(4)
            gather_rs(5)
        return carry
    lax.fori_loop(0, 3, phase, 0)

    def width_copy(d):
        return pltpu.make_async_remote_copy(
            src_ref=wsend, dst_ref=wrecv, send_sem=w_sem.at[0], recv_sem=w_sem.at[1],
            device_id=(d, grid), device_id_type=MESH)

    @pl.when(level == 6)
    def _():
        wsend[0] = jnp.sqrt(csend[0, pl.ds(512, 8), :] / (32 * 3072) + 1e-06)
        for d in range(31):
            width_copy(d).start()
        width_ref[...] = wsend[0]
        pltpu.make_async_copy(abuf.at[pl.ds(0, 248)], abuf.at[pl.ds(0, 248)], w_sem.at[0]).wait()

    @pl.when(level < 6)
    def _():
        width_copy(0).wait_recv()
        width_ref[...] = wrecv[0]

    pltpu.make_async_copy(abuf.at[pl.ds(0, 1016)], abuf.at[pl.ds(0, 1016)], a2a_sem.at[0]).wait()

    @pl.when(yh == 0)
    def _():
        to_sibling(0).wait_send()
        across().wait_send()

    @pl.when(c == 0)
    def _():
        to_sibling(1).wait_send()
    y_out.wait()
    pltpu.make_async_copy(solv, sol_hbm, out_sem.at[1]).wait()
    for t in range(6):
        u_copy(t).wait_send()
    wait_pieces(*piece_1)
    wait_pieces(*piece_2)
    for t in range(2, 6):
        for k in range(1, 4):
            rs_copy(t, k).wait_send()
        wait_pieces(*piece_3(t))

    def sent(m, carry):
        @pl.when(m == 0)
        def _():
            up_copy(m, 520).wait_send()

        @pl.when(m > 0)
        def _():
            up_copy(m, 512).wait_send()
        return carry
    lax.fori_loop(0, n_pan, sent, 0)


def local(rhs_rows, order, leaf_inverse, leaf_panels, panel_mask, sep_rhs, sep_inverse, sep_panels):
    twice = jnp.broadcast_to(order.reshape(128, 1, 4), (128, 2, 4)).reshape(1024, 1)
    mask = jnp.broadcast_to(panel_mask.reshape(24, 1).astype(BF16), (24, 128))
    vmem = pl.BlockSpec(memory_space=pltpu.VMEM)
    hbm = pl.BlockSpec(memory_space=pl.ANY)
    V = pltpu.VMEM
    leaf_y, solved, width = pl.pallas_call(
        kernel,
        out_shape=(
            jax.ShapeDtypeStruct((512, 256), F32),
            jax.ShapeDtypeStruct((1024, 64), F32),
            jax.ShapeDtypeStruct((8, 128), F32),
        ),
        in_specs=[vmem] * 3 + [hbm] * 5,
        out_specs=(hbm, hbm, vmem),
        scratch_shapes=[
            V((1024, 128), F32), V((1024, 128), F32),
            V((512, 256), BF16), V((512, 256), BF16),
            V((2048, 512), F32),
            V((3, 512, 256), F32), V((2, 512, 256), F32), V((512, 256), F32),
            V((512, 256), F32), V((512, 256), BF16), V((512, 256), BF16),
            V((3, 1024, 512), F32),
            V((6, 1032, 128), F32), V((6, 1032, 128), F32), V((6, 1032, 128), F32),
            V((4, 3, 256, 128), F32),
            V((2, 2, 520, 128), F32), V((4, 2, 128, 128), F32),
            V((8192, 128), F32),
            V((520, 128), F32), V((512, 128), F32),
            V((1024, 64), F32), V((1024, 128), F32),
            V((2, 1024, 128), BF16), V((2, 1024, 128), BF16),
            V((1024, 64), F32),
            V((1024, 1024), F32), V((3, 1024, 1024), F32),
            V((5, 520, 128), F32), V((2, 5, 520, 128), F32),
            V((1, 8, 128), F32), V((1, 8, 128), F32),
            DMA((3,)), DMA((3,)), DMA((3,)), DMA((2,)), DMA((3,)), DMA((2,)), DMA, DMA((6,)), DMA((6,)),
            DMA((4, 3)), DMA((4, 3)), DMA((2, 2)), DMA((4, 2)), DMA((4,)), DMA((5,)), DMA((2, 5)), DMA((2,)), DMA((2,)),
        ],
        compiler_params=pltpu.CompilerParams(
            collective_id=0, has_side_effects=True, vmem_limit_bytes=62 * 2 ** 20),
        cost_estimate=pl.CostEstimate(flops=7 * 10 ** 9, bytes_accessed=44 * 10 ** 6, transcendentals=0),
    )(twice, mask, rhs_rows, leaf_inverse, leaf_panels[0], sep_rhs[0], sep_inverse[0], sep_panels[0])
    return leaf_y, solved[None], width[0, :64]


def solution(mesh):
    placed = (
        P(("leaf", "grid"), None),
        P(("leaf", "grid")),
        P("leaf", "grid"),
        P("leaf", None, None, "grid"),
        P("leaf", None, "grid"),
        P("leaf", None, "grid"),
        P("leaf", None, None),
        P("leaf", None, None, None),
    )
    return jax.shard_map(
        local,
        mesh=mesh,
        in_specs=placed,
        out_specs=(P(("leaf", "grid"), None), P("leaf", None, "grid"), P("grid")),
        check_vma=False,
    )
```

```python
import jax
import jax.numpy as jnp
from jax import lax
from jax.experimental import pallas as pl
from jax.experimental.pallas import tpu as pltpu
from jax.sharding import PartitionSpec as P

F32, BF16 = jnp.float32, jnp.bfloat16
MESH = pl.DeviceIdType.MESH
DMA = pltpu.SemaphoreType.DMA


def split(value):
    high = value.astype(BF16)
    return high, (value - high.astype(F32)).astype(BF16)


def dot(a, b):
    return jnp.dot(a, b, preferred_element_type=F32)


def dot3(a, b_high, b_low):
    high, low = split(a)
    return dot(high, b_high) + dot(high, b_low) + dot(low, b_high)


def lane_left(shape):
    return lax.broadcasted_iota(jnp.int32, shape, 1) < 64


def turned(value):
    return pltpu.roll(value, 64, 1)


def packed_pair(top, bottom):
    left = lane_left(top.shape)
    return jnp.where(left, top, turned(bottom)), jnp.where(left, turned(top), bottom)


def unpacked(value):
    left = lane_left(value.shape)
    other = turned(value)
    return jnp.where(left, value, other), jnp.where(left, other, value)


def rows(start, size, unit=8):
    if isinstance(start, int):
        return pl.ds(start, size)
    return pl.ds(pl.multiple_of(start, unit), size)


def kernel(order_ref, mask_ref, rhs_ref, linv_hbm, lpan_hbm, srhs_hbm, sinv_hbm, span_hbm,
           leafy_hbm, sol_hbm, width_ref,
           abuf, xbuf, xh, xl, lbuf, zs, zr, za, ybuf, yh_s, yl_s, pbuf, own, snd, rcv, zrs,
           pk12, pk3, ubuf, accp, pend, squares, cacc, racc, rhsv, rhsp, vcat, vh0, solv, invb, spb, csend, crecv, wsend, wrecv,
           ld_sem, lp_sem, sp_sem, a2a_sem, zs_sem, zr_sem, za_sem, us_sem, ur_sem, rs_sem, rr_sem,
           ps_sem, p3_sem, u_sem, cs_sem, cr_sem, w_sem, out_sem):
    leaf = lax.axis_index("leaf")
    grid = lax.axis_index("grid")
    me = leaf * 4 + grid
    yl = lax.rem(leaf, 2)
    z = lax.rem(lax.div(leaf, 2), 4)
    x = lax.div(leaf, 8)
    yh = lax.div(grid, 2)
    c = lax.rem(grid, 2)
    sib = yh * 2 + 1 - c

    level = jnp.int32(1)
    for bit in range(1, 6):
        level = level + (lax.rem(leaf + 1, 2 ** bit) == 0).astype(jnp.int32)
    parent = jnp.int32(0)
    for tier in range(1, 6):
        size = 2 ** (tier + 1)
        parent = jnp.where(level == tier, lax.div(leaf, size) * size + 2 ** tier - 1, parent)
    side = (leaf > parent).astype(jnp.int32)
    n_pan = 6 - level

    l_copy = pltpu.make_async_copy(linv_hbm, lbuf, ld_sem.at[0])
    l_copy.start()
    inv_copy = pltpu.make_async_copy(sinv_hbm, invb, ld_sem.at[1])
    srhs_copy = pltpu.make_async_copy(srhs_hbm, rhsv, ld_sem.at[2])

    def lp_copy(t):
        return pltpu.make_async_copy(lpan_hbm.at[t], pbuf.at[t % 3], lp_sem.at[t % 3])

    def sp_copy(m):
        slot = lax.rem(m, 3)
        return pltpu.make_async_copy(span_hbm.at[m], spb.at[slot], sp_sem.at[slot])

    rh, rl = split(rhs_ref[...])
    index = order_ref[...].astype(F32)
    index = jnp.transpose(jnp.concatenate([index, index], axis=0)).astype(jnp.int32)
    upper = lax.broadcasted_iota(jnp.int32, (16, 8, 128), 1) < 4
    for part in range(4):
        hot = (lax.broadcasted_iota(jnp.int32, (128, 512), 1) == index[:, part:part + 1]).astype(F32).astype(BF16)
        got = dot(hot, rh) + dot(hot, rl)
        first, second = got[:, :128].reshape(16, 8, 128), got[:, 128:].reshape(16, 8, 128)
        even = jnp.where(upper, first, pltpu.roll(second, 4, 1))
        odd = jnp.where(upper, pltpu.roll(first, 4, 1), second)
        abuf[rows(part * 256, 256), :] = jnp.stack([even, odd], axis=1).reshape(256, 128)

    barrier = pltpu.get_barrier_semaphore()

    def greet(k, carry):
        d = lax.rem(me + k, 128)
        pl.semaphore_signal(barrier, inc=1, device_id=(lax.div(d, 4), lax.rem(d, 4)), device_id_type=MESH)
        return carry

    lax.fori_loop(1, 128, greet, 0)
    for t in range(3):
        lp_copy(t).start()
    srhs_copy.start()
    pl.semaphore_wait(barrier, 127)

    def a2a(k, carry):
        d = lax.rem(me + k, 128)
        pltpu.make_async_remote_copy(
            src_ref=abuf.at[rows(d * 8, 8)], dst_ref=xbuf.at[rows(me * 8, 8)],
            send_sem=a2a_sem.at[0], recv_sem=a2a_sem.at[1],
            device_id=(lax.div(d, 4), lax.rem(d, 4)), device_id_type=MESH).start()
        return carry

    lax.fori_loop(1, 128, a2a, 0)
    xbuf[rows(me * 8, 8), :] = abuf[rows(me * 8, 8), :]
    inv_copy.start()
    for m in range(3):
        @pl.when(m < n_pan)
        def _():
            sp_copy(jnp.int32(m)).start()
    pltpu.make_async_copy(xbuf.at[pl.ds(0, 1016)], xbuf.at[pl.ds(0, 1016)], a2a_sem.at[1]).wait()

    raw = xbuf[...].reshape(64, 2, 8, 128)
    first, second = raw[:, 0], raw[:, 1]
    upper = lax.broadcasted_iota(jnp.int32, (64, 8, 128), 1) < 4
    left = jnp.where(upper, first, pltpu.roll(second, 4, 1)).reshape(512, 128)
    right = jnp.where(upper, pltpu.roll(first, 4, 1), second).reshape(512, 128)
    for half, value in enumerate((left, right)):
        high, low = split(value)
        xh[:, half * 128:(half + 1) * 128] = high
        xl[:, half * 128:(half + 1) * 128] = low

    l_copy.wait()

    def leaf_block(r, dst):
        def body(i, carry):
            dst[rows(i * 256, 256), :] = dot3(lbuf[rows(r * 512 + i * 256, 256), :], xh[...], xl[...])
            return carry
        lax.fori_loop(0, 2, body, 0)

    def to_sibling(slot):
        return pltpu.make_async_remote_copy(
            src_ref=zs.at[slot], dst_ref=zr.at[slot], send_sem=zs_sem.at[slot], recv_sem=zr_sem.at[slot],
            device_id=(leaf, sib), device_id_type=MESH)

    def across():
        return pltpu.make_async_remote_copy(
            src_ref=zs.at[2], dst_ref=za, send_sem=zs_sem.at[2], recv_sem=za_sem,
            device_id=(leaf, 2 + c), device_id_type=MESH)

    @pl.when(yh == 0)
    def _():
        leaf_block(3 - c, zs.at[0])
        to_sibling(0).start()
        leaf_block(2 + c, zs.at[2])
        to_sibling(0).wait_recv()
        zs[2] = zs[2] + zr[0]
        across().start()

        @pl.when(c == 0)
        def _():
            leaf_block(1, zs.at[1])
            to_sibling(1).start()

    @pl.when((yh == 1) & (c == 0))
    def _():
        leaf_block(3, zs.at[1])
        to_sibling(1).start()

    leaf_block(grid, ybuf)

    @pl.when(c == 1)
    def _():
        to_sibling(1).wait_recv()
        ybuf[...] = ybuf[...] + zr[1]

    @pl.when(yh == 1)
    def _():
        across().wait_recv()
        ybuf[...] = ybuf[...] + za[...]

    y_out = pltpu.make_async_copy(ybuf, leafy_hbm, out_sem.at[0])
    y_out.start()

    y_left, y_right = ybuf[:, :128], ybuf[:, 128:]
    for_0, for_1 = packed_pair(y_left, y_right)
    mine = jnp.where(c == 0, for_0, for_1)
    other = jnp.where(c == 0, for_1, for_0)
    own[0, pl.ds(1024, 8), :] = jnp.broadcast_to(jnp.sum(mine * mine, axis=0, keepdims=True), (8, 128))
    snd[0, pl.ds(1024, 8), :] = jnp.broadcast_to(jnp.sum(other * other, axis=0, keepdims=True), (8, 128))
    for half, value in enumerate((mine, other)):
        high, low = split(value)
        yh_s[:, half * 128:(half + 1) * 128] = high
        yl_s[:, half * 128:(half + 1) * 128] = low

    def u_copy(t):
        size = 1032 if t == 0 else 1024
        return pltpu.make_async_remote_copy(
            src_ref=snd.at[t, pl.ds(0, size)], dst_ref=rcv.at[t, pl.ds(0, size)],
            send_sem=us_sem.at[t], recv_sem=ur_sem.at[t], device_id=(leaf, sib), device_id_type=MESH)

    def send_pieces(src, base, size, to_leaf, sems, recv_sem):
        for to_yh in range(2):
            to_me = (to_leaf == leaf) & (yh == to_yh)

            @pl.when(to_me)
            def _():
                ubuf[rows(base, size), :] = src[to_yh]

            @pl.when(jnp.logical_not(to_me))
            def _():
                pltpu.make_async_remote_copy(
                    src_ref=src.at[to_yh], dst_ref=ubuf.at[rows(base, size)],
                    send_sem=sems.at[to_yh], recv_sem=recv_sem,
                    device_id=(to_leaf, to_yh * 2 + c), device_id_type=MESH).start()

    def wait_pieces(src, base, size, to_leaf, sems):
        for to_yh in range(2):
            @pl.when(jnp.logical_not((to_leaf == leaf) & (yh == to_yh)))
            def _():
                pltpu.make_async_copy(src.at[to_yh], src.at[to_yh], sems.at[to_yh]).wait()

    y_src = yl * 2 + yh
    leaf_1 = leaf - yl
    leaf_2 = (x * 4 + z - lax.rem(z, 2)) * 2 + 1
    leaf_3 = x * 8 + 3
    piece_1 = (pk12.at[0], y_src * 520, 520, leaf_1, ps_sem.at[0])
    piece_2 = (pk12.at[1, :, pl.ds(0, 512)], (lax.rem(z, 2) * 4 + y_src) * 512, 512, leaf_2, ps_sem.at[1])

    def piece_3(t):
        return (pk3.at[t - 2], ((t - 2) * 16 + y_src * 4 + z) * 128, 128, leaf_3, p3_sem.at[t - 2])

    def rs_copy(t, k):
        at = z if t < 4 else x
        q = lax.rem(at + k, 4)
        to_leaf = (x * 4 + q) * 2 + yl if t < 4 else (q * 4 + z) * 2 + yl
        return pltpu.make_async_remote_copy(
            src_ref=own.at[t, rows(q * 256, 256)], dst_ref=zrs.at[t - 2, 3 - k],
            send_sem=rs_sem.at[t - 2, k - 1], recv_sem=rr_sem.at[t - 2, 3 - k],
            device_id=(to_leaf, grid), device_id_type=MESH)

    def spread(t):
        u_copy(t).wait_recv()
        if t < 2:
            def body(i, carry):
                base = i * 256
                top = own[t, rows(base, 128), :] + rcv[t, rows(base, 128), :]
                bottom = own[t, rows(base + 128, 128), :] + rcv[t, rows(base + 128, 128), :]
                p0, p1 = packed_pair(top, bottom)
                pk12[t, 0, rows(i * 128, 128), :] = p0
                pk12[t, 1, rows(i * 128, 128), :] = p1
                return carry
            lax.fori_loop(0, 4, body, 0)
            if t == 0:
                squares = own[0, pl.ds(1024, 8), :] + rcv[0, pl.ds(1024, 8), :]
                pk12[0, 0, pl.ds(512, 8), :] = squares
                pk12[0, 1, pl.ds(512, 8), :] = turned(squares)
            send_pieces(*(piece_1 if t == 0 else piece_2), u_sem.at[0])
        else:
            def body(i, carry):
                part = rows(i * 256, 256)
                own[t, part, :] = own[t, part, :] + rcv[t, part, :]
                return carry
            lax.fori_loop(0, 4, body, 0)
            for k in range(1, 4):
                rs_copy(t, k).start()

    for t in range(6):
        lp_copy(t).wait()
        masks = [jnp.full((1, 256), mask_ref[t, b].astype(F32)).astype(BF16) for b in range(4)]
        masked = lambda ref: jnp.concatenate(
            [ref[b * 128:(b + 1) * 128, :] * masks[b] for b in range(4)], axis=0)
        y_high, y_low = masked(yh_s), masked(yl_s)
        xh[...] = y_high
        xl[...] = y_low

        def body(i, carry):
            part = rows(i * 256, 256)
            product = dot3(pbuf[t % 3, part, :], xh[...], xl[...])
            own[t, part, :] = product[:, :128]
            snd[t, part, :] = product[:, 128:]
            return carry
        lax.fori_loop(0, 4, body, 0)
        if t + 3 < 6:
            lp_copy(t + 3).start()
        u_copy(t).start()
        if t > 0:
            spread(t - 1)
    spread(5)

    def gather_rs(t):
        for k in range(3):
            pltpu.make_async_copy(zrs.at[t - 2, k], zrs.at[t - 2, k], rr_sem.at[t - 2, k]).wait()
        base = jnp.where(t < 4, z, x) * 256

        def total(start):
            value = own[t, rows(base + start, 128), :]
            for k in range(3):
                value = value + zrs[t - 2, k, pl.ds(start, 128), :]
            return value
        p0, p1 = packed_pair(total(0), total(128))
        pk3[t - 2, 0] = p0
        pk3[t - 2, 1] = p1
        send_pieces(*piece_3(t), u_sem.at[t - 2])

    def up_copy(m, i, size):
        part = rows(i * 128, size)
        return pltpu.make_async_remote_copy(
            src_ref=csend.at[m, part], dst_ref=crecv.at[side, m, part],
            send_sem=cs_sem.at[m, i], recv_sem=cr_sem.at[side, m, i], device_id=(parent, grid), device_id_type=MESH)

    def wait_child(s, m, i, size):
        part = rows(i * 128, size)
        pltpu.make_async_copy(csend.at[m, part], crecv.at[s, m, part], cr_sem.at[s, m, i]).wait()

    def take_3(k, dst):
        start = k * 2048
        pltpu.make_async_copy(ubuf.at[pl.ds(0, 1920)], ubuf.at[pl.ds(0, 1920)], u_sem.at[k]).wait()

        @pl.when(k < 2)
        def _():
            value = ubuf[rows(start, 512), :]
            for s in range(1, 4):
                value = value + ubuf[rows(start + s * 512, 512), :]
            dst[...] = value

        @pl.when(k >= 2)
        def _():
            value = ubuf[rows(start, 128), :]
            for s in range(1, 16):
                value = value + ubuf[rows(start + s * 128, 128), :]
            dst[...] = jnp.zeros_like(dst)
            dst[rows(x * 128, 128), :] = value

    def dot2(a, which, part):
        high, low = split(a)
        return dot(high, vcat[which, part, :]) + dot(low, vh0[which, part, :])

    def stacked(value, which, part):
        left = lane_left(value.shape)
        high, low = split(value)
        vcat[which, part, :] = jnp.where(left, high.astype(F32), low.astype(F32)).astype(BF16)
        vh0[which, part, :] = jnp.where(left, high.astype(F32), 0.0).astype(BF16)

    def finished(product, m, i):
        total = product + turned(product)
        part = rows(i * 128, 128)
        csend[m, part, :] = jnp.where(lane_left((128, 128)), total[:128], total[128:])

        @pl.when(level == 3)
        def _():
            csend[m, part, :] = csend[m, part, :] + pend[part, :]

        @pl.when(level > 1)
        def _():
            wait_child(0, m + 1, i, 128)
            wait_child(1, m + 1, i, 128)
            csend[m, part, :] = csend[m, part, :] + (crecv[0, m + 1, part, :] + crecv[1, m + 1, part, :])

    def head():
        squares[...] = jnp.zeros_like(squares)

        @pl.when(level == 1)
        def _():
            pltpu.make_async_copy(ubuf.at[pl.ds(0, 1560)], ubuf.at[pl.ds(0, 1560)], u_sem.at[0]).wait()
            accp[...] = ubuf[0:512, :] + ubuf[520:1032, :] + ubuf[1040:1552, :] + ubuf[1560:2072, :]
            squares[...] = ubuf[512:520, :] + ubuf[1032:1040, :] + ubuf[1552:1560, :] + ubuf[2072:2080, :]

        @pl.when(level == 2)
        def _():
            pltpu.make_async_copy(ubuf.at[pl.ds(0, 3584)], ubuf.at[pl.ds(0, 3584)], u_sem.at[0]).wait()
            value = ubuf[0:512, :]
            for s in range(1, 8):
                value = value + ubuf[s * 512:(s + 1) * 512, :]
            accp[...] = value

        @pl.when(level == 3)
        def _():
            take_3(0, accp)
            take_3(1, pend)

        @pl.when(level > 3)
        def _():
            accp[...] = jnp.zeros_like(accp)

        @pl.when(n_pan > 0)
        def _():
            sp_copy(jnp.int32(0)).wait()

        for k in range(4):
            packed = pl.ds(k * 128, 128)
            size = 136 if k == 3 else 128

            @pl.when(level > 1)
            def _():
                wait_child(0, 0, k, size)
                accp[packed, :] = accp[packed, :] + crecv[0, 0, packed, :]

            @pl.when((level > 1) & (level < 6))
            def _():
                wait_child(1, 0, k, size)
                accp[packed, :] = accp[packed, :] + crecv[1, 0, packed, :]

            left = lane_left((128, 128))
            for j, value in enumerate(unpacked(accp[packed, :])):
                part = pl.ds(k * 256 + j * 128, 128)
                right_side = rhsp[part, :]
                stacked(jnp.where(left, right_side, turned(right_side)) - value, 0, part)
            part = pl.ds(k * 256, 256)
            product = dot2(invb[part, k * 256:(k + 1) * 256], 0, part)
            if k > 0:
                product = product + racc[part, :]
            s_value = product + turned(product)
            stacked(s_value, 1, part)

            @pl.when(n_pan > 0)
            def _():
                if k < 3:
                    product = dot2(spb[0, :, k * 256:(k + 1) * 256], 1, part)
                    cacc[...] = product if k == 0 else cacc[...] + product
                else:
                    squares[...] = squares[...] + jnp.sum(s_value * s_value, axis=0, keepdims=True)
                    squares[...] = squares[...] + crecv_squares()
                    csend[0, pl.ds(512, 8), :] = squares[...]
                    for i in range(4):
                        out = pl.ds(i * 256, 256)
                        finished(cacc[out, :] + dot2(spb[0, out, k * 256:(k + 1) * 256], 1, part), 0, i)
                        up_copy(0, i, 136 if i == 3 else 128).start()
            solv[part, :] = s_value[:, :64]
            if k < 3:
                squares[...] = squares[...] + jnp.sum(s_value * s_value, axis=0, keepdims=True)
                rest = slice((k + 1) * 256, 1024)
                product = dot2(invb[rest, k * 256:(k + 1) * 256], 0, part)
                racc[rest, :] = product if k == 0 else racc[rest, :] + product
            else:
                @pl.when(level == 6)
                def _():
                    squares[...] = squares[...] + jnp.sum(s_value * s_value, axis=0, keepdims=True) + crecv[0, 0, pl.ds(512, 8), :]

        @pl.when(3 < n_pan)
        def _():
            sp_copy(jnp.int32(3)).start()
        pltpu.make_async_copy(solv, sol_hbm, out_sem.at[1]).start()

    def crecv_squares():
        return jnp.where(level > 1, crecv[0, 0, pl.ds(512, 8), :] + crecv[1, 0, pl.ds(512, 8), :], 0.0)

    def panel(m):
        sp_copy(m).wait()

        @pl.when(level == 3)
        def _():
            take_3(m + 1, pend)
        slot = lax.rem(m, 3)
        for i in range(4):
            out = pl.ds(i * 256, 256)
            finished(dot2(spb[slot, out, :], 1, slice(None)), m, i)
            up_copy(m, i, 128).start()

        @pl.when(m + 3 < n_pan)
        def _():
            sp_copy(m + 3).start()

    srhs_copy.wait()
    rhsp[:, :64] = rhsv[...]
    inv_copy.wait()

    start_at = jnp.where(level == 1, 0, 5)

    def phase(p, carry):
        @pl.when(p == start_at)
        def _():
            head()

        @pl.when((p > 0) & (p < 5))
        def _():
            gather_rs(p + 1)

        @pl.when((p > start_at) & (p - start_at < n_pan))
        def _():
            panel(p - start_at)
        return carry
    lax.fori_loop(0, 9, phase, 0)

    def width_copy(d):
        return pltpu.make_async_remote_copy(
            src_ref=wsend, dst_ref=wrecv, send_sem=w_sem.at[0], recv_sem=w_sem.at[1],
            device_id=(d, grid), device_id_type=MESH)

    @pl.when(level == 6)
    def _():
        wsend[0] = jnp.sqrt(squares[...] / (32 * 3072) + 1e-06)
        for d in range(31):
            width_copy(d).start()
        width_ref[...] = wsend[0]
        pltpu.make_async_copy(abuf.at[pl.ds(0, 248)], abuf.at[pl.ds(0, 248)], w_sem.at[0]).wait()

    @pl.when(level < 6)
    def _():
        width_copy(0).wait_recv()
        width_ref[...] = wrecv[0]

    pltpu.make_async_copy(abuf.at[pl.ds(0, 1016)], abuf.at[pl.ds(0, 1016)], a2a_sem.at[0]).wait()

    @pl.when(yh == 0)
    def _():
        to_sibling(0).wait_send()
        across().wait_send()

    @pl.when(c == 0)
    def _():
        to_sibling(1).wait_send()
    y_out.wait()
    pltpu.make_async_copy(solv, sol_hbm, out_sem.at[1]).wait()
    for t in range(6):
        u_copy(t).wait_send()
    wait_pieces(*piece_1)
    wait_pieces(*piece_2)
    for t in range(2, 6):
        for k in range(1, 4):
            rs_copy(t, k).wait_send()
        wait_pieces(*piece_3(t))

    def sent(m, carry):
        for i in range(3):
            up_copy(m, i, 128).wait_send()

        @pl.when(m == 0)
        def _():
            up_copy(m, 3, 136).wait_send()

        @pl.when(m > 0)
        def _():
            up_copy(m, 3, 128).wait_send()
        return carry
    lax.fori_loop(0, n_pan, sent, 0)


def local(rhs_rows, order, leaf_inverse, leaf_panels, panel_mask, sep_rhs, sep_inverse, sep_panels):
    vmem = pl.BlockSpec(memory_space=pltpu.VMEM)
    hbm = pl.BlockSpec(memory_space=pl.ANY)
    V = pltpu.VMEM
    leaf_y, solved, width = pl.pallas_call(
        kernel,
        out_shape=(
            jax.ShapeDtypeStruct((512, 256), F32),
            jax.ShapeDtypeStruct((1024, 64), F32),
            jax.ShapeDtypeStruct((8, 128), F32),
        ),
        in_specs=[vmem, pl.BlockSpec(memory_space=pltpu.SMEM), vmem] + [hbm] * 5,
        out_specs=(hbm, hbm, vmem),
        scratch_shapes=[
            V((1024, 128), F32), V((1024, 128), F32),
            V((512, 256), BF16), V((512, 256), BF16),
            V((2048, 512), F32),
            V((3, 512, 256), F32), V((2, 512, 256), F32), V((512, 256), F32),
            V((512, 256), F32), V((512, 256), BF16), V((512, 256), BF16),
            V((3, 1024, 512), F32),
            V((6, 1032, 128), F32), V((6, 1032, 128), F32), V((6, 1032, 128), F32),
            V((4, 3, 256, 128), F32),
            V((2, 2, 520, 128), F32), V((4, 2, 128, 128), F32),
            V((8192, 128), F32),
            V((512, 128), F32), V((512, 128), F32), V((8, 128), F32),
            V((1024, 128), F32), V((1024, 128), F32),
            V((1024, 64), F32), V((1024, 128), F32),
            V((2, 1024, 128), BF16), V((2, 1024, 128), BF16),
            V((1024, 64), F32),
            V((1024, 1024), F32), V((3, 1024, 1024), F32),
            V((5, 520, 128), F32), V((2, 5, 520, 128), F32),
            V((1, 8, 128), F32), V((1, 8, 128), F32),
            DMA((3,)), DMA((3,)), DMA((3,)), DMA((2,)), DMA((3,)), DMA((2,)), DMA, DMA((6,)), DMA((6,)),
            DMA((4, 3)), DMA((4, 3)), DMA((2, 2)), DMA((4, 2)), DMA((4,)), DMA((5, 4)), DMA((2, 5, 4)), DMA((2,)), DMA((2,)),
        ],
        compiler_params=pltpu.CompilerParams(
            collective_id=0, has_side_effects=True, vmem_limit_bytes=62 * 2 ** 20),
        cost_estimate=pl.CostEstimate(flops=7 * 10 ** 9, bytes_accessed=44 * 10 ** 6, transcendentals=0),
    )(order.reshape(4, 128), panel_mask[0], rhs_rows, leaf_inverse, leaf_panels[0], sep_rhs[0], sep_inverse[0], sep_panels[0])
    return leaf_y, solved[None], width[0, :64]


def solution(mesh):
    placed = (
        P(("leaf", "grid"), None),
        P(("leaf", "grid")),
        P("leaf", "grid"),
        P("leaf", None, None, "grid"),
        P("leaf", None, "grid"),
        P("leaf", None, "grid"),
        P("leaf", None, None),
        P("leaf", None, None, None),
    )
    return jax.shard_map(
        local,
        mesh=mesh,
        in_specs=placed,
        out_specs=(P(("leaf", "grid"), None), P("leaf", None, "grid"), P("grid")),
        check_vma=False,
    )
```

```python
import jax
import jax.numpy as jnp
from jax import lax
from jax.experimental import pallas as pl
from jax.experimental.pallas import tpu as pltpu
from jax.sharding import PartitionSpec as P

F32, BF16 = jnp.float32, jnp.bfloat16
MESH = pl.DeviceIdType.MESH
DMA = pltpu.SemaphoreType.DMA


def split(value):
    high = value.astype(BF16)
    return high, (value - high.astype(F32)).astype(BF16)


def dot(a, b):
    return jnp.dot(a, b, preferred_element_type=F32)


def dot3(a, b_high, b_low):
    high, low = split(a)
    return dot(high, b_high) + dot(high, b_low) + dot(low, b_high)


def lane_left(shape):
    return lax.broadcasted_iota(jnp.int32, shape, 1) < 64


def turned(value):
    return pltpu.roll(value, 64, 1)


def packed_pair(top, bottom):
    left = lane_left(top.shape)
    return jnp.where(left, top, turned(bottom)), jnp.where(left, turned(top), bottom)


def unpacked(value):
    left = lane_left(value.shape)
    other = turned(value)
    return jnp.where(left, value, other), jnp.where(left, other, value)


def rows(start, size, unit=8):
    if isinstance(start, int):
        return pl.ds(start, size)
    return pl.ds(pl.multiple_of(start, unit), size)


def kernel(order_ref, mask_ref, rhs_ref, linv_hbm, lpan_hbm, srhs_hbm, sinv_hbm, span_hbm,
           leafy_hbm, sol_hbm, width_ref,
           abuf, xbuf, xh, xl, lbuf, zs, zr, za, ybuf, yh_s, yl_s, pbuf, own, snd, rcv, zrs,
           pk1, pk, zpair, yrs, s2, grecv, ubuf, accp, pend, squares, cacc, racc, rhsv, rhsp, vcat, vh0, solv, invb, spb, csend, crecv, wsend, wrecv,
           ld_sem, lp_sem, sp_sem, a2a_sem, zs_sem, zr_sem, za_sem, us_sem, ur_sem, rs_sem, rr_sem,
           ps_sem, p3_sem, pair_sem, ys_sem, yr_sem, g_sem, u_sem, cs_sem, cr_sem, w_sem, out_sem):
    leaf = lax.axis_index("leaf")
    grid = lax.axis_index("grid")
    me = leaf * 4 + grid
    yl = lax.rem(leaf, 2)
    z = lax.rem(lax.div(leaf, 2), 4)
    x = lax.div(leaf, 8)
    yh = lax.div(grid, 2)
    y = yh * 2 + yl
    c = lax.rem(grid, 2)
    sib = yh * 2 + 1 - c

    level = jnp.int32(1)
    for bit in range(1, 6):
        level = level + (lax.rem(leaf + 1, 2 ** bit) == 0).astype(jnp.int32)
    parent = jnp.int32(0)
    for tier in range(1, 6):
        size = 2 ** (tier + 1)
        parent = jnp.where(level == tier, lax.div(leaf, size) * size + 2 ** tier - 1, parent)
    side = (leaf > parent).astype(jnp.int32)
    above = jnp.int32(0)
    for tier in range(1, 5):
        size = 2 ** (tier + 2)
        above = jnp.where(level == tier, lax.div(leaf, size) * size + 2 ** (tier + 1) - 1, above)
    place = (parent > above).astype(jnp.int32) * 2 + side
    n_pan = 6 - level

    l_copy = pltpu.make_async_copy(linv_hbm, lbuf, ld_sem.at[0])
    l_copy.start()
    inv_copy = pltpu.make_async_copy(sinv_hbm, invb, ld_sem.at[1])
    srhs_copy = pltpu.make_async_copy(srhs_hbm, rhsv, ld_sem.at[2])

    def lp_copy(t):
        return pltpu.make_async_copy(lpan_hbm.at[t], pbuf.at[t % 3], lp_sem.at[t % 3])

    def sp_copy(m):
        slot = lax.rem(m, 3)
        return pltpu.make_async_copy(span_hbm.at[m], spb.at[slot], sp_sem.at[slot])

    rh, rl = split(rhs_ref[...])
    index = order_ref[...].astype(F32)
    index = jnp.transpose(jnp.concatenate([index, index], axis=0)).astype(jnp.int32)
    upper = lax.broadcasted_iota(jnp.int32, (16, 8, 128), 1) < 4
    for part in range(4):
        hot = (lax.broadcasted_iota(jnp.int32, (128, 512), 1) == index[:, part:part + 1]).astype(F32).astype(BF16)
        got = dot(hot, rh) + dot(hot, rl)
        first, second = got[:, :128].reshape(16, 8, 128), got[:, 128:].reshape(16, 8, 128)
        even = jnp.where(upper, first, pltpu.roll(second, 4, 1))
        odd = jnp.where(upper, pltpu.roll(first, 4, 1), second)
        abuf[rows(part * 256, 256), :] = jnp.stack([even, odd], axis=1).reshape(256, 128)

    barrier = pltpu.get_barrier_semaphore()

    def greet(k, carry):
        d = lax.rem(me + k, 128)
        pl.semaphore_signal(barrier, inc=1, device_id=(lax.div(d, 4), lax.rem(d, 4)), device_id_type=MESH)
        return carry

    lax.fori_loop(1, 128, greet, 0)
    for t in range(3):
        lp_copy(t).start()
    srhs_copy.start()
    pl.semaphore_wait(barrier, 127)

    def a2a(k, carry):
        d = lax.rem(me + k, 128)
        pltpu.make_async_remote_copy(
            src_ref=abuf.at[rows(d * 8, 8)], dst_ref=xbuf.at[rows(me * 8, 8)],
            send_sem=a2a_sem.at[0], recv_sem=a2a_sem.at[1],
            device_id=(lax.div(d, 4), lax.rem(d, 4)), device_id_type=MESH).start()
        return carry

    lax.fori_loop(1, 128, a2a, 0)
    xbuf[rows(me * 8, 8), :] = abuf[rows(me * 8, 8), :]
    inv_copy.start()
    for m in range(3):
        @pl.when(m < n_pan)
        def _():
            sp_copy(jnp.int32(m)).start()
    pltpu.make_async_copy(xbuf.at[pl.ds(0, 1016)], xbuf.at[pl.ds(0, 1016)], a2a_sem.at[1]).wait()

    raw = xbuf[...].reshape(64, 2, 8, 128)
    first, second = raw[:, 0], raw[:, 1]
    upper = lax.broadcasted_iota(jnp.int32, (64, 8, 128), 1) < 4
    left = jnp.where(upper, first, pltpu.roll(second, 4, 1)).reshape(512, 128)
    right = jnp.where(upper, pltpu.roll(first, 4, 1), second).reshape(512, 128)
    for half, value in enumerate((left, right)):
        high, low = split(value)
        xh[:, half * 128:(half + 1) * 128] = high
        xl[:, half * 128:(half + 1) * 128] = low

    l_copy.wait()

    def leaf_block(r, dst):
        def body(i, carry):
            dst[rows(i * 256, 256), :] = dot3(lbuf[rows(r * 512 + i * 256, 256), :], xh[...], xl[...])
            return carry
        lax.fori_loop(0, 2, body, 0)

    def to_sibling(slot):
        return pltpu.make_async_remote_copy(
            src_ref=zs.at[slot], dst_ref=zr.at[slot], send_sem=zs_sem.at[slot], recv_sem=zr_sem.at[slot],
            device_id=(leaf, sib), device_id_type=MESH)

    def across():
        return pltpu.make_async_remote_copy(
            src_ref=zs.at[2], dst_ref=za, send_sem=zs_sem.at[2], recv_sem=za_sem,
            device_id=(leaf, 2 + c), device_id_type=MESH)

    @pl.when(yh == 0)
    def _():
        leaf_block(3 - c, zs.at[0])
        to_sibling(0).start()
        leaf_block(2 + c, zs.at[2])
        to_sibling(0).wait_recv()
        zs[2] = zs[2] + zr[0]
        across().start()

        @pl.when(c == 0)
        def _():
            leaf_block(1, zs.at[1])
            to_sibling(1).start()

    @pl.when((yh == 1) & (c == 0))
    def _():
        leaf_block(3, zs.at[1])
        to_sibling(1).start()

    leaf_block(grid, ybuf)

    @pl.when(c == 1)
    def _():
        to_sibling(1).wait_recv()
        ybuf[...] = ybuf[...] + zr[1]

    @pl.when(yh == 1)
    def _():
        across().wait_recv()
        ybuf[...] = ybuf[...] + za[...]

    y_out = pltpu.make_async_copy(ybuf, leafy_hbm, out_sem.at[0])
    y_out.start()

    y_left, y_right = ybuf[:, :128], ybuf[:, 128:]
    for_0, for_1 = packed_pair(y_left, y_right)
    mine = jnp.where(c == 0, for_0, for_1)
    other = jnp.where(c == 0, for_1, for_0)
    own[0, pl.ds(1024, 8), :] = jnp.broadcast_to(jnp.sum(mine * mine, axis=0, keepdims=True), (8, 128))
    snd[0, pl.ds(1024, 8), :] = jnp.broadcast_to(jnp.sum(other * other, axis=0, keepdims=True), (8, 128))
    for half, value in enumerate((mine, other)):
        high, low = split(value)
        yh_s[:, half * 128:(half + 1) * 128] = high
        yl_s[:, half * 128:(half + 1) * 128] = low

    def u_copy(t):
        size = 1032 if t == 0 else 1024
        return pltpu.make_async_remote_copy(
            src_ref=snd.at[t, pl.ds(0, size)], dst_ref=rcv.at[t, pl.ds(0, size)],
            send_sem=us_sem.at[t], recv_sem=ur_sem.at[t], device_id=(leaf, sib), device_id_type=MESH)

    def send_pieces(src, base, size, to_leaf, sems, recv_sem):
        for to_yh in range(2):
            to_me = (to_leaf == leaf) & (yh == to_yh)

            @pl.when(to_me)
            def _():
                ubuf[rows(base, size), :] = src[to_yh]

            @pl.when(jnp.logical_not(to_me))
            def _():
                pltpu.make_async_remote_copy(
                    src_ref=src.at[to_yh], dst_ref=ubuf.at[rows(base, size)],
                    send_sem=sems.at[to_yh], recv_sem=recv_sem,
                    device_id=(to_leaf, to_yh * 2 + c), device_id_type=MESH).start()

    def wait_pieces(src, base, size, to_leaf, sems):
        for to_yh in range(2):
            @pl.when(jnp.logical_not((to_leaf == leaf) & (yh == to_yh)))
            def _():
                pltpu.make_async_copy(src.at[to_yh], src.at[to_yh], sems.at[to_yh]).wait()

    leaf_1 = leaf - yl
    leaf_2 = (x * 4 + z - lax.rem(z, 2)) * 2 + 1
    leaf_3 = x * 8 + 3
    half_z = lax.rem(z, 2)
    piece_1 = (pk1, y * 520, 520, leaf_1, ps_sem)
    piece_2 = (s2.at[0], half_z * 256 + y * 64, 64, leaf_2, p3_sem.at[0])

    def piece_3(t):
        return (s2.at[t - 1, :, pl.ds(0, 32)], (t - 2) * 512 + z * 128 + y * 32, 32, leaf_3, p3_sem.at[t - 1])

    def pair_copy():
        return pltpu.make_async_remote_copy(
            src_ref=own.at[1, rows((1 - half_z) * 512, 512)], dst_ref=zpair,
            send_sem=pair_sem.at[0], recv_sem=pair_sem.at[1],
            device_id=((x * 4 + z + 1 - 2 * half_z) * 2 + yl, grid), device_id_type=MESH)

    def rs_copy(t, k):
        at = z if t < 4 else x
        q = lax.rem(at + k, 4)
        to_leaf = (x * 4 + q) * 2 + yl if t < 4 else (q * 4 + z) * 2 + yl
        return pltpu.make_async_remote_copy(
            src_ref=own.at[t, rows(q * 256, 256)], dst_ref=zrs.at[t - 2, 3 - k],
            send_sem=rs_sem.at[t - 2, k - 1], recv_sem=rr_sem.at[t - 2, 3 - k],
            device_id=(to_leaf, grid), device_id_type=MESH)

    def y_copy(t, k, size):
        q = lax.rem(y + k, 4)
        return pltpu.make_async_remote_copy(
            src_ref=pk.at[t - 1, :, rows(q * size, size)], dst_ref=yrs.at[t - 1, 3 - k, :, pl.ds(0, size)],
            send_sem=ys_sem.at[t - 1, k - 1], recv_sem=yr_sem.at[t - 1, 3 - k],
            device_id=((x * 4 + z) * 2 + lax.rem(q, 2), lax.div(q, 2) * 2 + c), device_id_type=MESH)

    def spread(t):
        u_copy(t).wait_recv()
        if t == 0:
            def body(i, carry):
                base = i * 256
                top = own[t, rows(base, 128), :] + rcv[t, rows(base, 128), :]
                bottom = own[t, rows(base + 128, 128), :] + rcv[t, rows(base + 128, 128), :]
                p0, p1 = packed_pair(top, bottom)
                pk1[0, rows(i * 128, 128), :] = p0
                pk1[1, rows(i * 128, 128), :] = p1
                return carry
            lax.fori_loop(0, 4, body, 0)
            squares = own[0, pl.ds(1024, 8), :] + rcv[0, pl.ds(1024, 8), :]
            pk1[0, pl.ds(512, 8), :] = squares
            pk1[1, pl.ds(512, 8), :] = turned(squares)
            send_pieces(*piece_1, u_sem.at[0])
        else:
            def body(i, carry):
                part = rows(i * 256, 256)
                own[t, part, :] = own[t, part, :] + rcv[t, part, :]
                return carry
            lax.fori_loop(0, 4, body, 0)
            if t == 1:
                pair_copy().start()
            else:
                for k in range(1, 4):
                    rs_copy(t, k).start()

    for t in range(6):
        lp_copy(t).wait()
        masks = [jnp.full((1, 256), mask_ref[t, b].astype(F32)).astype(BF16) for b in range(4)]
        masked = lambda ref: jnp.concatenate(
            [ref[b * 128:(b + 1) * 128, :] * masks[b] for b in range(4)], axis=0)
        y_high, y_low = masked(yh_s), masked(yl_s)
        xh[...] = y_high
        xl[...] = y_low

        def body(i, carry):
            part = rows(i * 256, 256)
            product = dot3(pbuf[t % 3, part, :], xh[...], xl[...])
            own[t, part, :] = product[:, :128]
            snd[t, part, :] = product[:, 128:]
            return carry
        lax.fori_loop(0, 4, body, 0)
        if t + 3 < 6:
            lp_copy(t + 3).start()
        u_copy(t).start()
        if t > 0:
            spread(t - 1)
    spread(5)

    def ring_start(t, size):
        for k in range(1, 4):
            y_copy(t, k, size).start()

    def first_sum_2():
        pair_copy().wait_recv()
        for i in range(2):
            base = half_z * 512 + i * 256
            top = own[1, rows(base, 128), :] + zpair[pl.ds(i * 256, 128), :]
            bottom = own[1, rows(base + 128, 128), :] + zpair[pl.ds(i * 256 + 128, 128), :]
            p0, p1 = packed_pair(top, bottom)
            pk[0, 0, pl.ds(i * 128, 128), :] = p0
            pk[0, 1, pl.ds(i * 128, 128), :] = p1
        ring_start(1, 64)

    def first_sum(t):
        for k in range(3):
            pltpu.make_async_copy(zrs.at[t - 2, k], zrs.at[t - 2, k], rr_sem.at[t - 2, k]).wait()
        base = jnp.where(t < 4, z, x) * 256

        def total(start):
            value = own[t, rows(base + start, 128), :]
            for k in range(3):
                value = value + zrs[t - 2, k, pl.ds(start, 128), :]
            return value
        p0, p1 = packed_pair(total(0), total(128))
        pk[t - 1, 0, pl.ds(0, 128), :] = p0
        pk[t - 1, 1, pl.ds(0, 128), :] = p1
        ring_start(t, 32)

    def second_sum(t, size):
        for k in range(3):
            ref = yrs.at[t - 1, k, :, pl.ds(0, size)]
            pltpu.make_async_copy(ref, ref, yr_sem.at[t - 1, k]).wait()
        value = pk[t - 1, :, rows(y * size, size), :]
        for k in range(3):
            value = value + yrs[t - 1, k, :, pl.ds(0, size), :]
        s2[t - 1, :, pl.ds(0, size), :] = value
        if size == 64:
            send_pieces(*piece_2, u_sem.at[0])
        else:
            send_pieces(*piece_3(t), u_sem.at[t - 2])

    def up_copy(m, i, size):
        part = rows(i * 128, size)
        return pltpu.make_async_remote_copy(
            src_ref=csend.at[m, part], dst_ref=crecv.at[side, m, part],
            send_sem=cs_sem.at[m, i], recv_sem=cr_sem.at[side, m, i], device_id=(parent, grid), device_id_type=MESH)

    def wait_child(s, m, i, size):
        part = rows(i * 128, size)
        pltpu.make_async_copy(csend.at[m, part], crecv.at[s, m, part], cr_sem.at[s, m, i]).wait()

    def wait_whole(s, m):
        ref = crecv.at[s, m, pl.ds(0, 512)]
        pltpu.make_async_copy(ref, ref, cr_sem.at[s, m, 0]).wait()

    def take_3(k, dst):
        start = k * 512
        pltpu.make_async_copy(ubuf.at[pl.ds(0, 480)], ubuf.at[pl.ds(0, 480)], u_sem.at[k]).wait()

        @pl.when(k < 2)
        def _():
            dst[...] = ubuf[rows(start, 512), :]

        @pl.when(k >= 2)
        def _():
            value = ubuf[rows(start, 128), :]
            for s in range(1, 4):
                value = value + ubuf[rows(start + s * 128, 128), :]
            dst[...] = jnp.zeros_like(dst)
            dst[rows(x * 128, 128), :] = value

    def far_copy():
        return pltpu.make_async_remote_copy(
            src_ref=csend.at[1, pl.ds(0, 512)], dst_ref=grecv.at[place],
            send_sem=cs_sem.at[1, 0], recv_sem=g_sem.at[place], device_id=(above, grid), device_id_type=MESH)

    def whole_copy(m):
        return pltpu.make_async_remote_copy(
            src_ref=csend.at[m, pl.ds(0, 512)], dst_ref=crecv.at[side, m, pl.ds(0, 512)],
            send_sem=cs_sem.at[m, 0], recv_sem=cr_sem.at[side, m, 0], device_id=(parent, grid), device_id_type=MESH)

    def take_far(slot):
        pltpu.make_async_copy(grecv.at[slot], grecv.at[slot], g_sem.at[slot]).wait()
        accp[...] = accp[...] + grecv[slot]

    def dot2(a, which, part):
        high, low = split(a)
        return dot(high, vcat[which, part, :]) + dot(low, vh0[which, part, :])

    def stacked(value, which, part):
        left = lane_left(value.shape)
        high, low = split(value)
        vcat[which, part, :] = jnp.where(left, high.astype(F32), low.astype(F32)).astype(BF16)
        vh0[which, part, :] = jnp.where(left, high.astype(F32), 0.0).astype(BF16)

    def finished(product, m, i):
        total = product + turned(product)
        part = rows(i * 128, 128)
        csend[m, part, :] = jnp.where(lane_left((128, 128)), total[:128], total[128:])

        @pl.when(level == 3)
        def _():
            csend[m, part, :] = csend[m, part, :] + pend[part, :]

    def head():
        squares[...] = jnp.zeros_like(squares)

        @pl.when(level == 1)
        def _():
            pltpu.make_async_copy(ubuf.at[pl.ds(0, 1560)], ubuf.at[pl.ds(0, 1560)], u_sem.at[0]).wait()
            accp[...] = ubuf[0:512, :] + ubuf[520:1032, :] + ubuf[1040:1552, :] + ubuf[1560:2072, :]
            squares[...] = ubuf[512:520, :] + ubuf[1032:1040, :] + ubuf[1552:1560, :] + ubuf[2072:2080, :]

        @pl.when(level == 2)
        def _():
            pltpu.make_async_copy(ubuf.at[pl.ds(0, 448)], ubuf.at[pl.ds(0, 448)], u_sem.at[0]).wait()
            accp[...] = ubuf[0:512, :]

        @pl.when(level == 3)
        def _():
            take_3(0, accp)
            take_3(1, pend)

        @pl.when(level > 3)
        def _():
            accp[...] = jnp.zeros_like(accp)

        @pl.when(level > 2)
        def _():
            take_far(0)
            take_far(1)

        @pl.when((level > 2) & (level < 6))
        def _():
            take_far(2)
            take_far(3)

        @pl.when(n_pan > 0)
        def _():
            sp_copy(jnp.int32(0)).wait()

        for k in range(4):
            packed = pl.ds(k * 128, 128)
            size = 136 if k == 3 else 128

            @pl.when(level > 1)
            def _():
                wait_child(0, 0, k, size)
                accp[packed, :] = accp[packed, :] + crecv[0, 0, packed, :]

            @pl.when((level > 1) & (level < 6))
            def _():
                wait_child(1, 0, k, size)
                accp[packed, :] = accp[packed, :] + crecv[1, 0, packed, :]

            left = lane_left((128, 128))
            for j, value in enumerate(unpacked(accp[packed, :])):
                part = pl.ds(k * 256 + j * 128, 128)
                right_side = rhsp[part, :]
                stacked(jnp.where(left, right_side, turned(right_side)) - value, 0, part)
            part = pl.ds(k * 256, 256)
            product = dot2(invb[part, k * 256:(k + 1) * 256], 0, part)
            if k > 0:
                product = product + racc[part, :]
            s_value = product + turned(product)
            stacked(s_value, 1, part)

            @pl.when(n_pan > 0)
            def _():
                if k < 3:
                    product = dot2(spb[0, :, k * 256:(k + 1) * 256], 1, part)
                    cacc[...] = product if k == 0 else cacc[...] + product
                else:
                    squares[...] = squares[...] + jnp.sum(s_value * s_value, axis=0, keepdims=True)
                    squares[...] = squares[...] + crecv_squares()
                    csend[0, pl.ds(512, 8), :] = squares[...]
                    for i in range(4):
                        out = pl.ds(i * 256, 256)
                        finished(cacc[out, :] + dot2(spb[0, out, k * 256:(k + 1) * 256], 1, part), 0, i)
                        up_copy(0, i, 136 if i == 3 else 128).start()
            solv[part, :] = s_value[:, :64]
            if k < 3:
                squares[...] = squares[...] + jnp.sum(s_value * s_value, axis=0, keepdims=True)
                rest = slice((k + 1) * 256, 1024)
                product = dot2(invb[rest, k * 256:(k + 1) * 256], 0, part)
                racc[rest, :] = product if k == 0 else racc[rest, :] + product
            else:
                @pl.when(level == 6)
                def _():
                    squares[...] = squares[...] + jnp.sum(s_value * s_value, axis=0, keepdims=True) + crecv[0, 0, pl.ds(512, 8), :]

        @pl.when(3 < n_pan)
        def _():
            sp_copy(jnp.int32(3)).start()
        pltpu.make_async_copy(solv, sol_hbm, out_sem.at[1]).start()

    def crecv_squares():
        return jnp.where(level > 1, crecv[0, 0, pl.ds(512, 8), :] + crecv[1, 0, pl.ds(512, 8), :], 0.0)

    def panel(m):
        sp_copy(m).wait()

        @pl.when(level == 3)
        def _():
            take_3(m + 1, pend)
        slot = lax.rem(m, 3)
        for i in range(4):
            out = pl.ds(i * 256, 256)
            finished(dot2(spb[slot, out, :], 1, slice(None)), m, i)

        @pl.when(level > 1)
        def _():
            for s in range(2):
                wait_whole(s, m + 1)
            csend[m, pl.ds(0, 512), :] = csend[m, pl.ds(0, 512), :] + (
                crecv[0, m + 1, pl.ds(0, 512), :] + crecv[1, m + 1, pl.ds(0, 512), :])

        @pl.when(m == 1)
        def _():
            far_copy().start()

        @pl.when(m > 1)
        def _():
            whole_copy(m).start()

        @pl.when(m + 3 < n_pan)
        def _():
            sp_copy(m + 3).start()

    srhs_copy.wait()
    rhsp[:, :64] = rhsv[...]
    inv_copy.wait()

    start_at = jnp.where(level == 1, 0, 5)

    def phase(p, carry):
        @pl.when(p == 0)
        def _():
            first_sum_2()

        @pl.when((p > 0) & (p < 5))
        def _():
            first_sum(p + 1)

        @pl.when(p == 1)
        def _():
            second_sum(1, 64)

        @pl.when((p > 1) & (p < 6))
        def _():
            second_sum(p, 32)

        @pl.when(p == start_at)
        def _():
            head()

        @pl.when((p > start_at) & (p - start_at < n_pan))
        def _():
            panel(p - start_at)
        return carry
    lax.fori_loop(0, 9, phase, 0)

    def width_copy(d):
        return pltpu.make_async_remote_copy(
            src_ref=wsend, dst_ref=wrecv, send_sem=w_sem.at[0], recv_sem=w_sem.at[1],
            device_id=(d, grid), device_id_type=MESH)

    @pl.when(level == 6)
    def _():
        wsend[0] = jnp.sqrt(squares[...] / (32 * 3072) + 1e-06)
        for d in range(31):
            width_copy(d).start()
        width_ref[...] = wsend[0]
        pltpu.make_async_copy(abuf.at[pl.ds(0, 248)], abuf.at[pl.ds(0, 248)], w_sem.at[0]).wait()

    @pl.when(level < 6)
    def _():
        width_copy(0).wait_recv()
        width_ref[...] = wrecv[0]

    pltpu.make_async_copy(abuf.at[pl.ds(0, 1016)], abuf.at[pl.ds(0, 1016)], a2a_sem.at[0]).wait()

    @pl.when(yh == 0)
    def _():
        to_sibling(0).wait_send()
        across().wait_send()

    @pl.when(c == 0)
    def _():
        to_sibling(1).wait_send()
    y_out.wait()
    pltpu.make_async_copy(solv, sol_hbm, out_sem.at[1]).wait()
    for t in range(6):
        u_copy(t).wait_send()
    wait_pieces(*piece_1)
    pair_copy().wait_send()
    for k in range(1, 4):
        y_copy(1, k, 64).wait_send()
    wait_pieces(*piece_2)
    for t in range(2, 6):
        for k in range(1, 4):
            rs_copy(t, k).wait_send()
            y_copy(t, k, 32).wait_send()
        wait_pieces(*piece_3(t))

    def sent(m, carry):
        @pl.when(m == 0)
        def _():
            for i in range(4):
                up_copy(0, i, 136 if i == 3 else 128).wait_send()

        @pl.when(m == 1)
        def _():
            far_copy().wait_send()

        @pl.when(m > 1)
        def _():
            whole_copy(m).wait_send()
        return carry
    lax.fori_loop(0, n_pan, sent, 0)


def local(rhs_rows, order, leaf_inverse, leaf_panels, panel_mask, sep_rhs, sep_inverse, sep_panels):
    vmem = pl.BlockSpec(memory_space=pltpu.VMEM)
    hbm = pl.BlockSpec(memory_space=pl.ANY)
    V = pltpu.VMEM
    leaf_y, solved, width = pl.pallas_call(
        kernel,
        out_shape=(
            jax.ShapeDtypeStruct((512, 256), F32),
            jax.ShapeDtypeStruct((1024, 64), F32),
            jax.ShapeDtypeStruct((8, 128), F32),
        ),
        in_specs=[vmem, pl.BlockSpec(memory_space=pltpu.SMEM), vmem] + [hbm] * 5,
        out_specs=(hbm, hbm, vmem),
        scratch_shapes=[
            V((1024, 128), F32), V((1024, 128), F32),
            V((512, 256), BF16), V((512, 256), BF16),
            V((2048, 512), F32),
            V((3, 512, 256), F32), V((2, 512, 256), F32), V((512, 256), F32),
            V((512, 256), F32), V((512, 256), BF16), V((512, 256), BF16),
            V((3, 1024, 512), F32),
            V((6, 1032, 128), F32), V((6, 1032, 128), F32), V((6, 1032, 128), F32),
            V((4, 3, 256, 128), F32),
            V((2, 520, 128), F32), V((5, 2, 256, 128), F32),
            V((512, 128), F32), V((5, 3, 2, 64, 128), F32),
            V((5, 2, 64, 128), F32), V((4, 512, 128), F32),
            V((2080, 128), F32),
            V((512, 128), F32), V((512, 128), F32), V((8, 128), F32),
            V((1024, 128), F32), V((1024, 128), F32),
            V((1024, 64), F32), V((1024, 128), F32),
            V((2, 1024, 128), BF16), V((2, 1024, 128), BF16),
            V((1024, 64), F32),
            V((1024, 1024), F32), V((3, 1024, 1024), F32),
            V((5, 520, 128), F32), V((2, 5, 520, 128), F32),
            V((1, 8, 128), F32), V((1, 8, 128), F32),
            DMA((3,)), DMA((3,)), DMA((3,)), DMA((2,)), DMA((3,)), DMA((2,)), DMA, DMA((6,)), DMA((6,)),
            DMA((4, 3)), DMA((4, 3)),
            DMA((2,)), DMA((5, 2)), DMA((2,)), DMA((5, 3)), DMA((5, 3)), DMA((4,)), DMA((4,)), DMA((5, 4)), DMA((2, 5, 4)), DMA((2,)), DMA((2,)),
        ],
        compiler_params=pltpu.CompilerParams(
            collective_id=0, has_side_effects=True, vmem_limit_bytes=62 * 2 ** 20),
        cost_estimate=pl.CostEstimate(flops=7 * 10 ** 9, bytes_accessed=44 * 10 ** 6, transcendentals=0),
    )(order.reshape(4, 128), panel_mask[0], rhs_rows, leaf_inverse, leaf_panels[0], sep_rhs[0], sep_inverse[0], sep_panels[0])
    return leaf_y, solved[None], width[0, :64]


def solution(mesh):
    placed = (
        P(("leaf", "grid"), None),
        P(("leaf", "grid")),
        P("leaf", "grid"),
        P("leaf", None, None, "grid"),
        P("leaf", None, "grid"),
        P("leaf", None, "grid"),
        P("leaf", None, None),
        P("leaf", None, None, None),
    )
    return jax.shard_map(
        local,
        mesh=mesh,
        in_specs=placed,
        out_specs=(P(("leaf", "grid"), None), P("leaf", None, "grid"), P("grid")),
        check_vma=False,
    )
```

```python
import jax
import jax.numpy as jnp
from jax import lax
from jax.experimental import pallas as pl
from jax.experimental.pallas import tpu as pltpu
from jax.sharding import PartitionSpec as P

F32, BF16 = jnp.float32, jnp.bfloat16
MESH = pl.DeviceIdType.MESH
DMA = pltpu.SemaphoreType.DMA


def split(value):
    high = value.astype(BF16)
    return high, (value - high.astype(F32)).astype(BF16)


def dot(a, b):
    return jnp.dot(a, b, preferred_element_type=F32)


def dot3(a, b_high, b_low):
    high, low = split(a)
    return dot(high, b_high) + dot(high, b_low) + dot(low, b_high)


def lane_left(shape):
    return lax.broadcasted_iota(jnp.int32, shape, 1) < 64


def turned(value):
    return pltpu.roll(value, 64, 1)


def packed_pair(top, bottom):
    left = lane_left(top.shape)
    return jnp.where(left, top, turned(bottom)), jnp.where(left, turned(top), bottom)


def unpacked(value):
    left = lane_left(value.shape)
    other = turned(value)
    return jnp.where(left, value, other), jnp.where(left, other, value)


def rows(start, size, unit=8):
    if isinstance(start, int):
        return pl.ds(start, size)
    return pl.ds(pl.multiple_of(start, unit), size)


def kernel(order_ref, mask_ref, rhs_ref, linv_hbm, lpan_hbm, srhs_hbm, sinv_hbm, span_hbm,
           leafy_hbm, sol_hbm, width_ref,
           abuf, xbuf, xh, xl, lbuf, zs, zr, za, ybuf, yh_s, yl_s, pbuf, own, snd, rcv, zrs,
           pk1, pk, zpair, yrs, s2, grecv, ubuf, accp, pend, squares, cacc, racc, rhsv, rhsp, vcat, vh0, solv, invb, spb, csend, crecv, relay, xrs, qsend, qrecv, top, wsend, wrecv,
           ld_sem, lp_sem, sp_sem, a2a_sem, zs_sem, zr_sem, za_sem, us_sem, ur_sem, rs_sem, rr_sem,
           relay_sem, xr_sem, q_sem, qr_sem, top_sem, ps_sem, p3_sem, pair_sem, ys_sem, yr_sem, g_sem, u_sem, cs_sem, cr_sem, w_sem, out_sem):
    leaf = lax.axis_index("leaf")
    grid = lax.axis_index("grid")
    me = leaf * 4 + grid
    yl = lax.rem(leaf, 2)
    z = lax.rem(lax.div(leaf, 2), 4)
    x = lax.div(leaf, 8)
    yh = lax.div(grid, 2)
    y = yh * 2 + yl
    c = lax.rem(grid, 2)
    sib = yh * 2 + 1 - c

    level = jnp.int32(1)
    for bit in range(1, 6):
        level = level + (lax.rem(leaf + 1, 2 ** bit) == 0).astype(jnp.int32)
    parent = jnp.int32(0)
    for tier in range(1, 6):
        size = 2 ** (tier + 1)
        parent = jnp.where(level == tier, lax.div(leaf, size) * size + 2 ** tier - 1, parent)
    side = (leaf > parent).astype(jnp.int32)
    above = jnp.int32(0)
    for tier in range(1, 5):
        size = 2 ** (tier + 2)
        above = jnp.where(level == tier, lax.div(leaf, size) * size + 2 ** (tier + 1) - 1, above)
    place = (parent > above).astype(jnp.int32) * 2 + side
    n_pan = 6 - level

    l_copy = pltpu.make_async_copy(linv_hbm, lbuf, ld_sem.at[0])
    l_copy.start()
    inv_copy = pltpu.make_async_copy(sinv_hbm, invb, ld_sem.at[1])
    srhs_copy = pltpu.make_async_copy(srhs_hbm, rhsv, ld_sem.at[2])

    def lp_copy(t):
        return pltpu.make_async_copy(lpan_hbm.at[t], pbuf.at[t % 3], lp_sem.at[t % 3])

    def sp_copy(m):
        slot = lax.rem(m, 3)
        return pltpu.make_async_copy(span_hbm.at[m], spb.at[slot], sp_sem.at[slot])

    rh, rl = split(rhs_ref[...])
    index = order_ref[...].astype(F32)
    index = jnp.transpose(jnp.concatenate([index, index], axis=0)).astype(jnp.int32)
    upper = lax.broadcasted_iota(jnp.int32, (16, 8, 128), 1) < 4
    for part in range(4):
        hot = (lax.broadcasted_iota(jnp.int32, (128, 512), 1) == index[:, part:part + 1]).astype(F32).astype(BF16)
        got = dot(hot, rh) + dot(hot, rl)
        first, second = got[:, :128].reshape(16, 8, 128), got[:, 128:].reshape(16, 8, 128)
        even = jnp.where(upper, first, pltpu.roll(second, 4, 1))
        odd = jnp.where(upper, pltpu.roll(first, 4, 1), second)
        abuf[rows(part * 256, 256), :] = jnp.stack([even, odd], axis=1).reshape(256, 128)

    barrier = pltpu.get_barrier_semaphore()

    def greet(k, carry):
        d = lax.rem(me + k, 128)
        pl.semaphore_signal(barrier, inc=1, device_id=(lax.div(d, 4), lax.rem(d, 4)), device_id_type=MESH)
        return carry

    lax.fori_loop(1, 128, greet, 0)
    for t in range(3):
        lp_copy(t).start()
    srhs_copy.start()
    pl.semaphore_wait(barrier, 127)

    def a2a(k, carry):
        d = lax.rem(me + k, 128)
        pltpu.make_async_remote_copy(
            src_ref=abuf.at[rows(d * 8, 8)], dst_ref=xbuf.at[rows(me * 8, 8)],
            send_sem=a2a_sem.at[0], recv_sem=a2a_sem.at[1],
            device_id=(lax.div(d, 4), lax.rem(d, 4)), device_id_type=MESH).start()
        return carry

    lax.fori_loop(1, 128, a2a, 0)
    xbuf[rows(me * 8, 8), :] = abuf[rows(me * 8, 8), :]
    inv_copy.start()
    for m in range(3):
        @pl.when(m < n_pan)
        def _():
            sp_copy(jnp.int32(m)).start()
    pltpu.make_async_copy(xbuf.at[pl.ds(0, 1016)], xbuf.at[pl.ds(0, 1016)], a2a_sem.at[1]).wait()

    raw = xbuf[...].reshape(64, 2, 8, 128)
    first, second = raw[:, 0], raw[:, 1]
    upper = lax.broadcasted_iota(jnp.int32, (64, 8, 128), 1) < 4
    left = jnp.where(upper, first, pltpu.roll(second, 4, 1)).reshape(512, 128)
    right = jnp.where(upper, pltpu.roll(first, 4, 1), second).reshape(512, 128)
    for half, value in enumerate((left, right)):
        high, low = split(value)
        xh[:, half * 128:(half + 1) * 128] = high
        xl[:, half * 128:(half + 1) * 128] = low

    l_copy.wait()

    def leaf_block(r, dst):
        def body(i, carry):
            dst[rows(i * 256, 256), :] = dot3(lbuf[rows(r * 512 + i * 256, 256), :], xh[...], xl[...])
            return carry
        lax.fori_loop(0, 2, body, 0)

    def to_sibling(slot):
        return pltpu.make_async_remote_copy(
            src_ref=zs.at[slot], dst_ref=zr.at[slot], send_sem=zs_sem.at[slot], recv_sem=zr_sem.at[slot],
            device_id=(leaf, sib), device_id_type=MESH)

    def across():
        return pltpu.make_async_remote_copy(
            src_ref=zs.at[2], dst_ref=za, send_sem=zs_sem.at[2], recv_sem=za_sem,
            device_id=(leaf, 2 + c), device_id_type=MESH)

    @pl.when(yh == 0)
    def _():
        leaf_block(3 - c, zs.at[0])
        to_sibling(0).start()
        leaf_block(2 + c, zs.at[2])
        to_sibling(0).wait_recv()
        zs[2] = zs[2] + zr[0]
        across().start()

        @pl.when(c == 0)
        def _():
            leaf_block(1, zs.at[1])
            to_sibling(1).start()

    @pl.when((yh == 1) & (c == 0))
    def _():
        leaf_block(3, zs.at[1])
        to_sibling(1).start()

    leaf_block(grid, ybuf)

    @pl.when(c == 1)
    def _():
        to_sibling(1).wait_recv()
        ybuf[...] = ybuf[...] + zr[1]

    @pl.when(yh == 1)
    def _():
        across().wait_recv()
        ybuf[...] = ybuf[...] + za[...]

    y_out = pltpu.make_async_copy(ybuf, leafy_hbm, out_sem.at[0])
    y_out.start()

    y_left, y_right = ybuf[:, :128], ybuf[:, 128:]
    for_0, for_1 = packed_pair(y_left, y_right)
    mine = jnp.where(c == 0, for_0, for_1)
    other = jnp.where(c == 0, for_1, for_0)
    own[0, pl.ds(1024, 8), :] = jnp.broadcast_to(jnp.sum(mine * mine, axis=0, keepdims=True), (8, 128))
    snd[0, pl.ds(1024, 8), :] = jnp.broadcast_to(jnp.sum(other * other, axis=0, keepdims=True), (8, 128))
    for half, value in enumerate((mine, other)):
        high, low = split(value)
        yh_s[:, half * 128:(half + 1) * 128] = high
        yl_s[:, half * 128:(half + 1) * 128] = low

    def u_copy(t):
        size = 1032 if t == 0 else 1024
        return pltpu.make_async_remote_copy(
            src_ref=snd.at[t, pl.ds(0, size)], dst_ref=rcv.at[t, pl.ds(0, size)],
            send_sem=us_sem.at[t], recv_sem=ur_sem.at[t], device_id=(leaf, sib), device_id_type=MESH)

    def send_pieces(src, base, size, to_leaf, sems, recv_sem):
        for to_yh in range(2):
            to_me = (to_leaf == leaf) & (yh == to_yh)

            @pl.when(to_me)
            def _():
                ubuf[rows(base, size), :] = src[to_yh]

            @pl.when(jnp.logical_not(to_me))
            def _():
                pltpu.make_async_remote_copy(
                    src_ref=src.at[to_yh], dst_ref=ubuf.at[rows(base, size)],
                    send_sem=sems.at[to_yh], recv_sem=recv_sem,
                    device_id=(to_leaf, to_yh * 2 + c), device_id_type=MESH).start()

    def wait_pieces(src, base, size, to_leaf, sems):
        for to_yh in range(2):
            @pl.when(jnp.logical_not((to_leaf == leaf) & (yh == to_yh)))
            def _():
                pltpu.make_async_copy(src.at[to_yh], src.at[to_yh], sems.at[to_yh]).wait()

    leaf_1 = leaf - yl
    leaf_2 = (x * 4 + z - lax.rem(z, 2)) * 2 + 1
    leaf_3 = x * 8 + 3
    half_z = lax.rem(z, 2)
    piece_1 = (pk1, y * 520, 520, leaf_1, ps_sem)
    piece_2 = (s2.at[0], half_z * 256 + y * 64, 64, leaf_2, p3_sem.at[0])

    def piece_3(t):
        return (s2.at[t - 1, :, pl.ds(0, 32)], (t - 2) * 512 + z * 128 + y * 32, 32, leaf_3, p3_sem.at[t - 1])

    def pair_copy():
        return pltpu.make_async_remote_copy(
            src_ref=own.at[1, rows((1 - half_z) * 512, 512)], dst_ref=zpair,
            send_sem=pair_sem.at[0], recv_sem=pair_sem.at[1],
            device_id=((x * 4 + z + 1 - 2 * half_z) * 2 + yl, grid), device_id_type=MESH)

    def rs_copy(t, k):
        at = z if t < 4 else x
        q = lax.rem(at + k, 4)
        to_leaf = (x * 4 + q) * 2 + yl if t < 4 else (q * 4 + z) * 2 + yl
        return pltpu.make_async_remote_copy(
            src_ref=own.at[t, rows(q * 256, 256)], dst_ref=zrs.at[t - 2, 3 - k],
            send_sem=rs_sem.at[t - 2, k - 1], recv_sem=rr_sem.at[t - 2, 3 - k],
            device_id=(to_leaf, grid), device_id_type=MESH)

    def y_copy(t, k, size):
        q = lax.rem(y + k, 4)
        return pltpu.make_async_remote_copy(
            src_ref=pk.at[t - 1, :, rows(q * size, size)], dst_ref=yrs.at[t - 1, 3 - k, :, pl.ds(0, size)],
            send_sem=ys_sem.at[t - 1, k - 1], recv_sem=yr_sem.at[t - 1, 3 - k],
            device_id=((x * 4 + z) * 2 + lax.rem(q, 2), lax.div(q, 2) * 2 + c), device_id_type=MESH)

    def spread(t):
        u_copy(t).wait_recv()
        if t == 0:
            def body(i, carry):
                base = i * 256
                top = own[t, rows(base, 128), :] + rcv[t, rows(base, 128), :]
                bottom = own[t, rows(base + 128, 128), :] + rcv[t, rows(base + 128, 128), :]
                p0, p1 = packed_pair(top, bottom)
                pk1[0, rows(i * 128, 128), :] = p0
                pk1[1, rows(i * 128, 128), :] = p1
                return carry
            lax.fori_loop(0, 4, body, 0)
            squares = own[0, pl.ds(1024, 8), :] + rcv[0, pl.ds(1024, 8), :]
            pk1[0, pl.ds(512, 8), :] = squares
            pk1[1, pl.ds(512, 8), :] = turned(squares)
            send_pieces(*piece_1, u_sem.at[0])
        else:
            def body(i, carry):
                part = rows(i * 256, 256)
                own[t, part, :] = own[t, part, :] + rcv[t, part, :]
                return carry
            lax.fori_loop(0, 4, body, 0)
            if t == 1:
                pair_copy().start()
            else:
                for k in range(1, 4):
                    rs_copy(t, k).start()

    for t in range(6):
        lp_copy(t).wait()
        masks = [jnp.full((1, 256), mask_ref[b, t].astype(F32)).astype(BF16) for b in range(4)]
        masked = lambda ref: jnp.concatenate(
            [ref[b * 128:(b + 1) * 128, :] * masks[b] for b in range(4)], axis=0)
        y_high, y_low = masked(yh_s), masked(yl_s)
        xh[...] = y_high
        xl[...] = y_low

        def body(i, carry):
            part = rows(i * 256, 256)
            product = dot3(pbuf[t % 3, part, :], xh[...], xl[...])
            own[t, part, :] = product[:, :128]
            snd[t, part, :] = product[:, 128:]
            return carry
        lax.fori_loop(0, 4, body, 0)
        if t + 3 < 6:
            lp_copy(t + 3).start()
        u_copy(t).start()
        if t > 0:
            spread(t - 1)
    spread(5)

    def ring_start(t, size):
        for k in range(1, 4):
            y_copy(t, k, size).start()

    def first_sum_2():
        pair_copy().wait_recv()
        for i in range(2):
            base = half_z * 512 + i * 256
            top = own[1, rows(base, 128), :] + zpair[pl.ds(i * 256, 128), :]
            bottom = own[1, rows(base + 128, 128), :] + zpair[pl.ds(i * 256 + 128, 128), :]
            p0, p1 = packed_pair(top, bottom)
            pk[0, 0, pl.ds(i * 128, 128), :] = p0
            pk[0, 1, pl.ds(i * 128, 128), :] = p1
        ring_start(1, 64)

    def first_sum(t):
        for k in range(3):
            pltpu.make_async_copy(zrs.at[t - 2, k], zrs.at[t - 2, k], rr_sem.at[t - 2, k]).wait()
        base = jnp.where(t < 4, z, x) * 256

        def total(start):
            value = own[t, rows(base + start, 128), :]
            for k in range(3):
                value = value + zrs[t - 2, k, pl.ds(start, 128), :]
            return value
        p0, p1 = packed_pair(total(0), total(128))
        pk[t - 1, 0, pl.ds(0, 128), :] = p0
        pk[t - 1, 1, pl.ds(0, 128), :] = p1
        ring_start(t, 32)

    def second_sum(t, size):
        for k in range(3):
            ref = yrs.at[t - 1, k, :, pl.ds(0, size)]
            pltpu.make_async_copy(ref, ref, yr_sem.at[t - 1, k]).wait()
        value = pk[t - 1, :, rows(y * size, size), :]
        for k in range(3):
            value = value + yrs[t - 1, k, :, pl.ds(0, size), :]
        s2[t - 1, :, pl.ds(0, size), :] = value
        if size == 64:
            send_pieces(*piece_2, u_sem.at[0])
        else:
            send_pieces(*piece_3(t), u_sem.at[t - 2])

    def up_copy(i, size):
        part = rows(i * 128, size)
        return pltpu.make_async_remote_copy(
            src_ref=csend.at[0, part], dst_ref=crecv.at[side, part],
            send_sem=cs_sem.at[0, i], recv_sem=cr_sem.at[side, i], device_id=(parent, grid), device_id_type=MESH)

    def wait_child(s, i, size):
        part = rows(i * 128, size)
        pltpu.make_async_copy(csend.at[0, part], crecv.at[s, part], cr_sem.at[s, i]).wait()

    def far_copy():
        return pltpu.make_async_remote_copy(
            src_ref=csend.at[1, pl.ds(0, 512)], dst_ref=grecv.at[place],
            send_sem=cs_sem.at[1, 0], recv_sem=g_sem.at[place], device_id=(above, grid), device_id_type=MESH)

    def relay_copy():
        return pltpu.make_async_remote_copy(
            src_ref=csend.at[2, pl.ds(0, 512)], dst_ref=relay.at[side],
            send_sem=cs_sem.at[2, 0], recv_sem=relay_sem.at[side], device_id=(parent, grid), device_id_type=MESH)

    def x_copy(m, u, k):
        q = lax.rem(x + k, 4)
        return pltpu.make_async_remote_copy(
            src_ref=csend.at[m, rows(q * 128, 128)], dst_ref=xrs.at[u, 3 - k],
            send_sem=cs_sem.at[m, k], recv_sem=xr_sem.at[u, 3 - k],
            device_id=((q * 4 + z) * 2 + yl, grid), device_id_type=MESH)

    def quarter_copy(u):
        return pltpu.make_async_remote_copy(
            src_ref=qsend.at[u], dst_ref=qrecv.at[u, side],
            send_sem=q_sem.at[u], recv_sem=qr_sem.at[u, side], device_id=(parent, grid), device_id_type=MESH)

    def top_copy(u):
        return pltpu.make_async_remote_copy(
            src_ref=qsend.at[u], dst_ref=top.at[rows(x * 128, 128)],
            send_sem=q_sem.at[u], recv_sem=top_sem, device_id=(15 + 16 * u, grid), device_id_type=MESH)

    def x_sum(u):
        for k in range(3):
            pltpu.make_async_copy(xrs.at[u, k], xrs.at[u, k], xr_sem.at[u, k]).wait()
        m = 4 - level + u
        qsend[u] = csend[m, rows(x * 128, 128), :] + xrs[u, 0] + (xrs[u, 1] + xrs[u, 2])

        @pl.when(level > 1)
        def _():
            for s in range(2):
                pltpu.make_async_copy(qrecv.at[u, s], qrecv.at[u, s], qr_sem.at[u, s]).wait()
            qsend[u] = qsend[u] + (qrecv[u, 0] + qrecv[u, 1])

        @pl.when(level < 3)
        def _():
            quarter_copy(u).start()

        @pl.when(level == 3)
        def _():
            pltpu.make_async_copy(ubuf.at[pl.ds(0, 480)], ubuf.at[pl.ds(0, 480)], u_sem.at[2 + u]).wait()
            start = (2 + u) * 512
            value = qsend[u]
            for s in range(4):
                value = value + ubuf[rows(start + s * 128, 128), :]
            qsend[u] = value
            top_copy(u).start()

    def take_3(k, dst):
        pltpu.make_async_copy(ubuf.at[pl.ds(0, 480)], ubuf.at[pl.ds(0, 480)], u_sem.at[k]).wait()
        dst[...] = ubuf[k * 512:(k + 1) * 512, :]

    def take_far(slot):
        pltpu.make_async_copy(grecv.at[slot], grecv.at[slot], g_sem.at[slot]).wait()
        accp[...] = accp[...] + grecv[slot]

    def dot2(a, which, part):
        high, low = split(a)
        return dot(high, vcat[which, part, :]) + dot(low, vh0[which, part, :])

    def stacked(value, which, part):
        left = lane_left(value.shape)
        high, low = split(value)
        vcat[which, part, :] = jnp.where(left, high.astype(F32), low.astype(F32)).astype(BF16)
        vh0[which, part, :] = jnp.where(left, high.astype(F32), 0.0).astype(BF16)

    def finished(product, m, i):
        total = product + turned(product)
        part = rows(i * 128, 128)
        csend[m, part, :] = jnp.where(lane_left((128, 128)), total[:128], total[128:])

    def head():
        squares[...] = jnp.zeros_like(squares)

        @pl.when(level == 1)
        def _():
            pltpu.make_async_copy(ubuf.at[pl.ds(0, 1560)], ubuf.at[pl.ds(0, 1560)], u_sem.at[0]).wait()
            accp[...] = ubuf[0:512, :] + ubuf[520:1032, :] + ubuf[1040:1552, :] + ubuf[1560:2072, :]
            squares[...] = ubuf[512:520, :] + ubuf[1032:1040, :] + ubuf[1552:1560, :] + ubuf[2072:2080, :]

        @pl.when(level == 2)
        def _():
            pltpu.make_async_copy(ubuf.at[pl.ds(0, 448)], ubuf.at[pl.ds(0, 448)], u_sem.at[0]).wait()
            accp[...] = ubuf[0:512, :]

        @pl.when(level == 3)
        def _():
            take_3(0, accp)
            take_3(1, pend)

        @pl.when(level > 3)
        def _():
            accp[...] = jnp.zeros_like(accp)

        @pl.when((level > 2) & (level != 5))
        def _():
            take_far(0)
            take_far(1)

        @pl.when((level == 3) | (level == 4))
        def _():
            take_far(2)
            take_far(3)

        @pl.when(level > 4)
        def _():
            pltpu.make_async_copy(top, top, top_sem).wait()
            accp[...] = accp[...] + top[...]

        @pl.when(n_pan > 0)
        def _():
            sp_copy(jnp.int32(0)).wait()

        for k in range(4):
            packed = pl.ds(k * 128, 128)
            size = 136 if k == 3 else 128

            @pl.when(level > 1)
            def _():
                wait_child(0, k, size)
                accp[packed, :] = accp[packed, :] + crecv[0, packed, :]

            @pl.when((level > 1) & (level < 6))
            def _():
                wait_child(1, k, size)
                accp[packed, :] = accp[packed, :] + crecv[1, packed, :]

            left = lane_left((128, 128))
            for j, value in enumerate(unpacked(accp[packed, :])):
                part = pl.ds(k * 256 + j * 128, 128)
                right_side = rhsp[part, :]
                stacked(jnp.where(left, right_side, turned(right_side)) - value, 0, part)
            part = pl.ds(k * 256, 256)
            product = dot2(invb[part, k * 256:(k + 1) * 256], 0, part)
            if k > 0:
                product = product + racc[part, :]
            s_value = product + turned(product)
            stacked(s_value, 1, part)

            @pl.when(n_pan > 0)
            def _():
                if k < 3:
                    product = dot2(spb[0, :, k * 256:(k + 1) * 256], 1, part)
                    cacc[...] = product if k == 0 else cacc[...] + product
                else:
                    squares[...] = squares[...] + jnp.sum(s_value * s_value, axis=0, keepdims=True)
                    squares[...] = squares[...] + crecv_squares()
                    csend[0, pl.ds(512, 8), :] = squares[...]
                    for i in range(4):
                        out = pl.ds(i * 256, 256)
                        finished(cacc[out, :] + dot2(spb[0, out, k * 256:(k + 1) * 256], 1, part), 0, i)

                        @pl.when(level == 3)
                        def _():
                            up = pl.ds(i * 128, 128)
                            csend[0, up, :] = csend[0, up, :] + pend[up, :]
                        up_copy(i, 136 if i == 3 else 128).start()
            solv[:, k * 256:(k + 1) * 256] = jnp.transpose(s_value)[:64]
            if k < 3:
                squares[...] = squares[...] + jnp.sum(s_value * s_value, axis=0, keepdims=True)
                rest = slice((k + 1) * 256, 1024)
                product = dot2(invb[rest, k * 256:(k + 1) * 256], 0, part)
                racc[rest, :] = product if k == 0 else racc[rest, :] + product
            else:
                @pl.when(level == 6)
                def _():
                    squares[...] = squares[...] + jnp.sum(s_value * s_value, axis=0, keepdims=True) + crecv[0, pl.ds(512, 8), :]

        @pl.when(3 < n_pan)
        def _():
            sp_copy(jnp.int32(3)).start()
        pltpu.make_async_copy(solv, sol_hbm, out_sem.at[1]).start()

    def crecv_squares():
        return jnp.where(level > 1, crecv[0, pl.ds(512, 8), :] + crecv[1, pl.ds(512, 8), :], 0.0)

    def panel(m):
        sp_copy(m).wait()
        slot = lax.rem(m, 3)
        for i in range(4):
            out = pl.ds(i * 256, 256)
            finished(dot2(spb[slot, out, :], 1, slice(None)), m, i)
        over_x = (level < 4) & (m >= 4 - level)

        @pl.when((level == 2) & (m == 1))
        def _():
            for s in range(2):
                pltpu.make_async_copy(relay.at[s], relay.at[s], relay_sem.at[s]).wait()
            csend[1, pl.ds(0, 512), :] = csend[1, pl.ds(0, 512), :] + (relay[0] + relay[1])

        @pl.when((m == 1) & jnp.logical_not(over_x))
        def _():
            far_copy().start()

        @pl.when((level == 1) & (m == 2))
        def _():
            relay_copy().start()

        @pl.when(over_x)
        def _():
            for k in range(1, 4):
                x_copy(m, m - 4 + level, k).start()

        @pl.when(m + 3 < n_pan)
        def _():
            sp_copy(m + 3).start()

    srhs_copy.wait()
    for k in range(4):
        rhsp[k * 256:(k + 1) * 256, :64] = jnp.transpose(rhsv[:, k * 256:(k + 1) * 256])
    inv_copy.wait()

    start_at = jnp.minimum(2 * (level - 1), 5)

    def phase(p, carry):
        @pl.when(p == 0)
        def _():
            first_sum_2()

        @pl.when((p > 0) & (p < 5))
        def _():
            first_sum(p + 1)

        @pl.when(p == 1)
        def _():
            second_sum(1, 64)

        @pl.when((p > 1) & (p < 6))
        def _():
            second_sum(p, 32)

        @pl.when(p == start_at)
        def _():
            head()

        m = p - start_at

        @pl.when((m > 0) & (m < n_pan))
        def _():
            panel(m)

        @pl.when((level < 4) & ((m == 5 - level) | (m == 6 - level)))
        def _():
            x_sum(m - 5 + level)
        return carry
    lax.fori_loop(0, 8, phase, 0)

    def width_copy(d):
        return pltpu.make_async_remote_copy(
            src_ref=wsend, dst_ref=wrecv, send_sem=w_sem.at[0], recv_sem=w_sem.at[1],
            device_id=(d, grid), device_id_type=MESH)

    @pl.when(level == 6)
    def _():
        wsend[0] = jnp.sqrt(squares[...] / (32 * 3072) + 1e-06)
        for d in range(31):
            width_copy(d).start()
        width_ref[...] = wsend[0]
        pltpu.make_async_copy(abuf.at[pl.ds(0, 248)], abuf.at[pl.ds(0, 248)], w_sem.at[0]).wait()

    @pl.when(level < 6)
    def _():
        width_copy(0).wait_recv()
        width_ref[...] = wrecv[0]

    pltpu.make_async_copy(abuf.at[pl.ds(0, 1016)], abuf.at[pl.ds(0, 1016)], a2a_sem.at[0]).wait()

    @pl.when(yh == 0)
    def _():
        to_sibling(0).wait_send()
        across().wait_send()

    @pl.when(c == 0)
    def _():
        to_sibling(1).wait_send()
    y_out.wait()
    pltpu.make_async_copy(solv, sol_hbm, out_sem.at[1]).wait()
    for t in range(6):
        u_copy(t).wait_send()
    wait_pieces(*piece_1)
    pair_copy().wait_send()
    for k in range(1, 4):
        y_copy(1, k, 64).wait_send()
    wait_pieces(*piece_2)
    for t in range(2, 6):
        for k in range(1, 4):
            rs_copy(t, k).wait_send()
            y_copy(t, k, 32).wait_send()
        wait_pieces(*piece_3(t))

    @pl.when(n_pan > 0)
    def _():
        for i in range(4):
            up_copy(i, 136 if i == 3 else 128).wait_send()

    @pl.when((level < 3) | (level == 4))
    def _():
        far_copy().wait_send()

    @pl.when(level == 1)
    def _():
        relay_copy().wait_send()

    @pl.when(level < 4)
    def _():
        for u in range(2):
            for k in range(1, 4):
                x_copy(4 - level + u, u, k).wait_send()
            quarter_copy(u).wait_send()


def write_out(y_in, s_in, w_in, y_out, s_out, w_out, sem):
    first = pltpu.make_async_copy(y_in, y_out, sem.at[0])
    second = pltpu.make_async_copy(s_in, s_out, sem.at[1])
    first.start()
    second.start()
    w_out[...] = w_in[0, :64]
    first.wait()
    second.wait()


def local(rhs_rows, order, leaf_inverse, leaf_panels, panel_mask, sep_rhs, sep_inverse, sep_panels):
    vmem = pl.BlockSpec(memory_space=pltpu.VMEM)
    hbm = pl.BlockSpec(memory_space=pl.ANY)
    V = pltpu.VMEM
    leaf_y, solved, width = pl.pallas_call(
        kernel,
        out_shape=(
            jax.ShapeDtypeStruct((512, 256), F32),
            jax.ShapeDtypeStruct((64, 1024), F32),
            jax.ShapeDtypeStruct((8, 128), F32),
        ),
        in_specs=[vmem, pl.BlockSpec(memory_space=pltpu.SMEM), vmem] + [hbm] * 5,
        out_specs=(hbm, hbm, vmem),
        scratch_shapes=[
            V((1024, 128), F32), V((1024, 128), F32),
            V((512, 256), BF16), V((512, 256), BF16),
            V((2048, 512), F32),
            V((3, 512, 256), F32), V((2, 512, 256), F32), V((512, 256), F32),
            V((512, 256), F32), V((512, 256), BF16), V((512, 256), BF16),
            V((3, 1024, 512), F32),
            V((6, 1032, 128), F32), V((6, 1032, 128), F32), V((6, 1032, 128), F32),
            V((4, 3, 256, 128), F32),
            V((2, 520, 128), F32), V((5, 2, 256, 128), F32),
            V((512, 128), F32), V((5, 3, 2, 64, 128), F32),
            V((5, 2, 64, 128), F32), V((4, 512, 128), F32),
            V((2080, 128), F32),
            V((512, 128), F32), V((512, 128), F32), V((8, 128), F32),
            V((1024, 128), F32), V((1024, 128), F32),
            V((64, 1024), F32), V((1024, 128), F32),
            V((2, 1024, 128), BF16), V((2, 1024, 128), BF16),
            V((64, 1024), F32),
            V((1024, 1024), F32), V((3, 1024, 1024), F32),
            V((5, 520, 128), F32), V((2, 520, 128), F32), V((2, 512, 128), F32),
            V((2, 3, 128, 128), F32), V((2, 128, 128), F32), V((2, 2, 128, 128), F32), V((512, 128), F32),
            V((1, 8, 128), F32), V((1, 8, 128), F32),
            DMA((3,)), DMA((3,)), DMA((3,)), DMA((2,)), DMA((3,)), DMA((2,)), DMA, DMA((6,)), DMA((6,)),
            DMA((4, 3)), DMA((4, 3)),
            DMA((2,)), DMA((2, 3)), DMA((2,)), DMA((2, 2)), DMA,
            DMA((2,)), DMA((5, 2)), DMA((2,)), DMA((5, 3)), DMA((5, 3)), DMA((4,)), DMA((4,)), DMA((5, 4)), DMA((2, 4)), DMA((2,)), DMA((2,)),
        ],
        compiler_params=pltpu.CompilerParams(
            collective_id=0, has_side_effects=True, vmem_limit_bytes=62 * 2 ** 20),
        cost_estimate=pl.CostEstimate(flops=7 * 10 ** 9, bytes_accessed=44 * 10 ** 6, transcendentals=0),
    )(order.reshape(4, 128), panel_mask[0].T, rhs_rows, leaf_inverse, leaf_panels[0], sep_rhs[0].T, sep_inverse[0], sep_panels[0])
    leaf_y, solved, width = pl.pallas_call(
        write_out,
        out_shape=(
            jax.ShapeDtypeStruct((512, 256), F32),
            jax.ShapeDtypeStruct((64, 1024), F32),
            jax.ShapeDtypeStruct((64,), F32),
        ),
        in_specs=[hbm, hbm, vmem],
        out_specs=(hbm, hbm, vmem),
        scratch_shapes=[DMA((2,))],
    )(leaf_y, solved, width)
    return leaf_y, solved.T[None], width


def solution(mesh):
    placed = (
        P(("leaf", "grid"), None),
        P(("leaf", "grid")),
        P("leaf", "grid"),
        P("leaf", None, None, "grid"),
        P("leaf", None, "grid"),
        P("leaf", None, "grid"),
        P("leaf", None, None),
        P("leaf", None, None, None),
    )
    return jax.shard_map(
        local,
        mesh=mesh,
        in_specs=placed,
        out_specs=(P(("leaf", "grid"), None), P("leaf", None, "grid"), P("grid")),
        check_vma=False,
    )
```

```python
import jax
import jax.numpy as jnp
from jax import lax
from jax.experimental import pallas as pl
from jax.experimental.pallas import tpu as pltpu
from jax.sharding import PartitionSpec as P

F32, BF16 = jnp.float32, jnp.bfloat16
MESH = pl.DeviceIdType.MESH
DMA = pltpu.SemaphoreType.DMA


def split(value):
    high = value.astype(BF16)
    return high, (value - high.astype(F32)).astype(BF16)


def dot(a, b):
    return jnp.dot(a, b, preferred_element_type=F32)


def dot3(a, b_high, b_low):
    high, low = split(a)
    return dot(high, b_high) + dot(high, b_low) + dot(low, b_high)


def lane_left(shape):
    return lax.broadcasted_iota(jnp.int32, shape, 1) < 64


def turned(value):
    return pltpu.roll(value, 64, 1)


def packed_pair(top, bottom):
    left = lane_left(top.shape)
    return jnp.where(left, top, turned(bottom)), jnp.where(left, turned(top), bottom)


def unpacked(value):
    left = lane_left(value.shape)
    other = turned(value)
    return jnp.where(left, value, other), jnp.where(left, other, value)


def rows(start, size, unit=8):
    if isinstance(start, int):
        return pl.ds(start, size)
    return pl.ds(pl.multiple_of(start, unit), size)


def kernel(order_ref, mask_ref, rhs_ref, linv_hbm, lpan_hbm, srhs_hbm, sinv_hbm, span_hbm,
           leafy_hbm, sol_hbm, width_ref,
           abuf, xbuf, xh, xl, lbuf, zs, zr, za, ybuf, yh_s, yl_s, pbuf, own, snd, rcv, zrs,
           pk1, pk, zpair, yrs, s2, grecv, ubuf, accp, pend, squares, cacc, racc, rhsv, rhsp, vcat, vh0, solv, invb, spb, csend, crecv, relay, xrs, qsend, qrecv, top, wsend, wrecv,
           ld_sem, lp_sem, sp_sem, a2a_sem, zs_sem, zr_sem, za_sem, us_sem, ur_sem, rs_sem, rr_sem,
           relay_sem, xr_sem, q_sem, qr_sem, top_sem, ps_sem, p3_sem, pair_sem, ys_sem, yr_sem, g_sem, u_sem, cs_sem, cr_sem, w_sem, out_sem):
    leaf = lax.axis_index("leaf")
    grid = lax.axis_index("grid")
    me = leaf * 4 + grid
    yl = lax.rem(leaf, 2)
    z = lax.rem(lax.div(leaf, 2), 4)
    x = lax.div(leaf, 8)
    yh = lax.div(grid, 2)
    y = yh * 2 + yl
    c = lax.rem(grid, 2)
    sib = yh * 2 + 1 - c

    level = jnp.int32(1)
    for bit in range(1, 6):
        level = level + (lax.rem(leaf + 1, 2 ** bit) == 0).astype(jnp.int32)
    parent = jnp.int32(0)
    for tier in range(1, 6):
        size = 2 ** (tier + 1)
        parent = jnp.where(level == tier, lax.div(leaf, size) * size + 2 ** tier - 1, parent)
    side = (leaf > parent).astype(jnp.int32)
    above = jnp.int32(0)
    for tier in range(1, 5):
        size = 2 ** (tier + 2)
        above = jnp.where(level == tier, lax.div(leaf, size) * size + 2 ** (tier + 1) - 1, above)
    place = (parent > above).astype(jnp.int32) * 2 + side
    n_pan = 6 - level

    l_copy = pltpu.make_async_copy(linv_hbm, lbuf, ld_sem.at[0])
    l_copy.start()
    inv_copy = pltpu.make_async_copy(sinv_hbm, invb, ld_sem.at[1])
    srhs_copy = pltpu.make_async_copy(srhs_hbm, rhsv, ld_sem.at[2])

    def lp_copy(t):
        return pltpu.make_async_copy(lpan_hbm.at[t], pbuf.at[t % 3], lp_sem.at[t % 3])

    def sp_copy(m):
        slot = lax.rem(m, 3)
        return pltpu.make_async_copy(span_hbm.at[m], spb.at[slot], sp_sem.at[slot])

    rh, rl = split(rhs_ref[...])
    index = order_ref[...].astype(F32)
    index = jnp.transpose(jnp.concatenate([index, index], axis=0)).astype(jnp.int32)
    upper = lax.broadcasted_iota(jnp.int32, (16, 8, 128), 1) < 4
    for part in range(4):
        hot = (lax.broadcasted_iota(jnp.int32, (128, 512), 1) == index[:, part:part + 1]).astype(F32).astype(BF16)
        got = dot(hot, rh) + dot(hot, rl)
        first, second = got[:, :128].reshape(16, 8, 128), got[:, 128:].reshape(16, 8, 128)
        even = jnp.where(upper, first, pltpu.roll(second, 4, 1))
        odd = jnp.where(upper, pltpu.roll(first, 4, 1), second)
        abuf[rows(part * 256, 256), :] = jnp.stack([even, odd], axis=1).reshape(256, 128)

    barrier = pltpu.get_barrier_semaphore()

    def greet(k, carry):
        d = lax.rem(me + k, 128)
        pl.semaphore_signal(barrier, inc=1, device_id=(lax.div(d, 4), lax.rem(d, 4)), device_id_type=MESH)
        return carry

    lax.fori_loop(1, 128, greet, 0)
    for t in range(3):
        lp_copy(t).start()
    srhs_copy.start()
    pl.semaphore_wait(barrier, 127)

    def a2a(k, carry):
        d = lax.rem(me + k, 128)
        pltpu.make_async_remote_copy(
            src_ref=abuf.at[rows(d * 8, 8)], dst_ref=xbuf.at[rows(me * 8, 8)],
            send_sem=a2a_sem.at[0], recv_sem=a2a_sem.at[1],
            device_id=(lax.div(d, 4), lax.rem(d, 4)), device_id_type=MESH).start()
        return carry

    lax.fori_loop(1, 128, a2a, 0)
    xbuf[rows(me * 8, 8), :] = abuf[rows(me * 8, 8), :]
    inv_copy.start()
    for m in range(3):
        @pl.when(m < n_pan)
        def _():
            sp_copy(jnp.int32(m)).start()
    pltpu.make_async_copy(xbuf.at[pl.ds(0, 1016)], xbuf.at[pl.ds(0, 1016)], a2a_sem.at[1]).wait()

    raw = xbuf[...].reshape(64, 2, 8, 128)
    first, second = raw[:, 0], raw[:, 1]
    upper = lax.broadcasted_iota(jnp.int32, (64, 8, 128), 1) < 4
    left = jnp.where(upper, first, pltpu.roll(second, 4, 1)).reshape(512, 128)
    right = jnp.where(upper, pltpu.roll(first, 4, 1), second).reshape(512, 128)
    for half, value in enumerate((left, right)):
        high, low = split(value)
        xh[:, half * 128:(half + 1) * 128] = high
        xl[:, half * 128:(half + 1) * 128] = low

    l_copy.wait()

    def leaf_block(r, dst):
        def body(i, carry):
            dst[rows(i * 256, 256), :] = dot3(lbuf[rows(r * 512 + i * 256, 256), :], xh[...], xl[...])
            return carry
        lax.fori_loop(0, 2, body, 0)

    def to_sibling(slot):
        return pltpu.make_async_remote_copy(
            src_ref=zs.at[slot], dst_ref=zr.at[slot], send_sem=zs_sem.at[slot], recv_sem=zr_sem.at[slot],
            device_id=(leaf, sib), device_id_type=MESH)

    def across():
        return pltpu.make_async_remote_copy(
            src_ref=zs.at[2], dst_ref=za, send_sem=zs_sem.at[2], recv_sem=za_sem,
            device_id=(leaf, 2 + c), device_id_type=MESH)

    @pl.when(yh == 0)
    def _():
        leaf_block(3 - c, zs.at[0])
        to_sibling(0).start()
        leaf_block(2 + c, zs.at[2])
        to_sibling(0).wait_recv()
        zs[2] = zs[2] + zr[0]
        across().start()

        @pl.when(c == 0)
        def _():
            leaf_block(1, zs.at[1])
            to_sibling(1).start()

    @pl.when((yh == 1) & (c == 0))
    def _():
        leaf_block(3, zs.at[1])
        to_sibling(1).start()

    leaf_block(grid, ybuf)

    @pl.when(c == 1)
    def _():
        to_sibling(1).wait_recv()
        ybuf[...] = ybuf[...] + zr[1]

    @pl.when(yh == 1)
    def _():
        across().wait_recv()
        ybuf[...] = ybuf[...] + za[...]

    y_out = pltpu.make_async_copy(ybuf, leafy_hbm, out_sem.at[0])
    y_out.start()

    y_left, y_right = ybuf[:, :128], ybuf[:, 128:]
    for_0, for_1 = packed_pair(y_left, y_right)
    mine = jnp.where(c == 0, for_0, for_1)
    other = jnp.where(c == 0, for_1, for_0)
    own[0, pl.ds(1024, 8), :] = jnp.broadcast_to(jnp.sum(mine * mine, axis=0, keepdims=True), (8, 128))
    snd[0, pl.ds(1024, 8), :] = jnp.broadcast_to(jnp.sum(other * other, axis=0, keepdims=True), (8, 128))
    for half, value in enumerate((mine, other)):
        high, low = split(value)
        yh_s[:, half * 128:(half + 1) * 128] = high
        yl_s[:, half * 128:(half + 1) * 128] = low

    def u_copy(t):
        size = 1032 if t == 0 else 1024
        return pltpu.make_async_remote_copy(
            src_ref=snd.at[t, pl.ds(0, size)], dst_ref=rcv.at[t, pl.ds(0, size)],
            send_sem=us_sem.at[t], recv_sem=ur_sem.at[t], device_id=(leaf, sib), device_id_type=MESH)

    def send_pieces(src, base, size, to_leaf, sems, recv_sem):
        for to_yh in range(2):
            to_me = (to_leaf == leaf) & (yh == to_yh)

            @pl.when(to_me)
            def _():
                ubuf[rows(base, size), :] = src[to_yh]

            @pl.when(jnp.logical_not(to_me))
            def _():
                pltpu.make_async_remote_copy(
                    src_ref=src.at[to_yh], dst_ref=ubuf.at[rows(base, size)],
                    send_sem=sems.at[to_yh], recv_sem=recv_sem,
                    device_id=(to_leaf, to_yh * 2 + c), device_id_type=MESH).start()

    def wait_pieces(src, base, size, to_leaf, sems):
        for to_yh in range(2):
            @pl.when(jnp.logical_not((to_leaf == leaf) & (yh == to_yh)))
            def _():
                pltpu.make_async_copy(src.at[to_yh], src.at[to_yh], sems.at[to_yh]).wait()

    leaf_1 = leaf - yl
    leaf_2 = (x * 4 + z - lax.rem(z, 2)) * 2 + 1
    leaf_3 = x * 8 + 3
    half_z = lax.rem(z, 2)
    piece_1 = (pk1, y * 520, 520, leaf_1, ps_sem)
    piece_2 = (s2.at[0], half_z * 256 + y * 64, 64, leaf_2, p3_sem.at[0])

    def piece_3(t):
        return (s2.at[t - 1, :, pl.ds(0, 32)], (t - 2) * 512 + z * 128 + y * 32, 32, leaf_3, p3_sem.at[t - 1])

    def pair_copy():
        return pltpu.make_async_remote_copy(
            src_ref=own.at[1, rows((1 - half_z) * 512, 512)], dst_ref=zpair,
            send_sem=pair_sem.at[0], recv_sem=pair_sem.at[1],
            device_id=((x * 4 + z + 1 - 2 * half_z) * 2 + yl, grid), device_id_type=MESH)

    def rs_copy(t, k):
        at = z if t < 4 else x
        q = lax.rem(at + k, 4)
        to_leaf = (x * 4 + q) * 2 + yl if t < 4 else (q * 4 + z) * 2 + yl
        return pltpu.make_async_remote_copy(
            src_ref=own.at[t, rows(q * 256, 256)], dst_ref=zrs.at[t - 2, 3 - k],
            send_sem=rs_sem.at[t - 2, k - 1], recv_sem=rr_sem.at[t - 2, 3 - k],
            device_id=(to_leaf, grid), device_id_type=MESH)

    def y_copy(t, k, size):
        q = lax.rem(y + k, 4)
        return pltpu.make_async_remote_copy(
            src_ref=pk.at[t - 1, :, rows(q * size, size)], dst_ref=yrs.at[t - 1, 3 - k, :, pl.ds(0, size)],
            send_sem=ys_sem.at[t - 1, k - 1], recv_sem=yr_sem.at[t - 1, 3 - k],
            device_id=((x * 4 + z) * 2 + lax.rem(q, 2), lax.div(q, 2) * 2 + c), device_id_type=MESH)

    def spread(t):
        u_copy(t).wait_recv()
        if t == 0:
            def body(i, carry):
                base = i * 256
                top = own[t, rows(base, 128), :] + rcv[t, rows(base, 128), :]
                bottom = own[t, rows(base + 128, 128), :] + rcv[t, rows(base + 128, 128), :]
                p0, p1 = packed_pair(top, bottom)
                pk1[0, rows(i * 128, 128), :] = p0
                pk1[1, rows(i * 128, 128), :] = p1
                return carry
            lax.fori_loop(0, 4, body, 0)
            squares = own[0, pl.ds(1024, 8), :] + rcv[0, pl.ds(1024, 8), :]
            pk1[0, pl.ds(512, 8), :] = squares
            pk1[1, pl.ds(512, 8), :] = turned(squares)
            send_pieces(*piece_1, u_sem.at[0])
        else:
            def body(i, carry):
                part = rows(i * 256, 256)
                own[t, part, :] = own[t, part, :] + rcv[t, part, :]
                return carry
            lax.fori_loop(0, 4, body, 0)
            if t == 1:
                pair_copy().start()
            else:
                for k in range(1, 4):
                    rs_copy(t, k).start()

    for t in range(6):
        lp_copy(t).wait()
        masks = [jnp.full((1, 256), mask_ref[b, t].astype(F32)).astype(BF16) for b in range(4)]
        masked = lambda ref: jnp.concatenate(
            [ref[b * 128:(b + 1) * 128, :] * masks[b] for b in range(4)], axis=0)
        y_high, y_low = masked(yh_s), masked(yl_s)
        xh[...] = y_high
        xl[...] = y_low

        def body(i, carry):
            part = rows(i * 256, 256)
            product = dot3(pbuf[t % 3, part, :], xh[...], xl[...])
            own[t, part, :] = product[:, :128]
            snd[t, part, :] = product[:, 128:]
            return carry
        lax.fori_loop(0, 4, body, 0)
        if t + 3 < 6:
            lp_copy(t + 3).start()
        u_copy(t).start()
        if t > 0:
            spread(t - 1)
    spread(5)

    def ring_start(t, size):
        for k in range(1, 4):
            y_copy(t, k, size).start()

    def first_sum_2():
        pair_copy().wait_recv()
        for i in range(2):
            base = half_z * 512 + i * 256
            top = own[1, rows(base, 128), :] + zpair[pl.ds(i * 256, 128), :]
            bottom = own[1, rows(base + 128, 128), :] + zpair[pl.ds(i * 256 + 128, 128), :]
            p0, p1 = packed_pair(top, bottom)
            pk[0, 0, pl.ds(i * 128, 128), :] = p0
            pk[0, 1, pl.ds(i * 128, 128), :] = p1
        ring_start(1, 64)

    def first_sum(t):
        for k in range(3):
            pltpu.make_async_copy(zrs.at[t - 2, k], zrs.at[t - 2, k], rr_sem.at[t - 2, k]).wait()
        base = jnp.where(t < 4, z, x) * 256

        def total(start):
            value = own[t, rows(base + start, 128), :]
            for k in range(3):
                value = value + zrs[t - 2, k, pl.ds(start, 128), :]
            return value
        p0, p1 = packed_pair(total(0), total(128))
        pk[t - 1, 0, pl.ds(0, 128), :] = p0
        pk[t - 1, 1, pl.ds(0, 128), :] = p1
        ring_start(t, 32)

    def second_sum(t, size):
        for k in range(3):
            ref = yrs.at[t - 1, k, :, pl.ds(0, size)]
            pltpu.make_async_copy(ref, ref, yr_sem.at[t - 1, k]).wait()
        value = pk[t - 1, :, rows(y * size, size), :]
        for k in range(3):
            value = value + yrs[t - 1, k, :, pl.ds(0, size), :]
        s2[t - 1, :, pl.ds(0, size), :] = value
        if size == 64:
            send_pieces(*piece_2, u_sem.at[0])
        else:
            send_pieces(*piece_3(t), u_sem.at[t - 2])

    def up_copy(i, size):
        part = rows(i * 128, size)
        return pltpu.make_async_remote_copy(
            src_ref=csend.at[0, part], dst_ref=crecv.at[side, part],
            send_sem=cs_sem.at[0, i], recv_sem=cr_sem.at[side, i], device_id=(parent, grid), device_id_type=MESH)

    def wait_child(s, i, size):
        part = rows(i * 128, size)
        pltpu.make_async_copy(csend.at[0, part], crecv.at[s, part], cr_sem.at[s, i]).wait()

    def far_copy():
        return pltpu.make_async_remote_copy(
            src_ref=csend.at[1, pl.ds(0, 512)], dst_ref=grecv.at[place],
            send_sem=cs_sem.at[1, 0], recv_sem=g_sem.at[place], device_id=(above, grid), device_id_type=MESH)

    def relay_copy():
        return pltpu.make_async_remote_copy(
            src_ref=csend.at[2, pl.ds(0, 512)], dst_ref=relay.at[side],
            send_sem=cs_sem.at[2, 0], recv_sem=relay_sem.at[side], device_id=(parent, grid), device_id_type=MESH)

    def x_copy(m, u, k):
        q = lax.rem(x + k, 4)
        return pltpu.make_async_remote_copy(
            src_ref=csend.at[m, rows(q * 128, 128)], dst_ref=xrs.at[u, 3 - k],
            send_sem=cs_sem.at[m, k], recv_sem=xr_sem.at[u, 3 - k],
            device_id=((q * 4 + z) * 2 + yl, grid), device_id_type=MESH)

    def quarter_copy(u):
        return pltpu.make_async_remote_copy(
            src_ref=qsend.at[u], dst_ref=qrecv.at[u, side],
            send_sem=q_sem.at[u], recv_sem=qr_sem.at[u, side], device_id=(parent, grid), device_id_type=MESH)

    def top_copy(u):
        return pltpu.make_async_remote_copy(
            src_ref=qsend.at[u], dst_ref=top.at[rows(x * 128, 128)],
            send_sem=q_sem.at[u], recv_sem=top_sem, device_id=(15 + 16 * u, grid), device_id_type=MESH)

    def x_sum(u):
        for k in range(3):
            pltpu.make_async_copy(xrs.at[u, k], xrs.at[u, k], xr_sem.at[u, k]).wait()
        m = 4 - level + u
        qsend[u] = csend[m, rows(x * 128, 128), :] + xrs[u, 0] + (xrs[u, 1] + xrs[u, 2])

        @pl.when(level > 1)
        def _():
            for s in range(2):
                pltpu.make_async_copy(qrecv.at[u, s], qrecv.at[u, s], qr_sem.at[u, s]).wait()
            qsend[u] = qsend[u] + (qrecv[u, 0] + qrecv[u, 1])

        @pl.when(level < 3)
        def _():
            quarter_copy(u).start()

        @pl.when(level == 3)
        def _():
            pltpu.make_async_copy(ubuf.at[pl.ds(0, 480)], ubuf.at[pl.ds(0, 480)], u_sem.at[2 + u]).wait()
            start = (2 + u) * 512
            value = qsend[u]
            for s in range(4):
                value = value + ubuf[rows(start + s * 128, 128), :]
            qsend[u] = value
            top_copy(u).start()

    def take_3(k, dst):
        pltpu.make_async_copy(ubuf.at[pl.ds(0, 480)], ubuf.at[pl.ds(0, 480)], u_sem.at[k]).wait()
        dst[...] = ubuf[k * 512:(k + 1) * 512, :]

    def take_far(slot):
        pltpu.make_async_copy(grecv.at[slot], grecv.at[slot], g_sem.at[slot]).wait()
        accp[...] = accp[...] + grecv[slot]

    def dot2(a, which, part):
        high, low = split(a)
        return dot(high, vcat[which, part, :]) + dot(low, vh0[which, part, :])

    def stacked(value, which, part):
        left = lane_left(value.shape)
        high, low = split(value)
        vcat[which, part, :] = jnp.where(left, high.astype(F32), low.astype(F32)).astype(BF16)
        vh0[which, part, :] = jnp.where(left, high.astype(F32), 0.0).astype(BF16)

    def finished(product, m, i):
        total = product + turned(product)
        part = rows(i * 128, 128)
        csend[m, part, :] = jnp.where(lane_left((128, 128)), total[:128], total[128:])

    def head():
        squares[...] = jnp.zeros_like(squares)

        @pl.when(level == 1)
        def _():
            pltpu.make_async_copy(ubuf.at[pl.ds(0, 1560)], ubuf.at[pl.ds(0, 1560)], u_sem.at[0]).wait()
            accp[...] = ubuf[0:512, :] + ubuf[520:1032, :] + ubuf[1040:1552, :] + ubuf[1560:2072, :]
            squares[...] = ubuf[512:520, :] + ubuf[1032:1040, :] + ubuf[1552:1560, :] + ubuf[2072:2080, :]

        @pl.when(level == 2)
        def _():
            pltpu.make_async_copy(ubuf.at[pl.ds(0, 448)], ubuf.at[pl.ds(0, 448)], u_sem.at[0]).wait()
            accp[...] = ubuf[0:512, :]

        @pl.when(level == 3)
        def _():
            take_3(0, accp)
            take_3(1, pend)

        @pl.when(level > 3)
        def _():
            accp[...] = jnp.zeros_like(accp)

        @pl.when((level > 2) & (level != 5))
        def _():
            take_far(0)
            take_far(1)

        @pl.when((level == 3) | (level == 4))
        def _():
            take_far(2)
            take_far(3)

        @pl.when(level > 4)
        def _():
            pltpu.make_async_copy(top, top, top_sem).wait()
            accp[...] = accp[...] + top[...]

        @pl.when(n_pan > 0)
        def _():
            sp_copy(jnp.int32(0)).wait()

        for k in range(4):
            packed = pl.ds(k * 128, 128)
            size = 136 if k == 3 else 128

            @pl.when(level > 1)
            def _():
                wait_child(0, k, size)
                accp[packed, :] = accp[packed, :] + crecv[0, packed, :]

            @pl.when((level > 1) & (level < 6))
            def _():
                wait_child(1, k, size)
                accp[packed, :] = accp[packed, :] + crecv[1, packed, :]

            left = lane_left((128, 128))
            for j, value in enumerate(unpacked(accp[packed, :])):
                part = pl.ds(k * 256 + j * 128, 128)
                right_side = rhsp[part, :]
                stacked(jnp.where(left, right_side, turned(right_side)) - value, 0, part)
            part = pl.ds(k * 256, 256)
            product = dot2(invb[part, k * 256:(k + 1) * 256], 0, part)
            if k > 0:
                product = product + racc[part, :]
            s_value = product + turned(product)
            stacked(s_value, 1, part)

            @pl.when(n_pan > 0)
            def _():
                if k < 3:
                    product = dot2(spb[0, :, k * 256:(k + 1) * 256], 1, part)
                    cacc[...] = product if k == 0 else cacc[...] + product
                else:
                    squares[...] = squares[...] + jnp.sum(s_value * s_value, axis=0, keepdims=True)
                    squares[...] = squares[...] + crecv_squares()
                    csend[0, pl.ds(512, 8), :] = squares[...]
                    for i in range(4):
                        out = pl.ds(i * 256, 256)
                        finished(cacc[out, :] + dot2(spb[0, out, k * 256:(k + 1) * 256], 1, part), 0, i)

                        @pl.when(level == 3)
                        def _():
                            up = pl.ds(i * 128, 128)
                            csend[0, up, :] = csend[0, up, :] + pend[up, :]
                        up_copy(i, 136 if i == 3 else 128).start()
            solv[:, k * 256:(k + 1) * 256] = jnp.transpose(s_value)[:64]
            if k < 3:
                squares[...] = squares[...] + jnp.sum(s_value * s_value, axis=0, keepdims=True)
                rest = slice((k + 1) * 256, 1024)
                product = dot2(invb[rest, k * 256:(k + 1) * 256], 0, part)
                racc[rest, :] = product if k == 0 else racc[rest, :] + product
            else:
                @pl.when(level == 6)
                def _():
                    squares[...] = squares[...] + jnp.sum(s_value * s_value, axis=0, keepdims=True) + crecv[0, pl.ds(512, 8), :]

        @pl.when(3 < n_pan)
        def _():
            sp_copy(jnp.int32(3)).start()
        pltpu.make_async_copy(solv, sol_hbm, out_sem.at[1]).start()

    def crecv_squares():
        return jnp.where(level > 1, crecv[0, pl.ds(512, 8), :] + crecv[1, pl.ds(512, 8), :], 0.0)

    def panel(m):
        sp_copy(m).wait()
        slot = lax.rem(m, 3)
        for i in range(4):
            out = pl.ds(i * 256, 256)
            finished(dot2(spb[slot, out, :], 1, slice(None)), m, i)
        over_x = (level < 4) & (m >= 4 - level)

        @pl.when((level == 2) & (m == 1))
        def _():
            for s in range(2):
                pltpu.make_async_copy(relay.at[s], relay.at[s], relay_sem.at[s]).wait()
            csend[1, pl.ds(0, 512), :] = csend[1, pl.ds(0, 512), :] + (relay[0] + relay[1])

        @pl.when((m == 1) & jnp.logical_not(over_x))
        def _():
            far_copy().start()

        @pl.when((level == 1) & (m == 2))
        def _():
            relay_copy().start()

        @pl.when(over_x)
        def _():
            for k in range(1, 4):
                x_copy(m, m - 4 + level, k).start()

        @pl.when(m + 3 < n_pan)
        def _():
            sp_copy(m + 3).start()

    srhs_copy.wait()
    for k in range(4):
        rhsp[k * 256:(k + 1) * 256, :64] = jnp.transpose(rhsv[:, k * 256:(k + 1) * 256])
    inv_copy.wait()

    start_at = jnp.minimum(2 * (level - 1), 5)

    def phase(p, carry):
        @pl.when(p == 0)
        def _():
            first_sum_2()

        @pl.when((p > 0) & (p < 5))
        def _():
            first_sum(p + 1)

        @pl.when(p == 1)
        def _():
            second_sum(1, 64)

        @pl.when((p > 1) & (p < 6))
        def _():
            second_sum(p, 32)

        @pl.when(p == start_at)
        def _():
            head()

        m = p - start_at

        @pl.when((m > 0) & (m < n_pan))
        def _():
            panel(m)

        @pl.when((level < 4) & ((m == 5 - level) | (m == 6 - level)))
        def _():
            x_sum(m - 5 + level)
        return carry
    lax.fori_loop(0, 8, phase, 0)

    def width_copy(d):
        return pltpu.make_async_remote_copy(
            src_ref=wsend, dst_ref=wrecv, send_sem=w_sem.at[0], recv_sem=w_sem.at[1],
            device_id=(d, grid), device_id_type=MESH)

    @pl.when(level == 6)
    def _():
        wsend[0] = jnp.sqrt(squares[...] / (32 * 3072) + 1e-06)
        for d in range(31):
            width_copy(d).start()
        width_ref[...] = wsend[0]
        pltpu.make_async_copy(abuf.at[pl.ds(0, 248)], abuf.at[pl.ds(0, 248)], w_sem.at[0]).wait()

    @pl.when(level < 6)
    def _():
        width_copy(0).wait_recv()
        width_ref[...] = wrecv[0]

    pltpu.make_async_copy(abuf.at[pl.ds(0, 1016)], abuf.at[pl.ds(0, 1016)], a2a_sem.at[0]).wait()

    @pl.when(yh == 0)
    def _():
        to_sibling(0).wait_send()
        across().wait_send()

    @pl.when(c == 0)
    def _():
        to_sibling(1).wait_send()
    y_out.wait()
    pltpu.make_async_copy(solv, sol_hbm, out_sem.at[1]).wait()
    for t in range(6):
        u_copy(t).wait_send()
    wait_pieces(*piece_1)
    pair_copy().wait_send()
    for k in range(1, 4):
        y_copy(1, k, 64).wait_send()
    wait_pieces(*piece_2)
    for t in range(2, 6):
        for k in range(1, 4):
            rs_copy(t, k).wait_send()
            y_copy(t, k, 32).wait_send()
        wait_pieces(*piece_3(t))

    @pl.when(n_pan > 0)
    def _():
        for i in range(4):
            up_copy(i, 136 if i == 3 else 128).wait_send()

    @pl.when((level < 3) | (level == 4))
    def _():
        far_copy().wait_send()

    @pl.when(level == 1)
    def _():
        relay_copy().wait_send()

    @pl.when(level < 4)
    def _():
        for u in range(2):
            for k in range(1, 4):
                x_copy(4 - level + u, u, k).wait_send()
            quarter_copy(u).wait_send()


def write_out(y_in, s_in, w_in, y_out, s_out, w_out):
    y_out[...] = y_in[...]
    s_out[...] = s_in[...]
    w_out[...] = w_in[0, :64]


def local(rhs_rows, order, leaf_inverse, leaf_panels, panel_mask, sep_rhs, sep_inverse, sep_panels):
    vmem = pl.BlockSpec(memory_space=pltpu.VMEM)
    hbm = pl.BlockSpec(memory_space=pl.ANY)
    V = pltpu.VMEM
    leaf_y, solved, width = pl.pallas_call(
        kernel,
        out_shape=(
            jax.ShapeDtypeStruct((512, 256), F32),
            jax.ShapeDtypeStruct((64, 1024), F32),
            jax.ShapeDtypeStruct((8, 128), F32),
        ),
        in_specs=[vmem, pl.BlockSpec(memory_space=pltpu.SMEM), vmem] + [hbm] * 5,
        out_specs=(hbm, hbm, vmem),
        scratch_shapes=[
            V((1024, 128), F32), V((1024, 128), F32),
            V((512, 256), BF16), V((512, 256), BF16),
            V((2048, 512), F32),
            V((3, 512, 256), F32), V((2, 512, 256), F32), V((512, 256), F32),
            V((512, 256), F32), V((512, 256), BF16), V((512, 256), BF16),
            V((3, 1024, 512), F32),
            V((6, 1032, 128), F32), V((6, 1032, 128), F32), V((6, 1032, 128), F32),
            V((4, 3, 256, 128), F32),
            V((2, 520, 128), F32), V((5, 2, 256, 128), F32),
            V((512, 128), F32), V((5, 3, 2, 64, 128), F32),
            V((5, 2, 64, 128), F32), V((4, 512, 128), F32),
            V((2080, 128), F32),
            V((512, 128), F32), V((512, 128), F32), V((8, 128), F32),
            V((1024, 128), F32), V((1024, 128), F32),
            V((64, 1024), F32), V((1024, 128), F32),
            V((2, 1024, 128), BF16), V((2, 1024, 128), BF16),
            V((64, 1024), F32),
            V((1024, 1024), F32), V((3, 1024, 1024), F32),
            V((5, 520, 128), F32), V((2, 520, 128), F32), V((2, 512, 128), F32),
            V((2, 3, 128, 128), F32), V((2, 128, 128), F32), V((2, 2, 128, 128), F32), V((512, 128), F32),
            V((1, 8, 128), F32), V((1, 8, 128), F32),
            DMA((3,)), DMA((3,)), DMA((3,)), DMA((2,)), DMA((3,)), DMA((2,)), DMA, DMA((6,)), DMA((6,)),
            DMA((4, 3)), DMA((4, 3)),
            DMA((2,)), DMA((2, 3)), DMA((2,)), DMA((2, 2)), DMA,
            DMA((2,)), DMA((5, 2)), DMA((2,)), DMA((5, 3)), DMA((5, 3)), DMA((4,)), DMA((4,)), DMA((5, 4)), DMA((2, 4)), DMA((2,)), DMA((2,)),
        ],
        compiler_params=pltpu.CompilerParams(
            collective_id=0, has_side_effects=True, vmem_limit_bytes=62 * 2 ** 20),
        cost_estimate=pl.CostEstimate(flops=7 * 10 ** 9, bytes_accessed=44 * 10 ** 6, transcendentals=0),
    )(order.reshape(4, 128), panel_mask[0].T, rhs_rows, leaf_inverse, leaf_panels[0], sep_rhs[0].T, sep_inverse[0], sep_panels[0])
    leaf_y, solved, width = pl.pallas_call(
        write_out,
        out_shape=(
            jax.ShapeDtypeStruct((512, 256), F32),
            jax.ShapeDtypeStruct((64, 1024), F32),
            jax.ShapeDtypeStruct((64,), F32),
        ),
        in_specs=[vmem] * 3,
        out_specs=(vmem,) * 3,
    )(leaf_y, solved, width)
    return leaf_y, solved.T[None], width


def solution(mesh):
    placed = (
        P(("leaf", "grid"), None),
        P(("leaf", "grid")),
        P("leaf", "grid"),
        P("leaf", None, None, "grid"),
        P("leaf", None, "grid"),
        P("leaf", None, "grid"),
        P("leaf", None, None),
        P("leaf", None, None, None),
    )
    return jax.shard_map(
        local,
        mesh=mesh,
        in_specs=placed,
        out_specs=(P(("leaf", "grid"), None), P("leaf", None, "grid"), P("grid")),
        check_vma=False,
    )
```

```python
import jax
import jax.numpy as jnp
from jax import lax
from jax.experimental import pallas as pl
from jax.experimental.pallas import tpu as pltpu
from jax.sharding import PartitionSpec as P

F32, BF16 = jnp.float32, jnp.bfloat16
MESH = pl.DeviceIdType.MESH
DMA = pltpu.SemaphoreType.DMA


def split(value):
    high = value.astype(BF16)
    return high, (value - high.astype(F32)).astype(BF16)


def dot(a, b):
    return jnp.dot(a, b, preferred_element_type=F32)


def dot3(a, b_high, b_low):
    high, low = split(a)
    return dot(high, b_high) + dot(high, b_low) + dot(low, b_high)


def lane_left(shape):
    return lax.broadcasted_iota(jnp.int32, shape, 1) < 64


def turned(value):
    return pltpu.roll(value, 64, 1)


def packed_pair(top, bottom):
    left = lane_left(top.shape)
    return jnp.where(left, top, turned(bottom)), jnp.where(left, turned(top), bottom)


def unpacked(value):
    left = lane_left(value.shape)
    other = turned(value)
    return jnp.where(left, value, other), jnp.where(left, other, value)


def rows(start, size, unit=8):
    if isinstance(start, int):
        return pl.ds(start, size)
    return pl.ds(pl.multiple_of(start, unit), size)


def kernel(order_ref, mask_ref, rhs_ref, linv_hbm, lpan_hbm, srhs_hbm, sinv_hbm, span_hbm,
           leafy_hbm, sol_hbm, width_ref,
           abuf, xbuf, xh, xl, lbuf, zs, zr, za, ybuf, yh_s, yl_s, pbuf, own, snd, rcv, zrs,
           pk1, pk, zpair, yrs, s2, grecv, ubuf, accp, pend, squares, cacc, racc, rhsv, rhsp, vcat, vh0, solv, invb, spb, csend, crecv, third, xrs, qsend, qrecv, top, wsend, wrecv,
           ld_sem, lp_sem, sp_sem, a2a_sem, zs_sem, zr_sem, za_sem, us_sem, ur_sem, rs_sem, rr_sem,
           third_sem, xr_sem, q_sem, qr_sem, top_sem, ps_sem, p3_sem, pair_sem, ys_sem, yr_sem, g_sem, u_sem, cs_sem, cr_sem, w_sem, out_sem):
    leaf = lax.axis_index("leaf")
    grid = lax.axis_index("grid")
    me = leaf * 4 + grid
    yl = lax.rem(leaf, 2)
    z = lax.rem(lax.div(leaf, 2), 4)
    x = lax.div(leaf, 8)
    yh = lax.div(grid, 2)
    y = yh * 2 + yl
    c = lax.rem(grid, 2)
    sib = yh * 2 + 1 - c

    level = jnp.int32(1)
    for bit in range(1, 6):
        level = level + (lax.rem(leaf + 1, 2 ** bit) == 0).astype(jnp.int32)
    parent = jnp.int32(0)
    for tier in range(1, 6):
        size = 2 ** (tier + 1)
        parent = jnp.where(level == tier, lax.div(leaf, size) * size + 2 ** tier - 1, parent)
    side = (leaf > parent).astype(jnp.int32)
    above = jnp.int32(0)
    for tier in range(1, 5):
        size = 2 ** (tier + 2)
        above = jnp.where(level == tier, lax.div(leaf, size) * size + 2 ** (tier + 1) - 1, above)
    place = (parent > above).astype(jnp.int32) * 2 + side
    n_pan = 6 - level

    l_copy = pltpu.make_async_copy(linv_hbm, lbuf, ld_sem.at[0])
    l_copy.start()
    inv_copy = pltpu.make_async_copy(sinv_hbm, invb, ld_sem.at[1])
    srhs_copy = pltpu.make_async_copy(srhs_hbm, rhsv, ld_sem.at[2])

    def lp_copy(t):
        return pltpu.make_async_copy(lpan_hbm.at[t], pbuf.at[t % 3], lp_sem.at[t % 3])

    def sp_copy(m):
        slot = lax.rem(m, 3)
        return pltpu.make_async_copy(span_hbm.at[m], spb.at[slot], sp_sem.at[slot])

    rh, rl = split(rhs_ref[...])
    index = order_ref[...].astype(F32)
    index = jnp.transpose(jnp.concatenate([index, index], axis=0)).astype(jnp.int32)
    upper = lax.broadcasted_iota(jnp.int32, (16, 8, 128), 1) < 4
    for part in range(4):
        hot = (lax.broadcasted_iota(jnp.int32, (128, 512), 1) == index[:, part:part + 1]).astype(F32).astype(BF16)
        got = dot(hot, rh) + dot(hot, rl)
        first, second = got[:, :128].reshape(16, 8, 128), got[:, 128:].reshape(16, 8, 128)
        even = jnp.where(upper, first, pltpu.roll(second, 4, 1))
        odd = jnp.where(upper, pltpu.roll(first, 4, 1), second)
        abuf[rows(part * 256, 256), :] = jnp.stack([even, odd], axis=1).reshape(256, 128)

    barrier = pltpu.get_barrier_semaphore()

    def greet(k, carry):
        d = lax.rem(me + k, 128)
        pl.semaphore_signal(barrier, inc=1, device_id=(lax.div(d, 4), lax.rem(d, 4)), device_id_type=MESH)
        return carry

    lax.fori_loop(1, 128, greet, 0)
    for t in range(3):
        lp_copy(t).start()
    srhs_copy.start()
    pl.semaphore_wait(barrier, 127)

    def a2a(k, carry):
        d = lax.rem(me + k, 128)
        pltpu.make_async_remote_copy(
            src_ref=abuf.at[rows(d * 8, 8)], dst_ref=xbuf.at[rows(me * 8, 8)],
            send_sem=a2a_sem.at[0], recv_sem=a2a_sem.at[1],
            device_id=(lax.div(d, 4), lax.rem(d, 4)), device_id_type=MESH).start()
        return carry

    lax.fori_loop(1, 128, a2a, 0)
    xbuf[rows(me * 8, 8), :] = abuf[rows(me * 8, 8), :]
    inv_copy.start()
    for m in range(3):
        @pl.when(m < n_pan)
        def _():
            sp_copy(jnp.int32(m)).start()
    pltpu.make_async_copy(xbuf.at[pl.ds(0, 1016)], xbuf.at[pl.ds(0, 1016)], a2a_sem.at[1]).wait()

    raw = xbuf[...].reshape(64, 2, 8, 128)
    first, second = raw[:, 0], raw[:, 1]
    upper = lax.broadcasted_iota(jnp.int32, (64, 8, 128), 1) < 4
    left = jnp.where(upper, first, pltpu.roll(second, 4, 1)).reshape(512, 128)
    right = jnp.where(upper, pltpu.roll(first, 4, 1), second).reshape(512, 128)
    for half, value in enumerate((left, right)):
        high, low = split(value)
        xh[:, half * 128:(half + 1) * 128] = high
        xl[:, half * 128:(half + 1) * 128] = low

    l_copy.wait()

    def leaf_block(r, dst):
        def body(i, carry):
            dst[rows(i * 256, 256), :] = dot3(lbuf[rows(r * 512 + i * 256, 256), :], xh[...], xl[...])
            return carry
        lax.fori_loop(0, 2, body, 0)

    def to_sibling(slot):
        return pltpu.make_async_remote_copy(
            src_ref=zs.at[slot], dst_ref=zr.at[slot], send_sem=zs_sem.at[slot], recv_sem=zr_sem.at[slot],
            device_id=(leaf, sib), device_id_type=MESH)

    def across():
        return pltpu.make_async_remote_copy(
            src_ref=zs.at[2], dst_ref=za, send_sem=zs_sem.at[2], recv_sem=za_sem,
            device_id=(leaf, 2 + c), device_id_type=MESH)

    @pl.when(yh == 0)
    def _():
        leaf_block(3 - c, zs.at[0])
        to_sibling(0).start()
        leaf_block(2 + c, zs.at[2])
        to_sibling(0).wait_recv()
        zs[2] = zs[2] + zr[0]
        across().start()

        @pl.when(c == 0)
        def _():
            leaf_block(1, zs.at[1])
            to_sibling(1).start()

    @pl.when((yh == 1) & (c == 0))
    def _():
        leaf_block(3, zs.at[1])
        to_sibling(1).start()

    leaf_block(grid, ybuf)

    @pl.when(c == 1)
    def _():
        to_sibling(1).wait_recv()
        ybuf[...] = ybuf[...] + zr[1]

    @pl.when(yh == 1)
    def _():
        across().wait_recv()
        ybuf[...] = ybuf[...] + za[...]

    y_out = pltpu.make_async_copy(ybuf, leafy_hbm, out_sem.at[0])
    y_out.start()

    y_left, y_right = ybuf[:, :128], ybuf[:, 128:]
    for_0, for_1 = packed_pair(y_left, y_right)
    mine = jnp.where(c == 0, for_0, for_1)
    other = jnp.where(c == 0, for_1, for_0)
    own[0, pl.ds(1024, 8), :] = jnp.broadcast_to(jnp.sum(mine * mine, axis=0, keepdims=True), (8, 128))
    snd[0, pl.ds(1024, 8), :] = jnp.broadcast_to(jnp.sum(other * other, axis=0, keepdims=True), (8, 128))
    for half, value in enumerate((mine, other)):
        high, low = split(value)
        yh_s[:, half * 128:(half + 1) * 128] = high
        yl_s[:, half * 128:(half + 1) * 128] = low

    def u_copy(t):
        size = 1032 if t == 0 else 1024
        return pltpu.make_async_remote_copy(
            src_ref=snd.at[t, pl.ds(0, size)], dst_ref=rcv.at[t, pl.ds(0, size)],
            send_sem=us_sem.at[t], recv_sem=ur_sem.at[t], device_id=(leaf, sib), device_id_type=MESH)

    def send_pieces(src, base, size, to_leaf, sems, recv_sem):
        for to_yh in range(2):
            to_me = (to_leaf == leaf) & (yh == to_yh)

            @pl.when(to_me)
            def _():
                ubuf[rows(base, size), :] = src[to_yh]

            @pl.when(jnp.logical_not(to_me))
            def _():
                pltpu.make_async_remote_copy(
                    src_ref=src.at[to_yh], dst_ref=ubuf.at[rows(base, size)],
                    send_sem=sems.at[to_yh], recv_sem=recv_sem,
                    device_id=(to_leaf, to_yh * 2 + c), device_id_type=MESH).start()

    def wait_pieces(src, base, size, to_leaf, sems):
        for to_yh in range(2):
            @pl.when(jnp.logical_not((to_leaf == leaf) & (yh == to_yh)))
            def _():
                pltpu.make_async_copy(src.at[to_yh], src.at[to_yh], sems.at[to_yh]).wait()

    leaf_1 = leaf - yl
    leaf_2 = (x * 4 + z - lax.rem(z, 2)) * 2 + 1
    leaf_3 = x * 8 + 3
    half_z = lax.rem(z, 2)
    piece_1 = (pk1, y * 520, 520, leaf_1, ps_sem)
    piece_2 = (s2.at[0], half_z * 256 + y * 64, 64, leaf_2, p3_sem.at[0])

    def piece_3(t):
        return (s2.at[t - 1, :, pl.ds(0, 32)], (t - 2) * 512 + z * 128 + y * 32, 32, leaf_3, p3_sem.at[t - 1])

    def pair_copy():
        return pltpu.make_async_remote_copy(
            src_ref=own.at[1, rows((1 - half_z) * 512, 512)], dst_ref=zpair,
            send_sem=pair_sem.at[0], recv_sem=pair_sem.at[1],
            device_id=((x * 4 + z + 1 - 2 * half_z) * 2 + yl, grid), device_id_type=MESH)

    def rs_copy(t, k):
        at = z if t < 4 else x
        q = lax.rem(at + k, 4)
        to_leaf = (x * 4 + q) * 2 + yl if t < 4 else (q * 4 + z) * 2 + yl
        return pltpu.make_async_remote_copy(
            src_ref=own.at[t, rows(q * 256, 256)], dst_ref=zrs.at[t - 2, 3 - k],
            send_sem=rs_sem.at[t - 2, k - 1], recv_sem=rr_sem.at[t - 2, 3 - k],
            device_id=(to_leaf, grid), device_id_type=MESH)

    def y_copy(t, k, size):
        q = lax.rem(y + k, 4)
        return pltpu.make_async_remote_copy(
            src_ref=pk.at[t - 1, :, rows(q * size, size)], dst_ref=yrs.at[t - 1, 3 - k, :, pl.ds(0, size)],
            send_sem=ys_sem.at[t - 1, k - 1], recv_sem=yr_sem.at[t - 1, 3 - k],
            device_id=((x * 4 + z) * 2 + lax.rem(q, 2), lax.div(q, 2) * 2 + c), device_id_type=MESH)

    def spread(t):
        u_copy(t).wait_recv()
        if t == 0:
            def body(i, carry):
                base = i * 256
                top = own[t, rows(base, 128), :] + rcv[t, rows(base, 128), :]
                bottom = own[t, rows(base + 128, 128), :] + rcv[t, rows(base + 128, 128), :]
                p0, p1 = packed_pair(top, bottom)
                pk1[0, rows(i * 128, 128), :] = p0
                pk1[1, rows(i * 128, 128), :] = p1
                return carry
            lax.fori_loop(0, 4, body, 0)
            squares = own[0, pl.ds(1024, 8), :] + rcv[0, pl.ds(1024, 8), :]
            pk1[0, pl.ds(512, 8), :] = squares
            pk1[1, pl.ds(512, 8), :] = turned(squares)
            send_pieces(*piece_1, u_sem.at[0])
        else:
            def body(i, carry):
                part = rows(i * 256, 256)
                own[t, part, :] = own[t, part, :] + rcv[t, part, :]
                return carry
            lax.fori_loop(0, 4, body, 0)
            if t == 1:
                pair_copy().start()
            else:
                for k in range(1, 4):
                    rs_copy(t, k).start()

    for t in range(6):
        lp_copy(t).wait()
        masks = [jnp.full((1, 256), mask_ref[b, t].astype(F32)).astype(BF16) for b in range(4)]
        masked = lambda ref: jnp.concatenate(
            [ref[b * 128:(b + 1) * 128, :] * masks[b] for b in range(4)], axis=0)
        y_high, y_low = masked(yh_s), masked(yl_s)
        xh[...] = y_high
        xl[...] = y_low

        def body(i, carry):
            part = rows(i * 256, 256)
            product = dot3(pbuf[t % 3, part, :], xh[...], xl[...])
            own[t, part, :] = product[:, :128]
            snd[t, part, :] = product[:, 128:]
            return carry
        lax.fori_loop(0, 4, body, 0)
        if t + 3 < 6:
            lp_copy(t + 3).start()
        u_copy(t).start()
        if t > 0:
            spread(t - 1)
    spread(5)

    def ring_start(t, size):
        for k in range(1, 4):
            y_copy(t, k, size).start()

    def first_sum_2():
        pair_copy().wait_recv()
        for i in range(2):
            base = half_z * 512 + i * 256
            top = own[1, rows(base, 128), :] + zpair[pl.ds(i * 256, 128), :]
            bottom = own[1, rows(base + 128, 128), :] + zpair[pl.ds(i * 256 + 128, 128), :]
            p0, p1 = packed_pair(top, bottom)
            pk[0, 0, pl.ds(i * 128, 128), :] = p0
            pk[0, 1, pl.ds(i * 128, 128), :] = p1
        ring_start(1, 64)

    def first_sum(t):
        for k in range(3):
            pltpu.make_async_copy(zrs.at[t - 2, k], zrs.at[t - 2, k], rr_sem.at[t - 2, k]).wait()
        base = jnp.where(t < 4, z, x) * 256

        def total(start):
            value = own[t, rows(base + start, 128), :]
            for k in range(3):
                value = value + zrs[t - 2, k, pl.ds(start, 128), :]
            return value
        p0, p1 = packed_pair(total(0), total(128))
        pk[t - 1, 0, pl.ds(0, 128), :] = p0
        pk[t - 1, 1, pl.ds(0, 128), :] = p1
        ring_start(t, 32)

    def second_sum(t, size):
        for k in range(3):
            ref = yrs.at[t - 1, k, :, pl.ds(0, size)]
            pltpu.make_async_copy(ref, ref, yr_sem.at[t - 1, k]).wait()
        value = pk[t - 1, :, rows(y * size, size), :]
        for k in range(3):
            value = value + yrs[t - 1, k, :, pl.ds(0, size), :]
        s2[t - 1, :, pl.ds(0, size), :] = value
        if size == 64:
            send_pieces(*piece_2, u_sem.at[0])
        else:
            send_pieces(*piece_3(t), u_sem.at[t - 2])

    def up_copy(i, size):
        part = rows(i * 128, size)
        return pltpu.make_async_remote_copy(
            src_ref=csend.at[0, part], dst_ref=crecv.at[side, part],
            send_sem=cs_sem.at[0, i], recv_sem=cr_sem.at[side, i], device_id=(parent, grid), device_id_type=MESH)

    def wait_child(s, i, size):
        part = rows(i * 128, size)
        pltpu.make_async_copy(csend.at[0, part], crecv.at[s, part], cr_sem.at[s, i]).wait()

    def far_copy():
        return pltpu.make_async_remote_copy(
            src_ref=csend.at[1, pl.ds(0, 512)], dst_ref=grecv.at[place],
            send_sem=cs_sem.at[1, 0], recv_sem=g_sem.at[place], device_id=(above, grid), device_id_type=MESH)

    def ring_copy(m, u, k):
        over_z = u < 2
        q = lax.rem(jnp.where(over_z, z, x) + k, 4)
        return pltpu.make_async_remote_copy(
            src_ref=csend.at[m, rows(q * 128, 128)], dst_ref=xrs.at[u, 3 - k],
            send_sem=cs_sem.at[m, k], recv_sem=xr_sem.at[u, 3 - k],
            device_id=((jnp.where(over_z, x, q) * 4 + jnp.where(over_z, q, z)) * 2 + yl, grid), device_id_type=MESH)

    def side_copy(u):
        return pltpu.make_async_remote_copy(
            src_ref=qsend.at[u], dst_ref=third.at[u, rows(z * 128, 128)],
            send_sem=q_sem.at[u], recv_sem=third_sem.at[u], device_id=(leaf_3, grid), device_id_type=MESH)

    def quarter_copy(u):
        return pltpu.make_async_remote_copy(
            src_ref=qsend.at[u], dst_ref=qrecv.at[u - 2, side],
            send_sem=q_sem.at[u], recv_sem=qr_sem.at[u - 2, side], device_id=(parent, grid), device_id_type=MESH)

    def top_copy(u):
        return pltpu.make_async_remote_copy(
            src_ref=qsend.at[u], dst_ref=top.at[rows(x * 128, 128)],
            send_sem=q_sem.at[u], recv_sem=top_sem, device_id=(16 * u - 17, grid), device_id_type=MESH)

    def ring_sum(u):
        for k in range(3):
            pltpu.make_async_copy(xrs.at[u, k], xrs.at[u, k], xr_sem.at[u, k]).wait()
        m = 2 - level + u
        base = jnp.where(u < 2, z, x) * 128
        qsend[u] = csend[m, rows(base, 128), :] + xrs[u, 0] + (xrs[u, 1] + xrs[u, 2])

        @pl.when(u < 2)
        def _():
            side_copy(u).start()

        @pl.when(level > 1)
        def _():
            for s in range(2):
                pltpu.make_async_copy(qrecv.at[u - 2, s], qrecv.at[u - 2, s], qr_sem.at[u - 2, s]).wait()
            qsend[u] = qsend[u] + (qrecv[u - 2, 0] + qrecv[u - 2, 1])

        @pl.when((u > 1) & (level < 3))
        def _():
            quarter_copy(u).start()

        @pl.when(level == 3)
        def _():
            pltpu.make_async_copy(ubuf.at[pl.ds(0, 480)], ubuf.at[pl.ds(0, 480)], u_sem.at[u]).wait()
            start = u * 512
            value = qsend[u]
            for s in range(4):
                value = value + ubuf[rows(start + s * 128, 128), :]
            qsend[u] = value
            top_copy(u).start()

    def take_3(k, dst):
        pltpu.make_async_copy(ubuf.at[pl.ds(0, 480)], ubuf.at[pl.ds(0, 480)], u_sem.at[k]).wait()
        pltpu.make_async_copy(third.at[k], third.at[k], third_sem.at[k]).wait()
        dst[...] = ubuf[k * 512:(k + 1) * 512, :] + third[k]

    def take_far(slot):
        pltpu.make_async_copy(grecv.at[slot], grecv.at[slot], g_sem.at[slot]).wait()
        accp[...] = accp[...] + grecv[slot]

    def dot2(a, which, part):
        high, low = split(a)
        return dot(high, vcat[which, part, :]) + dot(low, vh0[which, part, :])

    def stacked(value, which, part):
        left = lane_left(value.shape)
        high, low = split(value)
        vcat[which, part, :] = jnp.where(left, high.astype(F32), low.astype(F32)).astype(BF16)
        vh0[which, part, :] = jnp.where(left, high.astype(F32), 0.0).astype(BF16)

    def finished(product, m, i):
        total = product + turned(product)
        part = rows(i * 128, 128)
        csend[m, part, :] = jnp.where(lane_left((128, 128)), total[:128], total[128:])

    def head():
        squares[...] = jnp.zeros_like(squares)

        @pl.when(level == 1)
        def _():
            pltpu.make_async_copy(ubuf.at[pl.ds(0, 1560)], ubuf.at[pl.ds(0, 1560)], u_sem.at[0]).wait()
            accp[...] = ubuf[0:512, :] + ubuf[520:1032, :] + ubuf[1040:1552, :] + ubuf[1560:2072, :]
            squares[...] = ubuf[512:520, :] + ubuf[1032:1040, :] + ubuf[1552:1560, :] + ubuf[2072:2080, :]

        @pl.when(level == 2)
        def _():
            pltpu.make_async_copy(ubuf.at[pl.ds(0, 448)], ubuf.at[pl.ds(0, 448)], u_sem.at[0]).wait()
            accp[...] = ubuf[0:512, :]

        @pl.when(level == 3)
        def _():
            take_3(0, accp)

        @pl.when(level > 3)
        def _():
            accp[...] = jnp.zeros_like(accp)

        @pl.when((level == 4) | (level == 6))
        def _():
            take_far(0)
            take_far(1)

        @pl.when(level == 4)
        def _():
            take_far(2)
            take_far(3)

        @pl.when(level > 4)
        def _():
            pltpu.make_async_copy(top, top, top_sem).wait()
            accp[...] = accp[...] + top[...]

        @pl.when(n_pan > 0)
        def _():
            sp_copy(jnp.int32(0)).wait()

        for k in range(4):
            packed = pl.ds(k * 128, 128)
            size = 136 if k == 3 else 128

            @pl.when(level > 1)
            def _():
                wait_child(0, k, size)
                accp[packed, :] = accp[packed, :] + crecv[0, packed, :]

            @pl.when((level > 1) & (level < 6))
            def _():
                wait_child(1, k, size)
                accp[packed, :] = accp[packed, :] + crecv[1, packed, :]

            left = lane_left((128, 128))
            for j, value in enumerate(unpacked(accp[packed, :])):
                part = pl.ds(k * 256 + j * 128, 128)
                right_side = rhsp[part, :]
                stacked(jnp.where(left, right_side, turned(right_side)) - value, 0, part)
            part = pl.ds(k * 256, 256)
            product = dot2(invb[part, k * 256:(k + 1) * 256], 0, part)
            if k > 0:
                product = product + racc[part, :]
            s_value = product + turned(product)
            stacked(s_value, 1, part)

            @pl.when(n_pan > 0)
            def _():
                if k < 3:
                    product = dot2(spb[0, :, k * 256:(k + 1) * 256], 1, part)
                    cacc[...] = product if k == 0 else cacc[...] + product
                else:
                    squares[...] = squares[...] + jnp.sum(s_value * s_value, axis=0, keepdims=True)
                    squares[...] = squares[...] + crecv_squares()
                    csend[0, pl.ds(512, 8), :] = squares[...]

                    @pl.when(level == 3)
                    def _():
                        take_3(1, pend)
                    for i in range(4):
                        out = pl.ds(i * 256, 256)
                        finished(cacc[out, :] + dot2(spb[0, out, k * 256:(k + 1) * 256], 1, part), 0, i)

                        @pl.when(level == 3)
                        def _():
                            up = pl.ds(i * 128, 128)
                            csend[0, up, :] = csend[0, up, :] + pend[up, :]
                        up_copy(i, 136 if i == 3 else 128).start()
            solv[:, k * 256:(k + 1) * 256] = jnp.transpose(s_value)[:64]
            if k < 3:
                squares[...] = squares[...] + jnp.sum(s_value * s_value, axis=0, keepdims=True)
                rest = slice((k + 1) * 256, 1024)
                product = dot2(invb[rest, k * 256:(k + 1) * 256], 0, part)
                racc[rest, :] = product if k == 0 else racc[rest, :] + product
            else:
                @pl.when(level == 6)
                def _():
                    squares[...] = squares[...] + jnp.sum(s_value * s_value, axis=0, keepdims=True) + crecv[0, pl.ds(512, 8), :]

        @pl.when(3 < n_pan)
        def _():
            sp_copy(jnp.int32(3)).start()
        pltpu.make_async_copy(solv, sol_hbm, out_sem.at[1]).start()

    def crecv_squares():
        return jnp.where(level > 1, crecv[0, pl.ds(512, 8), :] + crecv[1, pl.ds(512, 8), :], 0.0)

    def panel(m):
        sp_copy(m).wait()
        slot = lax.rem(m, 3)
        for i in range(4):
            out = pl.ds(i * 256, 256)
            finished(dot2(spb[slot, out, :], 1, slice(None)), m, i)
        far = (m == 1) & ((level == 2) | (level == 4))

        @pl.when(far)
        def _():
            far_copy().start()

        @pl.when(jnp.logical_not(far))
        def _():
            for k in range(1, 4):
                ring_copy(m, m + level - 2, k).start()

        @pl.when(m + 3 < n_pan)
        def _():
            sp_copy(m + 3).start()

    srhs_copy.wait()
    for k in range(4):
        rhsp[k * 256:(k + 1) * 256, :64] = jnp.transpose(rhsv[:, k * 256:(k + 1) * 256])
    inv_copy.wait()

    start_at = jnp.minimum(2 * (level - 1), 5)

    def phase(p, carry):
        @pl.when(p == 0)
        def _():
            first_sum_2()

        @pl.when(p < 4)
        def _():
            first_sum(p + 2)

        @pl.when(p == 1)
        def _():
            second_sum(1, 64)

        @pl.when((p > 1) & (p < 6))
        def _():
            second_sum(p, 32)

        @pl.when(p == start_at)
        def _():
            head()

        m = p - start_at

        @pl.when((m > 0) & (m < n_pan))
        def _():
            panel(m)

        u = m + level - 3

        @pl.when((level < 4) & (u < 4) & ((u > 1) | ((level == 1) & (u >= 0))))
        def _():
            ring_sum(u)
        return carry
    lax.fori_loop(0, 8, phase, 0)

    def width_copy(d):
        return pltpu.make_async_remote_copy(
            src_ref=wsend, dst_ref=wrecv, send_sem=w_sem.at[0], recv_sem=w_sem.at[1],
            device_id=(d, grid), device_id_type=MESH)

    @pl.when(level == 6)
    def _():
        wsend[0] = jnp.sqrt(squares[...] / (32 * 3072) + 1e-06)
        for d in range(31):
            width_copy(d).start()
        width_ref[...] = wsend[0]
        pltpu.make_async_copy(abuf.at[pl.ds(0, 248)], abuf.at[pl.ds(0, 248)], w_sem.at[0]).wait()

    @pl.when(level < 6)
    def _():
        width_copy(0).wait_recv()
        width_ref[...] = wrecv[0]

    pltpu.make_async_copy(abuf.at[pl.ds(0, 1016)], abuf.at[pl.ds(0, 1016)], a2a_sem.at[0]).wait()

    @pl.when(yh == 0)
    def _():
        to_sibling(0).wait_send()
        across().wait_send()

    @pl.when(c == 0)
    def _():
        to_sibling(1).wait_send()
    y_out.wait()
    pltpu.make_async_copy(solv, sol_hbm, out_sem.at[1]).wait()
    for t in range(6):
        u_copy(t).wait_send()
    wait_pieces(*piece_1)
    pair_copy().wait_send()
    for k in range(1, 4):
        y_copy(1, k, 64).wait_send()
    wait_pieces(*piece_2)
    for t in range(2, 6):
        for k in range(1, 4):
            rs_copy(t, k).wait_send()
            y_copy(t, k, 32).wait_send()
        wait_pieces(*piece_3(t))

    @pl.when(n_pan > 0)
    def _():
        for i in range(4):
            up_copy(i, 136 if i == 3 else 128).wait_send()

    @pl.when((level == 2) | (level == 4))
    def _():
        far_copy().wait_send()

    def sent(u, carry):
        for k in range(1, 4):
            ring_copy(2 - level + u, u, k).wait_send()
        pltpu.make_async_copy(qsend.at[u], qsend.at[u], q_sem.at[u]).wait()
        return carry
    lax.fori_loop(jnp.where(level == 1, 0, jnp.where(level < 4, 2, 4)), 4, sent, 0)


def write_out(y_in, s_in, w_in, y_out, s_out, w_out):
    y_out[...] = y_in[...]
    s_out[...] = s_in[...]
    w_out[...] = w_in[0, :64]


def local(rhs_rows, order, leaf_inverse, leaf_panels, panel_mask, sep_rhs, sep_inverse, sep_panels):
    vmem = pl.BlockSpec(memory_space=pltpu.VMEM)
    hbm = pl.BlockSpec(memory_space=pl.ANY)
    V = pltpu.VMEM
    leaf_y, solved, width = pl.pallas_call(
        kernel,
        out_shape=(
            jax.ShapeDtypeStruct((512, 256), F32),
            jax.ShapeDtypeStruct((64, 1024), F32),
            jax.ShapeDtypeStruct((8, 128), F32),
        ),
        in_specs=[vmem, pl.BlockSpec(memory_space=pltpu.SMEM), vmem] + [hbm] * 5,
        out_specs=(hbm, hbm, vmem),
        scratch_shapes=[
            V((1024, 128), F32), V((1024, 128), F32),
            V((512, 256), BF16), V((512, 256), BF16),
            V((2048, 512), F32),
            V((3, 512, 256), F32), V((2, 512, 256), F32), V((512, 256), F32),
            V((512, 256), F32), V((512, 256), BF16), V((512, 256), BF16),
            V((3, 1024, 512), F32),
            V((6, 1032, 128), F32), V((6, 1032, 128), F32), V((6, 1032, 128), F32),
            V((4, 3, 256, 128), F32),
            V((2, 520, 128), F32), V((5, 2, 256, 128), F32),
            V((512, 128), F32), V((5, 3, 2, 64, 128), F32),
            V((5, 2, 64, 128), F32), V((4, 512, 128), F32),
            V((2080, 128), F32),
            V((512, 128), F32), V((512, 128), F32), V((8, 128), F32),
            V((1024, 128), F32), V((1024, 128), F32),
            V((64, 1024), F32), V((1024, 128), F32),
            V((2, 1024, 128), BF16), V((2, 1024, 128), BF16),
            V((64, 1024), F32),
            V((1024, 1024), F32), V((3, 1024, 1024), F32),
            V((5, 520, 128), F32), V((2, 520, 128), F32), V((2, 512, 128), F32),
            V((4, 3, 128, 128), F32), V((4, 128, 128), F32), V((2, 2, 128, 128), F32), V((512, 128), F32),
            V((1, 8, 128), F32), V((1, 8, 128), F32),
            DMA((3,)), DMA((3,)), DMA((3,)), DMA((2,)), DMA((3,)), DMA((2,)), DMA, DMA((6,)), DMA((6,)),
            DMA((4, 3)), DMA((4, 3)),
            DMA((2,)), DMA((4, 3)), DMA((4,)), DMA((2, 2)), DMA,
            DMA((2,)), DMA((5, 2)), DMA((2,)), DMA((5, 3)), DMA((5, 3)), DMA((4,)), DMA((4,)), DMA((5, 4)), DMA((2, 4)), DMA((2,)), DMA((2,)),
        ],
        compiler_params=pltpu.CompilerParams(
            collective_id=0, has_side_effects=True, vmem_limit_bytes=62 * 2 ** 20),
        cost_estimate=pl.CostEstimate(flops=7 * 10 ** 9, bytes_accessed=44 * 10 ** 6, transcendentals=0),
    )(order.reshape(4, 128), panel_mask[0].T, rhs_rows, leaf_inverse, leaf_panels[0], sep_rhs[0].T, sep_inverse[0], sep_panels[0])
    leaf_y, solved, width = pl.pallas_call(
        write_out,
        out_shape=(
            jax.ShapeDtypeStruct((512, 256), F32),
            jax.ShapeDtypeStruct((64, 1024), F32),
            jax.ShapeDtypeStruct((64,), F32),
        ),
        in_specs=[vmem] * 3,
        out_specs=(vmem,) * 3,
    )(leaf_y, solved, width)
    return leaf_y, solved.T[None], width


def solution(mesh):
    placed = (
        P(("leaf", "grid"), None),
        P(("leaf", "grid")),
        P("leaf", "grid"),
        P("leaf", None, None, "grid"),
        P("leaf", None, "grid"),
        P("leaf", None, "grid"),
        P("leaf", None, None),
        P("leaf", None, None, None),
    )
    return jax.shard_map(
        local,
        mesh=mesh,
        in_specs=placed,
        out_specs=(P(("leaf", "grid"), None), P("leaf", None, "grid"), P("grid")),
        check_vma=False,
    )
```

```python
import jax
import jax.numpy as jnp
from jax import lax
from jax.experimental import pallas as pl
from jax.experimental.pallas import tpu as pltpu
from jax.sharding import PartitionSpec as P

F32, BF16 = jnp.float32, jnp.bfloat16
MESH = pl.DeviceIdType.MESH
DMA = pltpu.SemaphoreType.DMA


def split(value):
    high = value.astype(BF16)
    return high, (value - high.astype(F32)).astype(BF16)


def dot(a, b):
    return jnp.dot(a, b, preferred_element_type=F32)


def dot3(a, b_high, b_low):
    high, low = split(a)
    return dot(high, b_high) + dot(high, b_low) + dot(low, b_high)


def lane_left(shape):
    return lax.broadcasted_iota(jnp.int32, shape, 1) < 64


def turned(value):
    return pltpu.roll(value, 64, 1)


def packed_pair(top, bottom):
    left = lane_left(top.shape)
    return jnp.where(left, top, turned(bottom)), jnp.where(left, turned(top), bottom)


def unpacked(value):
    left = lane_left(value.shape)
    other = turned(value)
    return jnp.where(left, value, other), jnp.where(left, other, value)


def rows(start, size, unit=8):
    if isinstance(start, int):
        return pl.ds(start, size)
    return pl.ds(pl.multiple_of(start, unit), size)


def kernel(order_ref, mask_ref, rhs_ref, linv_hbm, lpan_hbm, srhs_hbm, sinv_hbm, span_hbm,
           leafy_hbm, sol_hbm, width_ref,
           abuf, xbuf, xh, xl, lbuf, zs, zr, za, ybuf, yh_s, yl_s, pbuf, own, snd, rcv, zrs,
           pk1, pk, zpair, yrs, s2, grecv, ubuf, accp, pend, squares, cacc, racc, rhsv, rhsp, vcat, vh0, solv, invb, spb, csend, crecv, third, xrs, qsend, qrecv, top, wsend, wrecv,
           ld_sem, lp_sem, sp_sem, a2a_sem, zs_sem, zr_sem, za_sem, us_sem, ur_sem, rs_sem, rr_sem,
           third_sem, xr_sem, q_sem, qr_sem, top_sem, ps_sem, p3_sem, pair_sem, ys_sem, yr_sem, g_sem, u_sem, cs_sem, cr_sem, w_sem, out_sem):
    leaf = lax.axis_index("leaf")
    grid = lax.axis_index("grid")
    me = leaf * 4 + grid
    yl = lax.rem(leaf, 2)
    z = lax.rem(lax.div(leaf, 2), 4)
    x = lax.div(leaf, 8)
    yh = lax.div(grid, 2)
    y = yh * 2 + yl
    c = lax.rem(grid, 2)
    sib = yh * 2 + 1 - c

    level = jnp.int32(1)
    for bit in range(1, 6):
        level = level + (lax.rem(leaf + 1, 2 ** bit) == 0).astype(jnp.int32)
    parent = jnp.int32(0)
    for tier in range(1, 6):
        size = 2 ** (tier + 1)
        parent = jnp.where(level == tier, lax.div(leaf, size) * size + 2 ** tier - 1, parent)
    side = (leaf > parent).astype(jnp.int32)
    above = jnp.int32(0)
    for tier in range(1, 5):
        size = 2 ** (tier + 2)
        above = jnp.where(level == tier, lax.div(leaf, size) * size + 2 ** (tier + 1) - 1, above)
    place = (parent > above).astype(jnp.int32) * 2 + side
    n_pan = 6 - level

    l_copy = pltpu.make_async_copy(linv_hbm, lbuf, ld_sem.at[0])
    l_copy.start()
    inv_copy = pltpu.make_async_copy(sinv_hbm, invb, ld_sem.at[1])
    srhs_copy = pltpu.make_async_copy(srhs_hbm, rhsv, ld_sem.at[2])

    def lp_copy(t):
        return pltpu.make_async_copy(lpan_hbm.at[t], pbuf.at[t % 3], lp_sem.at[t % 3])

    def sp_copy(m):
        slot = lax.rem(m, 3)
        return pltpu.make_async_copy(span_hbm.at[m], spb.at[slot], sp_sem.at[slot])

    rh, rl = split(rhs_ref[...])
    index = order_ref[...].astype(F32)
    index = jnp.transpose(jnp.concatenate([index, index], axis=0)).astype(jnp.int32)
    upper = lax.broadcasted_iota(jnp.int32, (16, 8, 128), 1) < 4
    for part in range(4):
        hot = (lax.broadcasted_iota(jnp.int32, (128, 512), 1) == index[:, part:part + 1]).astype(F32).astype(BF16)
        got = dot(hot, rh) + dot(hot, rl)
        first, second = got[:, :128].reshape(16, 8, 128), got[:, 128:].reshape(16, 8, 128)
        even = jnp.where(upper, first, pltpu.roll(second, 4, 1))
        odd = jnp.where(upper, pltpu.roll(first, 4, 1), second)
        abuf[rows(part * 256, 256), :] = jnp.stack([even, odd], axis=1).reshape(256, 128)

    barrier = pltpu.get_barrier_semaphore()

    def greet(k, carry):
        d = lax.rem(me + k, 128)
        pl.semaphore_signal(barrier, inc=1, device_id=(lax.div(d, 4), lax.rem(d, 4)), device_id_type=MESH)
        return carry

    lax.fori_loop(1, 128, greet, 0)
    for t in range(3):
        lp_copy(t).start()
    srhs_copy.start()
    pl.semaphore_wait(barrier, 127)

    def a2a(k, carry):
        d = lax.rem(me + k, 128)
        pltpu.make_async_remote_copy(
            src_ref=abuf.at[rows(d * 8, 8)], dst_ref=xbuf.at[rows(me * 8, 8)],
            send_sem=a2a_sem.at[0], recv_sem=a2a_sem.at[1],
            device_id=(lax.div(d, 4), lax.rem(d, 4)), device_id_type=MESH).start()
        return carry

    lax.fori_loop(1, 128, a2a, 0)
    xbuf[rows(me * 8, 8), :] = abuf[rows(me * 8, 8), :]
    inv_copy.start()
    for m in range(3):
        @pl.when(m < n_pan)
        def _():
            sp_copy(jnp.int32(m)).start()
    pltpu.make_async_copy(xbuf.at[pl.ds(0, 1016)], xbuf.at[pl.ds(0, 1016)], a2a_sem.at[1]).wait()

    raw = xbuf[...].reshape(64, 2, 8, 128)
    first, second = raw[:, 0], raw[:, 1]
    upper = lax.broadcasted_iota(jnp.int32, (64, 8, 128), 1) < 4
    left = jnp.where(upper, first, pltpu.roll(second, 4, 1)).reshape(512, 128)
    right = jnp.where(upper, pltpu.roll(first, 4, 1), second).reshape(512, 128)
    for half, value in enumerate((left, right)):
        high, low = split(value)
        xh[:, half * 128:(half + 1) * 128] = high
        xl[:, half * 128:(half + 1) * 128] = low

    l_copy.wait()

    def leaf_block(r, dst):
        def body(i, carry):
            dst[rows(i * 256, 256), :] = dot3(lbuf[rows(r * 512 + i * 256, 256), :], xh[...], xl[...])
            return carry
        lax.fori_loop(0, 2, body, 0)

    def to_sibling(slot):
        return pltpu.make_async_remote_copy(
            src_ref=zs.at[slot], dst_ref=zr.at[slot], send_sem=zs_sem.at[slot], recv_sem=zr_sem.at[slot],
            device_id=(leaf, sib), device_id_type=MESH)

    def across():
        return pltpu.make_async_remote_copy(
            src_ref=zs.at[2], dst_ref=za, send_sem=zs_sem.at[2], recv_sem=za_sem,
            device_id=(leaf, 2 + c), device_id_type=MESH)

    @pl.when(yh == 0)
    def _():
        leaf_block(3 - c, zs.at[0])
        to_sibling(0).start()
        leaf_block(2 + c, zs.at[2])
        to_sibling(0).wait_recv()
        zs[2] = zs[2] + zr[0]
        across().start()

        @pl.when(c == 0)
        def _():
            leaf_block(1, zs.at[1])
            to_sibling(1).start()

    @pl.when((yh == 1) & (c == 0))
    def _():
        leaf_block(3, zs.at[1])
        to_sibling(1).start()

    leaf_block(grid, ybuf)

    @pl.when(c == 1)
    def _():
        to_sibling(1).wait_recv()
        ybuf[...] = ybuf[...] + zr[1]

    @pl.when(yh == 1)
    def _():
        across().wait_recv()
        ybuf[...] = ybuf[...] + za[...]

    y_out = pltpu.make_async_copy(ybuf, leafy_hbm, out_sem.at[0])
    y_out.start()

    y_left, y_right = ybuf[:, :128], ybuf[:, 128:]
    for_0, for_1 = packed_pair(y_left, y_right)
    mine = jnp.where(c == 0, for_0, for_1)
    other = jnp.where(c == 0, for_1, for_0)
    own[0, pl.ds(1024, 8), :] = jnp.broadcast_to(jnp.sum(mine * mine, axis=0, keepdims=True), (8, 128))
    snd[0, pl.ds(1024, 8), :] = jnp.broadcast_to(jnp.sum(other * other, axis=0, keepdims=True), (8, 128))
    for half, value in enumerate((mine, other)):
        high, low = split(value)
        yh_s[:, half * 128:(half + 1) * 128] = high
        yl_s[:, half * 128:(half + 1) * 128] = low

    def u_copy(t):
        size = 1032 if t == 0 else 1024
        return pltpu.make_async_remote_copy(
            src_ref=snd.at[t, pl.ds(0, size)], dst_ref=rcv.at[t, pl.ds(0, size)],
            send_sem=us_sem.at[t], recv_sem=ur_sem.at[t], device_id=(leaf, sib), device_id_type=MESH)

    def send_pieces(src, base, size, to_leaf, sems, recv_sem):
        for to_yh in range(2):
            to_me = (to_leaf == leaf) & (yh == to_yh)

            @pl.when(to_me)
            def _():
                ubuf[rows(base, size), :] = src[to_yh]

            @pl.when(jnp.logical_not(to_me))
            def _():
                pltpu.make_async_remote_copy(
                    src_ref=src.at[to_yh], dst_ref=ubuf.at[rows(base, size)],
                    send_sem=sems.at[to_yh], recv_sem=recv_sem,
                    device_id=(to_leaf, to_yh * 2 + c), device_id_type=MESH).start()

    def wait_pieces(src, base, size, to_leaf, sems):
        for to_yh in range(2):
            @pl.when(jnp.logical_not((to_leaf == leaf) & (yh == to_yh)))
            def _():
                pltpu.make_async_copy(src.at[to_yh], src.at[to_yh], sems.at[to_yh]).wait()

    leaf_1 = leaf - yl
    leaf_2 = (x * 4 + z - lax.rem(z, 2)) * 2 + 1
    leaf_3 = x * 8 + 3
    half_z = lax.rem(z, 2)
    piece_1 = (pk1, y * 520, 520, leaf_1, ps_sem)
    piece_2 = (s2.at[0], half_z * 256 + y * 64, 64, leaf_2, p3_sem.at[0])

    def piece_3(t):
        return (s2.at[t - 1, :, pl.ds(0, 32)], (t - 2) * 512 + z * 128 + y * 32, 32, leaf_3, p3_sem.at[t - 1])

    def pair_copy():
        return pltpu.make_async_remote_copy(
            src_ref=own.at[1, rows((1 - half_z) * 512, 512)], dst_ref=zpair,
            send_sem=pair_sem.at[0], recv_sem=pair_sem.at[1],
            device_id=((x * 4 + z + 1 - 2 * half_z) * 2 + yl, grid), device_id_type=MESH)

    def rs_copy(t, k):
        at = z if t < 4 else x
        q = lax.rem(at + k, 4)
        to_leaf = (x * 4 + q) * 2 + yl if t < 4 else (q * 4 + z) * 2 + yl
        return pltpu.make_async_remote_copy(
            src_ref=own.at[t, rows(q * 256, 256)], dst_ref=zrs.at[t - 2, 3 - k],
            send_sem=rs_sem.at[t - 2, k - 1], recv_sem=rr_sem.at[t - 2, 3 - k],
            device_id=(to_leaf, grid), device_id_type=MESH)

    def y_copy(t, k, size):
        q = lax.rem(y + k, 4)
        return pltpu.make_async_remote_copy(
            src_ref=pk.at[t - 1, :, rows(q * size, size)], dst_ref=yrs.at[t - 1, 3 - k, :, pl.ds(0, size)],
            send_sem=ys_sem.at[t - 1, k - 1], recv_sem=yr_sem.at[t - 1, 3 - k],
            device_id=((x * 4 + z) * 2 + lax.rem(q, 2), lax.div(q, 2) * 2 + c), device_id_type=MESH)

    def spread(t):
        u_copy(t).wait_recv()
        if t == 0:
            def body(i, carry):
                base = i * 256
                top = own[t, rows(base, 128), :] + rcv[t, rows(base, 128), :]
                bottom = own[t, rows(base + 128, 128), :] + rcv[t, rows(base + 128, 128), :]
                p0, p1 = packed_pair(top, bottom)
                pk1[0, rows(i * 128, 128), :] = p0
                pk1[1, rows(i * 128, 128), :] = p1
                return carry
            lax.fori_loop(0, 4, body, 0)
            squares = own[0, pl.ds(1024, 8), :] + rcv[0, pl.ds(1024, 8), :]
            pk1[0, pl.ds(512, 8), :] = squares
            pk1[1, pl.ds(512, 8), :] = turned(squares)
            send_pieces(*piece_1, u_sem.at[0])
        else:
            def body(i, carry):
                part = rows(i * 256, 256)
                own[t, part, :] = own[t, part, :] + rcv[t, part, :]
                return carry
            lax.fori_loop(0, 4, body, 0)
            if t == 1:
                pair_copy().start()
            else:
                for k in range(1, 4):
                    rs_copy(t, k).start()

    for t in range(6):
        lp_copy(t).wait()
        masks = [jnp.full((1, 256), mask_ref[b, t].astype(F32)).astype(BF16) for b in range(4)]
        masked = lambda ref: jnp.concatenate(
            [ref[b * 128:(b + 1) * 128, :] * masks[b] for b in range(4)], axis=0)
        y_high, y_low = masked(yh_s), masked(yl_s)
        xh[...] = y_high
        xl[...] = y_low

        def body(i, carry):
            part = rows(i * 256, 256)
            product = dot3(pbuf[t % 3, part, :], xh[...], xl[...])
            own[t, part, :] = product[:, :128]
            snd[t, part, :] = product[:, 128:]
            return carry
        lax.fori_loop(0, 4, body, 0)
        if t + 3 < 6:
            lp_copy(t + 3).start()
        u_copy(t).start()
        if t > 0:
            spread(t - 1)
    spread(5)

    def ring_start(t, size):
        for k in range(1, 4):
            y_copy(t, k, size).start()

    def first_sum_2():
        pair_copy().wait_recv()
        for i in range(2):
            base = half_z * 512 + i * 256
            top = own[1, rows(base, 128), :] + zpair[pl.ds(i * 256, 128), :]
            bottom = own[1, rows(base + 128, 128), :] + zpair[pl.ds(i * 256 + 128, 128), :]
            p0, p1 = packed_pair(top, bottom)
            pk[0, 0, pl.ds(i * 128, 128), :] = p0
            pk[0, 1, pl.ds(i * 128, 128), :] = p1
        ring_start(1, 64)

    def first_sum(t):
        for k in range(3):
            pltpu.make_async_copy(zrs.at[t - 2, k], zrs.at[t - 2, k], rr_sem.at[t - 2, k]).wait()
        base = jnp.where(t < 4, z, x) * 256

        def total(start):
            value = own[t, rows(base + start, 128), :]
            for k in range(3):
                value = value + zrs[t - 2, k, pl.ds(start, 128), :]
            return value
        p0, p1 = packed_pair(total(0), total(128))
        pk[t - 1, 0, pl.ds(0, 128), :] = p0
        pk[t - 1, 1, pl.ds(0, 128), :] = p1
        ring_start(t, 32)

    def second_sum(t, size):
        for k in range(3):
            ref = yrs.at[t - 1, k, :, pl.ds(0, size)]
            pltpu.make_async_copy(ref, ref, yr_sem.at[t - 1, k]).wait()
        value = pk[t - 1, :, rows(y * size, size), :]
        for k in range(3):
            value = value + yrs[t - 1, k, :, pl.ds(0, size), :]
        s2[t - 1, :, pl.ds(0, size), :] = value
        if size == 64:
            send_pieces(*piece_2, u_sem.at[0])
        else:
            send_pieces(*piece_3(t), u_sem.at[t - 2])

    def up_copy(i, size):
        part = rows(i * 128, size)
        return pltpu.make_async_remote_copy(
            src_ref=csend.at[0, part], dst_ref=crecv.at[side, part],
            send_sem=cs_sem.at[0, i], recv_sem=cr_sem.at[side, i], device_id=(parent, grid), device_id_type=MESH)

    def wait_child(s, i, size):
        part = rows(i * 128, size)
        pltpu.make_async_copy(csend.at[0, part], crecv.at[s, part], cr_sem.at[s, i]).wait()

    def far_copy():
        return pltpu.make_async_remote_copy(
            src_ref=csend.at[1, pl.ds(0, 512)], dst_ref=grecv.at[place],
            send_sem=cs_sem.at[1, 0], recv_sem=g_sem.at[place], device_id=(above, grid), device_id_type=MESH)

    def ring_copy(m, u, k):
        over_z = u < 2
        q = lax.rem(jnp.where(over_z, z, x) + k, 4)
        return pltpu.make_async_remote_copy(
            src_ref=csend.at[m, rows(q * 128, 128)], dst_ref=xrs.at[u, 3 - k],
            send_sem=cs_sem.at[m, k], recv_sem=xr_sem.at[u, 3 - k],
            device_id=((jnp.where(over_z, x, q) * 4 + jnp.where(over_z, q, z)) * 2 + yl, grid), device_id_type=MESH)

    def side_copy(u):
        return pltpu.make_async_remote_copy(
            src_ref=qsend.at[u], dst_ref=third.at[u, rows(z * 128, 128)],
            send_sem=q_sem.at[u], recv_sem=third_sem.at[u], device_id=(leaf_3, grid), device_id_type=MESH)

    def quarter_copy(u):
        return pltpu.make_async_remote_copy(
            src_ref=qsend.at[u], dst_ref=qrecv.at[u - 2, side],
            send_sem=q_sem.at[u], recv_sem=qr_sem.at[u - 2, side], device_id=(parent, grid), device_id_type=MESH)

    def top_copy(u):
        return pltpu.make_async_remote_copy(
            src_ref=qsend.at[u], dst_ref=top.at[rows(x * 128, 128)],
            send_sem=q_sem.at[u], recv_sem=top_sem, device_id=(16 * u - 17, grid), device_id_type=MESH)

    def ring_sum(u):
        for k in range(3):
            pltpu.make_async_copy(xrs.at[u, k], xrs.at[u, k], xr_sem.at[u, k]).wait()
        m = 2 - level + u
        base = jnp.where(u < 2, z, x) * 128
        qsend[u] = csend[m, rows(base, 128), :] + xrs[u, 0] + (xrs[u, 1] + xrs[u, 2])

        @pl.when(u < 2)
        def _():
            side_copy(u).start()

        @pl.when(level > 1)
        def _():
            for s in range(2):
                pltpu.make_async_copy(qrecv.at[u - 2, s], qrecv.at[u - 2, s], qr_sem.at[u - 2, s]).wait()
            qsend[u] = qsend[u] + (qrecv[u - 2, 0] + qrecv[u - 2, 1])

        @pl.when((u > 1) & (level < 3))
        def _():
            quarter_copy(u).start()

        @pl.when(level == 3)
        def _():
            pltpu.make_async_copy(ubuf.at[pl.ds(0, 480)], ubuf.at[pl.ds(0, 480)], u_sem.at[u]).wait()
            start = u * 512
            value = qsend[u]
            for s in range(4):
                value = value + ubuf[rows(start + s * 128, 128), :]
            qsend[u] = value
            top_copy(u).start()

    def take_3(k, dst):
        pltpu.make_async_copy(ubuf.at[pl.ds(0, 480)], ubuf.at[pl.ds(0, 480)], u_sem.at[k]).wait()
        pltpu.make_async_copy(third.at[k], third.at[k], third_sem.at[k]).wait()
        dst[...] = ubuf[k * 512:(k + 1) * 512, :] + third[k]

    def take_far(slot):
        pltpu.make_async_copy(grecv.at[slot], grecv.at[slot], g_sem.at[slot]).wait()
        accp[...] = accp[...] + grecv[slot]

    def dot2(a, which, part):
        high, low = split(a)
        return dot(high, vcat[which, part, :]) + dot(low, vh0[which, part, :])

    def stacked(value, which, part):
        left = lane_left(value.shape)
        high, low = split(value)
        vcat[which, part, :] = jnp.where(left, high.astype(F32), low.astype(F32)).astype(BF16)
        vh0[which, part, :] = jnp.where(left, high.astype(F32), 0.0).astype(BF16)

    def finished(product, m, i):
        total = product + turned(product)
        part = rows(i * 128, 128)
        csend[m, part, :] = jnp.where(lane_left((128, 128)), total[:128], total[128:])

    def head():
        squares[...] = jnp.zeros_like(squares)

        @pl.when(level == 1)
        def _():
            pltpu.make_async_copy(ubuf.at[pl.ds(0, 1560)], ubuf.at[pl.ds(0, 1560)], u_sem.at[0]).wait()
            accp[...] = ubuf[0:512, :] + ubuf[520:1032, :] + ubuf[1040:1552, :] + ubuf[1560:2072, :]
            squares[...] = ubuf[512:520, :] + ubuf[1032:1040, :] + ubuf[1552:1560, :] + ubuf[2072:2080, :]

        @pl.when(level == 2)
        def _():
            pltpu.make_async_copy(ubuf.at[pl.ds(0, 448)], ubuf.at[pl.ds(0, 448)], u_sem.at[0]).wait()
            accp[...] = ubuf[0:512, :]

        @pl.when(level == 3)
        def _():
            take_3(0, accp)

        @pl.when(level > 3)
        def _():
            accp[...] = jnp.zeros_like(accp)

        @pl.when((level == 4) | (level == 6))
        def _():
            take_far(0)
            take_far(1)

        @pl.when(level == 4)
        def _():
            take_far(2)
            take_far(3)

        @pl.when(level > 4)
        def _():
            pltpu.make_async_copy(top, top, top_sem).wait()
            accp[...] = accp[...] + top[...]

        @pl.when(n_pan > 0)
        def _():
            sp_copy(jnp.int32(0)).wait()

        for k in range(4):
            packed = pl.ds(k * 128, 128)
            size = 136 if k == 3 else 128

            @pl.when(level > 1)
            def _():
                wait_child(0, k, size)
                accp[packed, :] = accp[packed, :] + crecv[0, packed, :]

            @pl.when((level > 1) & (level < 6))
            def _():
                wait_child(1, k, size)
                accp[packed, :] = accp[packed, :] + crecv[1, packed, :]

            left = lane_left((128, 128))
            for j, value in enumerate(unpacked(accp[packed, :])):
                part = pl.ds(k * 256 + j * 128, 128)
                right_side = rhsp[part, :]
                stacked(jnp.where(left, right_side, turned(right_side)) - value, 0, part)
            part = pl.ds(k * 256, 256)
            product = dot2(invb[part, k * 256:(k + 1) * 256], 0, part)
            if k > 0:
                product = product + racc[part, :]
            s_value = product + turned(product)
            stacked(s_value, 1, part)

            @pl.when(n_pan > 0)
            def _():
                if k < 3:
                    product = dot2(spb[0, :, k * 256:(k + 1) * 256], 1, part)
                    cacc[...] = product if k == 0 else cacc[...] + product
                else:
                    squares[...] = squares[...] + jnp.sum(s_value * s_value, axis=0, keepdims=True)
                    squares[...] = squares[...] + crecv_squares()
                    csend[0, pl.ds(512, 8), :] = squares[...]

                    @pl.when(level == 3)
                    def _():
                        take_3(1, pend)
                    for i in range(4):
                        out = pl.ds(i * 256, 256)
                        finished(cacc[out, :] + dot2(spb[0, out, k * 256:(k + 1) * 256], 1, part), 0, i)

                        @pl.when(level == 3)
                        def _():
                            up = pl.ds(i * 128, 128)
                            csend[0, up, :] = csend[0, up, :] + pend[up, :]
                        up_copy(i, 136 if i == 3 else 128).start()
            solv[:, k * 256:(k + 1) * 256] = jnp.transpose(s_value)[:64]
            if k < 3:
                squares[...] = squares[...] + jnp.sum(s_value * s_value, axis=0, keepdims=True)
                rest = slice((k + 1) * 256, 1024)
                product = dot2(invb[rest, k * 256:(k + 1) * 256], 0, part)
                racc[rest, :] = product if k == 0 else racc[rest, :] + product
            else:
                @pl.when(level == 6)
                def _():
                    squares[...] = squares[...] + jnp.sum(s_value * s_value, axis=0, keepdims=True) + crecv[0, pl.ds(512, 8), :]

        @pl.when(3 < n_pan)
        def _():
            sp_copy(jnp.int32(3)).start()
        pltpu.make_async_copy(solv, sol_hbm, out_sem.at[1]).start()

    def crecv_squares():
        return jnp.where(level > 1, crecv[0, pl.ds(512, 8), :] + crecv[1, pl.ds(512, 8), :], 0.0)

    def panel(m):
        sp_copy(m).wait()
        slot = lax.rem(m, 3)
        for i in range(4):
            out = pl.ds(i * 256, 256)
            finished(dot2(spb[slot, out, :], 1, slice(None)), m, i)
        far = (m == 1) & ((level == 2) | (level == 4))

        @pl.when(far)
        def _():
            far_copy().start()

        @pl.when(jnp.logical_not(far))
        def _():
            for k in range(1, 4):
                ring_copy(m, m + level - 2, k).start()

        @pl.when(m + 3 < n_pan)
        def _():
            sp_copy(m + 3).start()

    srhs_copy.wait()
    for k in range(4):
        rhsp[k * 256:(k + 1) * 256, :64] = jnp.transpose(rhsv[:, k * 256:(k + 1) * 256])
    inv_copy.wait()

    start_at = jnp.minimum(2 * (level - 1), 5)

    def phase(p, carry):
        @pl.when(p == 0)
        def _():
            first_sum_2()

        @pl.when((p > 0) & (p < 4))
        def _():
            first_sum(p + 2)

        @pl.when((p > 1) & (p < 6))
        def _():
            second_sum(p, 32)

        @pl.when(p == start_at)
        def _():
            head()

        @pl.when(p == 0)
        def _():
            second_sum(1, 64)
            first_sum(2)

        m = p - start_at

        @pl.when((m > 0) & (m < n_pan))
        def _():
            panel(m)

        u = m + level - 3

        @pl.when((level < 4) & (u < 4) & ((u > 1) | ((level == 1) & (u >= 0))))
        def _():
            ring_sum(u)
        return carry
    lax.fori_loop(0, 8, phase, 0)

    def width_copy(d):
        return pltpu.make_async_remote_copy(
            src_ref=wsend, dst_ref=wrecv, send_sem=w_sem.at[0], recv_sem=w_sem.at[1],
            device_id=(d, grid), device_id_type=MESH)

    @pl.when(level == 6)
    def _():
        wsend[0] = jnp.sqrt(squares[...] / (32 * 3072) + 1e-06)
        for d in range(31):
            width_copy(d).start()
        width_ref[...] = wsend[0]
        pltpu.make_async_copy(abuf.at[pl.ds(0, 248)], abuf.at[pl.ds(0, 248)], w_sem.at[0]).wait()

    @pl.when(level < 6)
    def _():
        width_copy(0).wait_recv()
        width_ref[...] = wrecv[0]

    pltpu.make_async_copy(abuf.at[pl.ds(0, 1016)], abuf.at[pl.ds(0, 1016)], a2a_sem.at[0]).wait()

    @pl.when(yh == 0)
    def _():
        to_sibling(0).wait_send()
        across().wait_send()

    @pl.when(c == 0)
    def _():
        to_sibling(1).wait_send()
    y_out.wait()
    pltpu.make_async_copy(solv, sol_hbm, out_sem.at[1]).wait()
    for t in range(6):
        u_copy(t).wait_send()
    wait_pieces(*piece_1)
    pair_copy().wait_send()
    for k in range(1, 4):
        y_copy(1, k, 64).wait_send()
    wait_pieces(*piece_2)
    for t in range(2, 6):
        for k in range(1, 4):
            rs_copy(t, k).wait_send()
            y_copy(t, k, 32).wait_send()
        wait_pieces(*piece_3(t))

    @pl.when(n_pan > 0)
    def _():
        for i in range(4):
            up_copy(i, 136 if i == 3 else 128).wait_send()

    @pl.when((level == 2) | (level == 4))
    def _():
        far_copy().wait_send()

    def sent(u, carry):
        for k in range(1, 4):
            ring_copy(2 - level + u, u, k).wait_send()
        pltpu.make_async_copy(qsend.at[u], qsend.at[u], q_sem.at[u]).wait()
        return carry
    lax.fori_loop(jnp.where(level == 1, 0, jnp.where(level < 4, 2, 4)), 4, sent, 0)


def write_out(y_in, s_in, w_in, y_out, s_out, w_out):
    y_out[...] = y_in[...]
    s_out[...] = s_in[...]
    w_out[...] = w_in[0, :64]


def local(rhs_rows, order, leaf_inverse, leaf_panels, panel_mask, sep_rhs, sep_inverse, sep_panels):
    vmem = pl.BlockSpec(memory_space=pltpu.VMEM)
    hbm = pl.BlockSpec(memory_space=pl.ANY)
    V = pltpu.VMEM
    leaf_y, solved, width = pl.pallas_call(
        kernel,
        out_shape=(
            jax.ShapeDtypeStruct((512, 256), F32),
            jax.ShapeDtypeStruct((64, 1024), F32),
            jax.ShapeDtypeStruct((8, 128), F32),
        ),
        in_specs=[vmem, pl.BlockSpec(memory_space=pltpu.SMEM), vmem] + [hbm] * 5,
        out_specs=(hbm, hbm, vmem),
        scratch_shapes=[
            V((1024, 128), F32), V((1024, 128), F32),
            V((512, 256), BF16), V((512, 256), BF16),
            V((2048, 512), F32),
            V((3, 512, 256), F32), V((2, 512, 256), F32), V((512, 256), F32),
            V((512, 256), F32), V((512, 256), BF16), V((512, 256), BF16),
            V((3, 1024, 512), F32),
            V((6, 1032, 128), F32), V((6, 1032, 128), F32), V((6, 1032, 128), F32),
            V((4, 3, 256, 128), F32),
            V((2, 520, 128), F32), V((5, 2, 256, 128), F32),
            V((512, 128), F32), V((5, 3, 2, 64, 128), F32),
            V((5, 2, 64, 128), F32), V((4, 512, 128), F32),
            V((2080, 128), F32),
            V((512, 128), F32), V((512, 128), F32), V((8, 128), F32),
            V((1024, 128), F32), V((1024, 128), F32),
            V((64, 1024), F32), V((1024, 128), F32),
            V((2, 1024, 128), BF16), V((2, 1024, 128), BF16),
            V((64, 1024), F32),
            V((1024, 1024), F32), V((3, 1024, 1024), F32),
            V((5, 520, 128), F32), V((2, 520, 128), F32), V((2, 512, 128), F32),
            V((4, 3, 128, 128), F32), V((4, 128, 128), F32), V((2, 2, 128, 128), F32), V((512, 128), F32),
            V((1, 8, 128), F32), V((1, 8, 128), F32),
            DMA((3,)), DMA((3,)), DMA((3,)), DMA((2,)), DMA((3,)), DMA((2,)), DMA, DMA((6,)), DMA((6,)),
            DMA((4, 3)), DMA((4, 3)),
            DMA((2,)), DMA((4, 3)), DMA((4,)), DMA((2, 2)), DMA,
            DMA((2,)), DMA((5, 2)), DMA((2,)), DMA((5, 3)), DMA((5, 3)), DMA((4,)), DMA((4,)), DMA((5, 4)), DMA((2, 4)), DMA((2,)), DMA((2,)),
        ],
        compiler_params=pltpu.CompilerParams(
            collective_id=0, has_side_effects=True, vmem_limit_bytes=62 * 2 ** 20),
        cost_estimate=pl.CostEstimate(flops=7 * 10 ** 9, bytes_accessed=44 * 10 ** 6, transcendentals=0),
    )(order.reshape(4, 128), panel_mask[0].T, rhs_rows, leaf_inverse, leaf_panels[0], sep_rhs[0].T, sep_inverse[0], sep_panels[0])
    leaf_y, solved, width = pl.pallas_call(
        write_out,
        out_shape=(
            jax.ShapeDtypeStruct((512, 256), F32),
            jax.ShapeDtypeStruct((64, 1024), F32),
            jax.ShapeDtypeStruct((64,), F32),
        ),
        in_specs=[vmem] * 3,
        out_specs=(vmem,) * 3,
    )(leaf_y, solved, width)
    return leaf_y, solved.T[None], width


def solution(mesh):
    placed = (
        P(("leaf", "grid"), None),
        P(("leaf", "grid")),
        P("leaf", "grid"),
        P("leaf", None, None, "grid"),
        P("leaf", None, "grid"),
        P("leaf", None, "grid"),
        P("leaf", None, None),
        P("leaf", None, None, None),
    )
    return jax.shard_map(
        local,
        mesh=mesh,
        in_specs=placed,
        out_specs=(P(("leaf", "grid"), None), P("leaf", None, "grid"), P("grid")),
        check_vma=False,
    )
```

```python
import jax
import jax.numpy as jnp
from jax import lax
from jax.experimental import pallas as pl
from jax.experimental.pallas import tpu as pltpu
from jax.sharding import PartitionSpec as P

F32, BF16 = jnp.float32, jnp.bfloat16
MESH = pl.DeviceIdType.MESH
DMA = pltpu.SemaphoreType.DMA


def split(value):
    high = value.astype(BF16)
    return high, (value - high.astype(F32)).astype(BF16)


def dot(a, b):
    return jnp.dot(a, b, preferred_element_type=F32)


def dot3(a, b_high, b_low):
    high, low = split(a)
    return dot(high, b_high) + dot(high, b_low) + dot(low, b_high)


def lane_left(shape):
    return lax.broadcasted_iota(jnp.int32, shape, 1) < 64


def turned(value):
    return pltpu.roll(value, 64, 1)


def packed_pair(top, bottom):
    left = lane_left(top.shape)
    return jnp.where(left, top, turned(bottom)), jnp.where(left, turned(top), bottom)


def unpacked(value):
    left = lane_left(value.shape)
    other = turned(value)
    return jnp.where(left, value, other), jnp.where(left, other, value)


def rows(start, size, unit=8):
    if isinstance(start, int):
        return pl.ds(start, size)
    return pl.ds(pl.multiple_of(start, unit), size)


def kernel(order_ref, mask_ref, rhs_ref, linv_hbm, lpan_hbm, srhs_hbm, sinv_hbm, span_hbm,
           leafy_hbm, sol_hbm, width_ref,
           abuf, xbuf, xh, xl, lbuf, zs, zr, za, ybuf, yh_s, yl_s, pbuf, own, snd, rcv, zrs,
           pk1, yr1, s1, pk, zpair, yrs, s2, grecv, ubuf, accp, pend, squares, cacc, racc, rhsv, rhsp, vcat, vh0, solv, invb, spb, csend, crecv, third, xrs, qsend, qrecv, top, wsend, wrecv,
           ld_sem, lp_sem, sp_sem, a2a_sem, zs_sem, zr_sem, za_sem, us_sem, ur_sem, rs_sem, rr_sem,
           third_sem, xr_sem, q_sem, qr_sem, top_sem, ps_sem, y1_sem, p3_sem, pair_sem, ys_sem, yr_sem, g_sem, u_sem, cs_sem, cr_sem, w_sem, out_sem):
    leaf = lax.axis_index("leaf")
    grid = lax.axis_index("grid")
    me = leaf * 4 + grid
    yl = lax.rem(leaf, 2)
    z = lax.rem(lax.div(leaf, 2), 4)
    x = lax.div(leaf, 8)
    yh = lax.div(grid, 2)
    y = yh * 2 + yl
    c = lax.rem(grid, 2)
    sib = yh * 2 + 1 - c

    level = jnp.int32(1)
    for bit in range(1, 6):
        level = level + (lax.rem(leaf + 1, 2 ** bit) == 0).astype(jnp.int32)
    parent = jnp.int32(0)
    for tier in range(1, 6):
        size = 2 ** (tier + 1)
        parent = jnp.where(level == tier, lax.div(leaf, size) * size + 2 ** tier - 1, parent)
    side = (leaf > parent).astype(jnp.int32)
    above = jnp.int32(0)
    for tier in range(1, 5):
        size = 2 ** (tier + 2)
        above = jnp.where(level == tier, lax.div(leaf, size) * size + 2 ** (tier + 1) - 1, above)
    place = (parent > above).astype(jnp.int32) * 2 + side
    n_pan = 6 - level

    l_copy = pltpu.make_async_copy(linv_hbm, lbuf, ld_sem.at[0])
    l_copy.start()
    inv_copy = pltpu.make_async_copy(sinv_hbm, invb, ld_sem.at[1])
    srhs_copy = pltpu.make_async_copy(srhs_hbm, rhsv, ld_sem.at[2])

    def lp_copy(t):
        return pltpu.make_async_copy(lpan_hbm.at[t], pbuf.at[t % 3], lp_sem.at[t % 3])

    def sp_copy(m):
        slot = lax.rem(m, 3)
        return pltpu.make_async_copy(span_hbm.at[m], spb.at[slot], sp_sem.at[slot])

    rh, rl = split(rhs_ref[...])
    index = order_ref[...].astype(F32)
    index = jnp.transpose(jnp.concatenate([index, index], axis=0)).astype(jnp.int32)
    upper = lax.broadcasted_iota(jnp.int32, (16, 8, 128), 1) < 4
    for part in range(4):
        hot = (lax.broadcasted_iota(jnp.int32, (128, 512), 1) == index[:, part:part + 1]).astype(F32).astype(BF16)
        got = dot(hot, rh) + dot(hot, rl)
        first, second = got[:, :128].reshape(16, 8, 128), got[:, 128:].reshape(16, 8, 128)
        even = jnp.where(upper, first, pltpu.roll(second, 4, 1))
        odd = jnp.where(upper, pltpu.roll(first, 4, 1), second)
        abuf[rows(part * 256, 256), :] = jnp.stack([even, odd], axis=1).reshape(256, 128)

    barrier = pltpu.get_barrier_semaphore()

    def greet(k, carry):
        d = lax.rem(me + k, 128)
        pl.semaphore_signal(barrier, inc=1, device_id=(lax.div(d, 4), lax.rem(d, 4)), device_id_type=MESH)
        return carry

    lax.fori_loop(1, 128, greet, 0)
    for t in range(3):
        lp_copy(t).start()
    srhs_copy.start()
    pl.semaphore_wait(barrier, 127)

    def a2a(k, carry):
        d = lax.rem(me + k, 128)
        pltpu.make_async_remote_copy(
            src_ref=abuf.at[rows(d * 8, 8)], dst_ref=xbuf.at[rows(me * 8, 8)],
            send_sem=a2a_sem.at[0], recv_sem=a2a_sem.at[1],
            device_id=(lax.div(d, 4), lax.rem(d, 4)), device_id_type=MESH).start()
        return carry

    lax.fori_loop(1, 128, a2a, 0)
    xbuf[rows(me * 8, 8), :] = abuf[rows(me * 8, 8), :]
    inv_copy.start()
    for m in range(3):
        @pl.when(m < n_pan)
        def _():
            sp_copy(jnp.int32(m)).start()
    pltpu.make_async_copy(xbuf.at[pl.ds(0, 1016)], xbuf.at[pl.ds(0, 1016)], a2a_sem.at[1]).wait()

    raw = xbuf[...].reshape(64, 2, 8, 128)
    first, second = raw[:, 0], raw[:, 1]
    upper = lax.broadcasted_iota(jnp.int32, (64, 8, 128), 1) < 4
    left = jnp.where(upper, first, pltpu.roll(second, 4, 1)).reshape(512, 128)
    right = jnp.where(upper, pltpu.roll(first, 4, 1), second).reshape(512, 128)
    for half, value in enumerate((left, right)):
        high, low = split(value)
        xh[:, half * 128:(half + 1) * 128] = high
        xl[:, half * 128:(half + 1) * 128] = low

    l_copy.wait()

    def leaf_block(r, dst):
        def body(i, carry):
            dst[rows(i * 256, 256), :] = dot3(lbuf[rows(r * 512 + i * 256, 256), :], xh[...], xl[...])
            return carry
        lax.fori_loop(0, 2, body, 0)

    def to_sibling(slot):
        return pltpu.make_async_remote_copy(
            src_ref=zs.at[slot], dst_ref=zr.at[slot], send_sem=zs_sem.at[slot], recv_sem=zr_sem.at[slot],
            device_id=(leaf, sib), device_id_type=MESH)

    def across():
        return pltpu.make_async_remote_copy(
            src_ref=zs.at[2], dst_ref=za, send_sem=zs_sem.at[2], recv_sem=za_sem,
            device_id=(leaf, 2 + c), device_id_type=MESH)

    @pl.when(yh == 0)
    def _():
        leaf_block(3 - c, zs.at[0])
        to_sibling(0).start()
        leaf_block(2 + c, zs.at[2])
        to_sibling(0).wait_recv()
        zs[2] = zs[2] + zr[0]
        across().start()

        @pl.when(c == 0)
        def _():
            leaf_block(1, zs.at[1])
            to_sibling(1).start()

    @pl.when((yh == 1) & (c == 0))
    def _():
        leaf_block(3, zs.at[1])
        to_sibling(1).start()

    leaf_block(grid, ybuf)

    @pl.when(c == 1)
    def _():
        to_sibling(1).wait_recv()
        ybuf[...] = ybuf[...] + zr[1]

    @pl.when(yh == 1)
    def _():
        across().wait_recv()
        ybuf[...] = ybuf[...] + za[...]

    y_out = pltpu.make_async_copy(ybuf, leafy_hbm, out_sem.at[0])
    y_out.start()

    y_left, y_right = ybuf[:, :128], ybuf[:, 128:]
    for_0, for_1 = packed_pair(y_left, y_right)
    mine = jnp.where(c == 0, for_0, for_1)
    other = jnp.where(c == 0, for_1, for_0)
    own[0, pl.ds(1024, 8), :] = jnp.broadcast_to(jnp.sum(mine * mine, axis=0, keepdims=True), (8, 128))
    snd[0, pl.ds(1024, 8), :] = jnp.broadcast_to(jnp.sum(other * other, axis=0, keepdims=True), (8, 128))
    for half, value in enumerate((mine, other)):
        high, low = split(value)
        yh_s[:, half * 128:(half + 1) * 128] = high
        yl_s[:, half * 128:(half + 1) * 128] = low

    def u_copy(t):
        size = 1032 if t == 0 else 1024
        return pltpu.make_async_remote_copy(
            src_ref=snd.at[t, pl.ds(0, size)], dst_ref=rcv.at[t, pl.ds(0, size)],
            send_sem=us_sem.at[t], recv_sem=ur_sem.at[t], device_id=(leaf, sib), device_id_type=MESH)

    def send_pieces(src, base, size, to_leaf, sems, recv_sem):
        for to_yh in range(2):
            to_me = (to_leaf == leaf) & (yh == to_yh)

            @pl.when(to_me)
            def _():
                ubuf[rows(base, size), :] = src[to_yh]

            @pl.when(jnp.logical_not(to_me))
            def _():
                pltpu.make_async_remote_copy(
                    src_ref=src.at[to_yh], dst_ref=ubuf.at[rows(base, size)],
                    send_sem=sems.at[to_yh], recv_sem=recv_sem,
                    device_id=(to_leaf, to_yh * 2 + c), device_id_type=MESH).start()

    def wait_pieces(src, base, size, to_leaf, sems):
        for to_yh in range(2):
            @pl.when(jnp.logical_not((to_leaf == leaf) & (yh == to_yh)))
            def _():
                pltpu.make_async_copy(src.at[to_yh], src.at[to_yh], sems.at[to_yh]).wait()

    leaf_1 = leaf - yl
    leaf_2 = (x * 4 + z - lax.rem(z, 2)) * 2 + 1
    leaf_3 = x * 8 + 3
    half_z = lax.rem(z, 2)
    piece_1 = (s1, y * 136, 136, leaf_1, ps_sem)
    piece_2 = (s2.at[0], half_z * 256 + y * 64, 64, leaf_2, p3_sem.at[0])

    def piece_3(t):
        return (s2.at[t - 1, :, pl.ds(0, 32)], (t - 2) * 512 + z * 128 + y * 32, 32, leaf_3, p3_sem.at[t - 1])

    def first_copy(k):
        q = lax.rem(y + k, 4)
        return pltpu.make_async_remote_copy(
            src_ref=pk1.at[:, q], dst_ref=yr1.at[3 - k], send_sem=y1_sem.at[0, k - 1], recv_sem=y1_sem.at[1, 3 - k],
            device_id=((x * 4 + z) * 2 + lax.rem(q, 2), lax.div(q, 2) * 2 + c), device_id_type=MESH)

    def pair_copy():
        return pltpu.make_async_remote_copy(
            src_ref=own.at[1, rows((1 - half_z) * 512, 512)], dst_ref=zpair,
            send_sem=pair_sem.at[0], recv_sem=pair_sem.at[1],
            device_id=((x * 4 + z + 1 - 2 * half_z) * 2 + yl, grid), device_id_type=MESH)

    def rs_copy(t, k):
        at = z if t < 4 else x
        q = lax.rem(at + k, 4)
        to_leaf = (x * 4 + q) * 2 + yl if t < 4 else (q * 4 + z) * 2 + yl
        return pltpu.make_async_remote_copy(
            src_ref=own.at[t, rows(q * 256, 256)], dst_ref=zrs.at[t - 2, 3 - k],
            send_sem=rs_sem.at[t - 2, k - 1], recv_sem=rr_sem.at[t - 2, 3 - k],
            device_id=(to_leaf, grid), device_id_type=MESH)

    def y_copy(t, k, size):
        q = lax.rem(y + k, 4)
        return pltpu.make_async_remote_copy(
            src_ref=pk.at[t - 1, :, rows(q * size, size)], dst_ref=yrs.at[t - 1, 3 - k, :, pl.ds(0, size)],
            send_sem=ys_sem.at[t - 1, k - 1], recv_sem=yr_sem.at[t - 1, 3 - k],
            device_id=((x * 4 + z) * 2 + lax.rem(q, 2), lax.div(q, 2) * 2 + c), device_id_type=MESH)

    def spread(t):
        u_copy(t).wait_recv()
        if t == 0:
            def body(i, carry):
                base = i * 256
                top = own[t, rows(base, 128), :] + rcv[t, rows(base, 128), :]
                bottom = own[t, rows(base + 128, 128), :] + rcv[t, rows(base + 128, 128), :]
                p0, p1 = packed_pair(top, bottom)
                pk1[0, i, pl.ds(0, 128), :] = p0
                pk1[1, i, pl.ds(0, 128), :] = p1
                pk1[0, i, pl.ds(128, 8), :] = squares_1
                pk1[1, i, pl.ds(128, 8), :] = turned(squares_1)
                return carry
            squares_1 = own[0, pl.ds(1024, 8), :] + rcv[0, pl.ds(1024, 8), :]
            lax.fori_loop(0, 4, body, 0)
            for k in range(1, 4):
                first_copy(k).start()
        else:
            def body(i, carry):
                part = rows(i * 256, 256)
                own[t, part, :] = own[t, part, :] + rcv[t, part, :]
                return carry
            lax.fori_loop(0, 4, body, 0)
            if t == 1:
                pair_copy().start()
            else:
                for k in range(1, 4):
                    rs_copy(t, k).start()

    for t in range(6):
        lp_copy(t).wait()
        masks = [jnp.full((1, 256), mask_ref[b, t].astype(F32)).astype(BF16) for b in range(4)]
        masked = lambda ref: jnp.concatenate(
            [ref[b * 128:(b + 1) * 128, :] * masks[b] for b in range(4)], axis=0)
        y_high, y_low = masked(yh_s), masked(yl_s)
        xh[...] = y_high
        xl[...] = y_low

        def body(i, carry):
            part = rows(i * 256, 256)
            product = dot3(pbuf[t % 3, part, :], xh[...], xl[...])
            own[t, part, :] = product[:, :128]
            snd[t, part, :] = product[:, 128:]
            return carry
        lax.fori_loop(0, 4, body, 0)
        if t + 3 < 6:
            lp_copy(t + 3).start()
        u_copy(t).start()
        if t > 0:
            spread(t - 1)
    spread(5)
    for k in range(3):
        pltpu.make_async_copy(yr1.at[k], yr1.at[k], y1_sem.at[1, k]).wait()
    for part in range(2):
        s1[part] = pk1[part, y] + yr1[0, part] + (yr1[1, part] + yr1[2, part])
    send_pieces(*piece_1, u_sem.at[0])

    def ring_start(t, size):
        for k in range(1, 4):
            y_copy(t, k, size).start()

    def first_sum_2():
        pair_copy().wait_recv()
        for i in range(2):
            base = half_z * 512 + i * 256
            top = own[1, rows(base, 128), :] + zpair[pl.ds(i * 256, 128), :]
            bottom = own[1, rows(base + 128, 128), :] + zpair[pl.ds(i * 256 + 128, 128), :]
            p0, p1 = packed_pair(top, bottom)
            pk[0, 0, pl.ds(i * 128, 128), :] = p0
            pk[0, 1, pl.ds(i * 128, 128), :] = p1
        ring_start(1, 64)

    def first_sum(t):
        for k in range(3):
            pltpu.make_async_copy(zrs.at[t - 2, k], zrs.at[t - 2, k], rr_sem.at[t - 2, k]).wait()
        base = jnp.where(t < 4, z, x) * 256

        def total(start):
            value = own[t, rows(base + start, 128), :]
            for k in range(3):
                value = value + zrs[t - 2, k, pl.ds(start, 128), :]
            return value
        p0, p1 = packed_pair(total(0), total(128))
        pk[t - 1, 0, pl.ds(0, 128), :] = p0
        pk[t - 1, 1, pl.ds(0, 128), :] = p1
        ring_start(t, 32)

    def second_sum(t, size):
        for k in range(3):
            ref = yrs.at[t - 1, k, :, pl.ds(0, size)]
            pltpu.make_async_copy(ref, ref, yr_sem.at[t - 1, k]).wait()
        value = pk[t - 1, :, rows(y * size, size), :]
        for k in range(3):
            value = value + yrs[t - 1, k, :, pl.ds(0, size), :]
        s2[t - 1, :, pl.ds(0, size), :] = value
        if size == 64:
            send_pieces(*piece_2, u_sem.at[0])
        else:
            send_pieces(*piece_3(t), u_sem.at[t - 2])

    def up_copy(i, size):
        part = rows(i * 128, size)
        return pltpu.make_async_remote_copy(
            src_ref=csend.at[0, part], dst_ref=crecv.at[side, part],
            send_sem=cs_sem.at[0, i], recv_sem=cr_sem.at[side, i], device_id=(parent, grid), device_id_type=MESH)

    def wait_child(s, i, size):
        part = rows(i * 128, size)
        pltpu.make_async_copy(csend.at[0, part], crecv.at[s, part], cr_sem.at[s, i]).wait()

    def far_copy():
        return pltpu.make_async_remote_copy(
            src_ref=csend.at[1, pl.ds(0, 512)], dst_ref=grecv.at[place],
            send_sem=cs_sem.at[1, 0], recv_sem=g_sem.at[place], device_id=(above, grid), device_id_type=MESH)

    def ring_copy(m, u, k):
        over_z = u < 2
        q = lax.rem(jnp.where(over_z, z, x) + k, 4)
        return pltpu.make_async_remote_copy(
            src_ref=csend.at[m, rows(q * 128, 128)], dst_ref=xrs.at[u, 3 - k],
            send_sem=cs_sem.at[m, k], recv_sem=xr_sem.at[u, 3 - k],
            device_id=((jnp.where(over_z, x, q) * 4 + jnp.where(over_z, q, z)) * 2 + yl, grid), device_id_type=MESH)

    def side_copy(u):
        return pltpu.make_async_remote_copy(
            src_ref=qsend.at[u], dst_ref=third.at[u, rows(z * 128, 128)],
            send_sem=q_sem.at[u], recv_sem=third_sem.at[u], device_id=(leaf_3, grid), device_id_type=MESH)

    def quarter_copy(u):
        return pltpu.make_async_remote_copy(
            src_ref=qsend.at[u], dst_ref=qrecv.at[u - 2, side],
            send_sem=q_sem.at[u], recv_sem=qr_sem.at[u - 2, side], device_id=(parent, grid), device_id_type=MESH)

    def top_copy(u):
        return pltpu.make_async_remote_copy(
            src_ref=qsend.at[u], dst_ref=top.at[rows(x * 128, 128)],
            send_sem=q_sem.at[u], recv_sem=top_sem, device_id=(16 * u - 17, grid), device_id_type=MESH)

    def ring_sum(u):
        for k in range(3):
            pltpu.make_async_copy(xrs.at[u, k], xrs.at[u, k], xr_sem.at[u, k]).wait()
        m = 2 - level + u
        base = jnp.where(u < 2, z, x) * 128
        qsend[u] = csend[m, rows(base, 128), :] + xrs[u, 0] + (xrs[u, 1] + xrs[u, 2])

        @pl.when(u < 2)
        def _():
            side_copy(u).start()

        @pl.when(level > 1)
        def _():
            for s in range(2):
                pltpu.make_async_copy(qrecv.at[u - 2, s], qrecv.at[u - 2, s], qr_sem.at[u - 2, s]).wait()
            qsend[u] = qsend[u] + (qrecv[u - 2, 0] + qrecv[u - 2, 1])

        @pl.when((u > 1) & (level < 3))
        def _():
            quarter_copy(u).start()

        @pl.when(level == 3)
        def _():
            pltpu.make_async_copy(ubuf.at[pl.ds(0, 480)], ubuf.at[pl.ds(0, 480)], u_sem.at[u]).wait()
            start = u * 512
            value = qsend[u]
            for s in range(4):
                value = value + ubuf[rows(start + s * 128, 128), :]
            qsend[u] = value
            top_copy(u).start()

    def take_3(k, dst):
        pltpu.make_async_copy(ubuf.at[pl.ds(0, 480)], ubuf.at[pl.ds(0, 480)], u_sem.at[k]).wait()
        pltpu.make_async_copy(third.at[k], third.at[k], third_sem.at[k]).wait()
        dst[...] = ubuf[k * 512:(k + 1) * 512, :] + third[k]

    def take_far(slot):
        pltpu.make_async_copy(grecv.at[slot], grecv.at[slot], g_sem.at[slot]).wait()
        accp[...] = accp[...] + grecv[slot]

    def dot2(a, which, part):
        high, low = split(a)
        return dot(high, vcat[which, part, :]) + dot(low, vh0[which, part, :])

    def stacked(value, which, part):
        left = lane_left(value.shape)
        high, low = split(value)
        vcat[which, part, :] = jnp.where(left, high.astype(F32), low.astype(F32)).astype(BF16)
        vh0[which, part, :] = jnp.where(left, high.astype(F32), 0.0).astype(BF16)

    def finished(product, m, i):
        total = product + turned(product)
        part = rows(i * 128, 128)
        csend[m, part, :] = jnp.where(lane_left((128, 128)), total[:128], total[128:])

    def head():
        squares[...] = jnp.zeros_like(squares)

        @pl.when(level == 1)
        def _():
            pltpu.make_async_copy(ubuf.at[pl.ds(0, 408)], ubuf.at[pl.ds(0, 408)], u_sem.at[0]).wait()
            for q in range(4):
                accp[q * 128:(q + 1) * 128, :] = ubuf[q * 136:q * 136 + 128, :]
            squares[...] = ubuf[128:136, :]

        @pl.when(level == 2)
        def _():
            pltpu.make_async_copy(ubuf.at[pl.ds(0, 448)], ubuf.at[pl.ds(0, 448)], u_sem.at[0]).wait()
            accp[...] = ubuf[0:512, :]

        @pl.when(level == 3)
        def _():
            take_3(0, accp)

        @pl.when(level > 3)
        def _():
            accp[...] = jnp.zeros_like(accp)

        @pl.when((level == 4) | (level == 6))
        def _():
            take_far(0)
            take_far(1)

        @pl.when(level == 4)
        def _():
            take_far(2)
            take_far(3)

        @pl.when(level > 4)
        def _():
            pltpu.make_async_copy(top, top, top_sem).wait()
            accp[...] = accp[...] + top[...]

        @pl.when(n_pan > 0)
        def _():
            sp_copy(jnp.int32(0)).wait()

        for k in range(4):
            packed = pl.ds(k * 128, 128)
            size = 136 if k == 3 else 128

            @pl.when(level > 1)
            def _():
                wait_child(0, k, size)
                accp[packed, :] = accp[packed, :] + crecv[0, packed, :]

            @pl.when((level > 1) & (level < 6))
            def _():
                wait_child(1, k, size)
                accp[packed, :] = accp[packed, :] + crecv[1, packed, :]

            left = lane_left((128, 128))
            for j, value in enumerate(unpacked(accp[packed, :])):
                part = pl.ds(k * 256 + j * 128, 128)
                right_side = rhsp[part, :]
                stacked(jnp.where(left, right_side, turned(right_side)) - value, 0, part)
            part = pl.ds(k * 256, 256)
            product = dot2(invb[part, k * 256:(k + 1) * 256], 0, part)
            if k > 0:
                product = product + racc[part, :]
            s_value = product + turned(product)
            stacked(s_value, 1, part)

            @pl.when(n_pan > 0)
            def _():
                if k < 3:
                    product = dot2(spb[0, :, k * 256:(k + 1) * 256], 1, part)
                    cacc[...] = product if k == 0 else cacc[...] + product
                else:
                    squares[...] = squares[...] + jnp.sum(s_value * s_value, axis=0, keepdims=True)
                    squares[...] = squares[...] + crecv_squares()
                    csend[0, pl.ds(512, 8), :] = squares[...]

                    @pl.when(level == 3)
                    def _():
                        take_3(1, pend)
                    for i in range(4):
                        out = pl.ds(i * 256, 256)
                        finished(cacc[out, :] + dot2(spb[0, out, k * 256:(k + 1) * 256], 1, part), 0, i)

                        @pl.when(level == 3)
                        def _():
                            up = pl.ds(i * 128, 128)
                            csend[0, up, :] = csend[0, up, :] + pend[up, :]
                        up_copy(i, 136 if i == 3 else 128).start()
            solv[:, k * 256:(k + 1) * 256] = jnp.transpose(s_value)[:64]
            if k < 3:
                squares[...] = squares[...] + jnp.sum(s_value * s_value, axis=0, keepdims=True)
                rest = slice((k + 1) * 256, 1024)
                product = dot2(invb[rest, k * 256:(k + 1) * 256], 0, part)
                racc[rest, :] = product if k == 0 else racc[rest, :] + product
            else:
                @pl.when(level == 6)
                def _():
                    squares[...] = squares[...] + jnp.sum(s_value * s_value, axis=0, keepdims=True) + crecv[0, pl.ds(512, 8), :]

        @pl.when(3 < n_pan)
        def _():
            sp_copy(jnp.int32(3)).start()
        pltpu.make_async_copy(solv, sol_hbm, out_sem.at[1]).start()

    def crecv_squares():
        return jnp.where(level > 1, crecv[0, pl.ds(512, 8), :] + crecv[1, pl.ds(512, 8), :], 0.0)

    def panel(m):
        sp_copy(m).wait()
        slot = lax.rem(m, 3)
        for i in range(4):
            out = pl.ds(i * 256, 256)
            finished(dot2(spb[slot, out, :], 1, slice(None)), m, i)
        far = (m == 1) & ((level == 2) | (level == 4))

        @pl.when(far)
        def _():
            far_copy().start()

        @pl.when(jnp.logical_not(far))
        def _():
            for k in range(1, 4):
                ring_copy(m, m + level - 2, k).start()

        @pl.when(m + 3 < n_pan)
        def _():
            sp_copy(m + 3).start()

    srhs_copy.wait()
    for k in range(4):
        rhsp[k * 256:(k + 1) * 256, :64] = jnp.transpose(rhsv[:, k * 256:(k + 1) * 256])
    inv_copy.wait()

    start_at = jnp.minimum(2 * (level - 1), 5)

    def phase(p, carry):
        @pl.when(p == 0)
        def _():
            first_sum_2()

        @pl.when(p < 4)
        def _():
            first_sum(p + 2)

        @pl.when(p == 1)
        def _():
            second_sum(1, 64)

        @pl.when((p > 1) & (p < 6))
        def _():
            second_sum(p, 32)

        @pl.when(p == start_at)
        def _():
            head()

        m = p - start_at

        @pl.when((m > 0) & (m < n_pan))
        def _():
            panel(m)

        u = m + level - 3

        @pl.when((level < 4) & (u < 4) & ((u > 1) | ((level == 1) & (u >= 0))))
        def _():
            ring_sum(u)
        return carry
    lax.fori_loop(0, 8, phase, 0)

    def width_copy(d):
        return pltpu.make_async_remote_copy(
            src_ref=wsend, dst_ref=wrecv, send_sem=w_sem.at[0], recv_sem=w_sem.at[1],
            device_id=(d, grid), device_id_type=MESH)

    @pl.when(level == 6)
    def _():
        wsend[0] = jnp.sqrt(squares[...] / (32 * 3072) + 1e-06)
        for d in range(31):
            width_copy(d).start()
        width_ref[...] = wsend[0]
        pltpu.make_async_copy(abuf.at[pl.ds(0, 248)], abuf.at[pl.ds(0, 248)], w_sem.at[0]).wait()

    @pl.when(level < 6)
    def _():
        width_copy(0).wait_recv()
        width_ref[...] = wrecv[0]

    pltpu.make_async_copy(abuf.at[pl.ds(0, 1016)], abuf.at[pl.ds(0, 1016)], a2a_sem.at[0]).wait()

    @pl.when(yh == 0)
    def _():
        to_sibling(0).wait_send()
        across().wait_send()

    @pl.when(c == 0)
    def _():
        to_sibling(1).wait_send()
    y_out.wait()
    pltpu.make_async_copy(solv, sol_hbm, out_sem.at[1]).wait()
    for t in range(6):
        u_copy(t).wait_send()
    for k in range(1, 4):
        first_copy(k).wait_send()
    wait_pieces(*piece_1)
    pair_copy().wait_send()
    for k in range(1, 4):
        y_copy(1, k, 64).wait_send()
    wait_pieces(*piece_2)
    for t in range(2, 6):
        for k in range(1, 4):
            rs_copy(t, k).wait_send()
            y_copy(t, k, 32).wait_send()
        wait_pieces(*piece_3(t))

    @pl.when(n_pan > 0)
    def _():
        for i in range(4):
            up_copy(i, 136 if i == 3 else 128).wait_send()

    @pl.when((level == 2) | (level == 4))
    def _():
        far_copy().wait_send()

    def sent(u, carry):
        for k in range(1, 4):
            ring_copy(2 - level + u, u, k).wait_send()
        pltpu.make_async_copy(qsend.at[u], qsend.at[u], q_sem.at[u]).wait()
        return carry
    lax.fori_loop(jnp.where(level == 1, 0, jnp.where(level < 4, 2, 4)), 4, sent, 0)


def write_out(y_in, s_in, w_in, y_out, s_out, w_out):
    y_out[...] = y_in[...]
    s_out[...] = s_in[...]
    w_out[...] = w_in[0, :64]


def local(rhs_rows, order, leaf_inverse, leaf_panels, panel_mask, sep_rhs, sep_inverse, sep_panels):
    vmem = pl.BlockSpec(memory_space=pltpu.VMEM)
    hbm = pl.BlockSpec(memory_space=pl.ANY)
    V = pltpu.VMEM
    leaf_y, solved, width = pl.pallas_call(
        kernel,
        out_shape=(
            jax.ShapeDtypeStruct((512, 256), F32),
            jax.ShapeDtypeStruct((64, 1024), F32),
            jax.ShapeDtypeStruct((8, 128), F32),
        ),
        in_specs=[vmem, pl.BlockSpec(memory_space=pltpu.SMEM), vmem] + [hbm] * 5,
        out_specs=(hbm, hbm, vmem),
        scratch_shapes=[
            V((1024, 128), F32), V((1024, 128), F32),
            V((512, 256), BF16), V((512, 256), BF16),
            V((2048, 512), F32),
            V((3, 512, 256), F32), V((2, 512, 256), F32), V((512, 256), F32),
            V((512, 256), F32), V((512, 256), BF16), V((512, 256), BF16),
            V((3, 1024, 512), F32),
            V((6, 1032, 128), F32), V((6, 1032, 128), F32), V((6, 1032, 128), F32),
            V((4, 3, 256, 128), F32),
            V((2, 4, 136, 128), F32), V((3, 2, 136, 128), F32), V((2, 136, 128), F32),
            V((5, 2, 256, 128), F32),
            V((512, 128), F32), V((5, 3, 2, 64, 128), F32),
            V((5, 2, 64, 128), F32), V((4, 512, 128), F32),
            V((2080, 128), F32),
            V((512, 128), F32), V((512, 128), F32), V((8, 128), F32),
            V((1024, 128), F32), V((1024, 128), F32),
            V((64, 1024), F32), V((1024, 128), F32),
            V((2, 1024, 128), BF16), V((2, 1024, 128), BF16),
            V((64, 1024), F32),
            V((1024, 1024), F32), V((3, 1024, 1024), F32),
            V((5, 520, 128), F32), V((2, 520, 128), F32), V((2, 512, 128), F32),
            V((4, 3, 128, 128), F32), V((4, 128, 128), F32), V((2, 2, 128, 128), F32), V((512, 128), F32),
            V((1, 8, 128), F32), V((1, 8, 128), F32),
            DMA((3,)), DMA((3,)), DMA((3,)), DMA((2,)), DMA((3,)), DMA((2,)), DMA, DMA((6,)), DMA((6,)),
            DMA((4, 3)), DMA((4, 3)),
            DMA((2,)), DMA((4, 3)), DMA((4,)), DMA((2, 2)), DMA,
            DMA((2,)), DMA((2, 3)), DMA((5, 2)), DMA((2,)), DMA((5, 3)), DMA((5, 3)), DMA((4,)), DMA((4,)), DMA((5, 4)), DMA((2, 4)), DMA((2,)), DMA((2,)),
        ],
        compiler_params=pltpu.CompilerParams(
            collective_id=0, has_side_effects=True, vmem_limit_bytes=62 * 2 ** 20),
        cost_estimate=pl.CostEstimate(flops=7 * 10 ** 9, bytes_accessed=44 * 10 ** 6, transcendentals=0),
    )(order.reshape(4, 128), panel_mask[0].T, rhs_rows, leaf_inverse, leaf_panels[0], sep_rhs[0].T, sep_inverse[0], sep_panels[0])
    leaf_y, solved, width = pl.pallas_call(
        write_out,
        out_shape=(
            jax.ShapeDtypeStruct((512, 256), F32),
            jax.ShapeDtypeStruct((64, 1024), F32),
            jax.ShapeDtypeStruct((64,), F32),
        ),
        in_specs=[vmem] * 3,
        out_specs=(vmem,) * 3,
    )(leaf_y, solved, width)
    return leaf_y, solved.T[None], width


def solution(mesh):
    placed = (
        P(("leaf", "grid"), None),
        P(("leaf", "grid")),
        P("leaf", "grid"),
        P("leaf", None, None, "grid"),
        P("leaf", None, "grid"),
        P("leaf", None, "grid"),
        P("leaf", None, None),
        P("leaf", None, None, None),
    )
    return jax.shard_map(
        local,
        mesh=mesh,
        in_specs=placed,
        out_specs=(P(("leaf", "grid"), None), P("leaf", None, "grid"), P("grid")),
        check_vma=False,
    )
```

```python
import jax
import jax.numpy as jnp
from jax import lax
from jax.experimental import pallas as pl
from jax.experimental.pallas import tpu as pltpu
from jax.sharding import PartitionSpec as P

F32, BF16 = jnp.float32, jnp.bfloat16
MESH = pl.DeviceIdType.MESH
DMA = pltpu.SemaphoreType.DMA


def split(value):
    high = value.astype(BF16)
    return high, (value - high.astype(F32)).astype(BF16)


def dot(a, b):
    return jnp.dot(a, b, preferred_element_type=F32)


def dot3(a, b_high, b_low):
    high, low = split(a)
    return dot(high, b_high) + dot(high, b_low) + dot(low, b_high)


def lane_left(shape):
    return lax.broadcasted_iota(jnp.int32, shape, 1) < 64


def turned(value):
    return pltpu.roll(value, 64, 1)


def packed_pair(top, bottom):
    left = lane_left(top.shape)
    return jnp.where(left, top, turned(bottom)), jnp.where(left, turned(top), bottom)


def unpacked(value):
    left = lane_left(value.shape)
    other = turned(value)
    return jnp.where(left, value, other), jnp.where(left, other, value)


def rows(start, size, unit=8):
    if isinstance(start, int):
        return pl.ds(start, size)
    return pl.ds(pl.multiple_of(start, unit), size)


def kernel(order_ref, mask_ref, rhs_ref, linv_hbm, lpan_hbm, srhs_hbm, sinv_hbm, span_hbm,
           leafy_hbm, sol_hbm, width_ref,
           abuf, xbuf, xh, xl, lbuf, zs, zr, za, ybuf, yh_s, yl_s, pbuf, own, snd, rcv, zrs,
           pk1, yr1, s1, pk, zpair, yrs, s2, grecv, ubuf, accp, pend, squares, cacc, racc, rhsv, rhsp, vcat, vh0, solv, invb, spb, csend, crecv, third, xrs, qsend, qrecv, top, wsend, wrecv,
           ld_sem, lp_sem, sp_sem, a2a_sem, zs_sem, zr_sem, za_sem, us_sem, ur_sem, rs_sem, rr_sem,
           third_sem, xr_sem, q_sem, qr_sem, top_sem, ps_sem, y1_sem, p3_sem, pair_sem, ys_sem, yr_sem, g_sem, u_sem, cs_sem, cr_sem, w_sem, out_sem):
    leaf = lax.axis_index("leaf")
    grid = lax.axis_index("grid")
    me = leaf * 4 + grid
    yl = lax.rem(leaf, 2)
    z = lax.rem(lax.div(leaf, 2), 4)
    x = lax.div(leaf, 8)
    yh = lax.div(grid, 2)
    y = yh * 2 + yl
    c = lax.rem(grid, 2)
    sib = yh * 2 + 1 - c

    level = jnp.int32(1)
    for bit in range(1, 6):
        level = level + (lax.rem(leaf + 1, 2 ** bit) == 0).astype(jnp.int32)
    parent = jnp.int32(0)
    for tier in range(1, 6):
        size = 2 ** (tier + 1)
        parent = jnp.where(level == tier, lax.div(leaf, size) * size + 2 ** tier - 1, parent)
    side = (leaf > parent).astype(jnp.int32)
    above = jnp.int32(0)
    for tier in range(1, 5):
        size = 2 ** (tier + 2)
        above = jnp.where(level == tier, lax.div(leaf, size) * size + 2 ** (tier + 1) - 1, above)
    place = (parent > above).astype(jnp.int32) * 2 + side
    n_pan = 6 - level

    l_copy = pltpu.make_async_copy(linv_hbm, lbuf, ld_sem.at[0])
    l_copy.start()
    inv_copy = pltpu.make_async_copy(sinv_hbm, invb, ld_sem.at[1])
    srhs_copy = pltpu.make_async_copy(srhs_hbm, rhsv, ld_sem.at[2])

    def lp_copy(t):
        return pltpu.make_async_copy(lpan_hbm.at[t], pbuf.at[t % 3], lp_sem.at[t % 3])

    def sp_copy(m):
        slot = lax.rem(m, 3)
        return pltpu.make_async_copy(span_hbm.at[m], spb.at[slot], sp_sem.at[slot])

    rh, rl = split(rhs_ref[...])
    index = order_ref[...].astype(F32)
    index = jnp.transpose(jnp.concatenate([index, index], axis=0)).astype(jnp.int32)
    upper = lax.broadcasted_iota(jnp.int32, (16, 8, 128), 1) < 4
    for part in range(4):
        hot = (lax.broadcasted_iota(jnp.int32, (128, 512), 1) == index[:, part:part + 1]).astype(F32).astype(BF16)
        got = dot(hot, rh) + dot(hot, rl)
        first, second = got[:, :128].reshape(16, 8, 128), got[:, 128:].reshape(16, 8, 128)
        even = jnp.where(upper, first, pltpu.roll(second, 4, 1))
        odd = jnp.where(upper, pltpu.roll(first, 4, 1), second)
        abuf[rows(part * 256, 256), :] = jnp.stack([even, odd], axis=1).reshape(256, 128)

    barrier = pltpu.get_barrier_semaphore()

    def greet(k, carry):
        d = lax.rem(me + k, 128)
        pl.semaphore_signal(barrier, inc=1, device_id=(lax.div(d, 4), lax.rem(d, 4)), device_id_type=MESH)
        return carry

    lax.fori_loop(1, 128, greet, 0)
    for t in range(3):
        lp_copy(t).start()
    srhs_copy.start()
    pl.semaphore_wait(barrier, 127)

    def a2a(k, carry):
        d = lax.rem(me + k, 128)
        pltpu.make_async_remote_copy(
            src_ref=abuf.at[rows(d * 8, 8)], dst_ref=xbuf.at[rows(me * 8, 8)],
            send_sem=a2a_sem.at[0], recv_sem=a2a_sem.at[1],
            device_id=(lax.div(d, 4), lax.rem(d, 4)), device_id_type=MESH).start()
        return carry

    lax.fori_loop(1, 128, a2a, 0)
    xbuf[rows(me * 8, 8), :] = abuf[rows(me * 8, 8), :]
    inv_copy.start()
    for m in range(3):
        @pl.when(m < n_pan)
        def _():
            sp_copy(jnp.int32(m)).start()
    pltpu.make_async_copy(xbuf.at[pl.ds(0, 1016)], xbuf.at[pl.ds(0, 1016)], a2a_sem.at[1]).wait()

    raw = xbuf[...].reshape(64, 2, 8, 128)
    first, second = raw[:, 0], raw[:, 1]
    upper = lax.broadcasted_iota(jnp.int32, (64, 8, 128), 1) < 4
    left = jnp.where(upper, first, pltpu.roll(second, 4, 1)).reshape(512, 128)
    right = jnp.where(upper, pltpu.roll(first, 4, 1), second).reshape(512, 128)
    for half, value in enumerate((left, right)):
        high, low = split(value)
        xh[:, half * 128:(half + 1) * 128] = high
        xl[:, half * 128:(half + 1) * 128] = low

    l_copy.wait()

    def leaf_block(r, dst):
        def body(i, carry):
            dst[rows(i * 256, 256), :] = dot3(lbuf[rows(r * 512 + i * 256, 256), :], xh[...], xl[...])
            return carry
        lax.fori_loop(0, 2, body, 0)

    def to_sibling(slot):
        return pltpu.make_async_remote_copy(
            src_ref=zs.at[slot], dst_ref=zr.at[slot], send_sem=zs_sem.at[slot], recv_sem=zr_sem.at[slot],
            device_id=(leaf, sib), device_id_type=MESH)

    def across():
        return pltpu.make_async_remote_copy(
            src_ref=zs.at[2], dst_ref=za, send_sem=zs_sem.at[2], recv_sem=za_sem,
            device_id=(leaf, 2 + c), device_id_type=MESH)

    @pl.when(yh == 0)
    def _():
        leaf_block(3 - c, zs.at[0])
        to_sibling(0).start()
        leaf_block(2 + c, zs.at[2])
        to_sibling(0).wait_recv()
        zs[2] = zs[2] + zr[0]
        across().start()

        @pl.when(c == 0)
        def _():
            leaf_block(1, zs.at[1])
            to_sibling(1).start()

    @pl.when((yh == 1) & (c == 0))
    def _():
        leaf_block(3, zs.at[1])
        to_sibling(1).start()

    leaf_block(grid, ybuf)

    @pl.when(c == 1)
    def _():
        to_sibling(1).wait_recv()
        ybuf[...] = ybuf[...] + zr[1]

    @pl.when(yh == 1)
    def _():
        across().wait_recv()
        ybuf[...] = ybuf[...] + za[...]

    y_out = pltpu.make_async_copy(ybuf, leafy_hbm, out_sem.at[0])
    y_out.start()

    y_left, y_right = ybuf[:, :128], ybuf[:, 128:]
    for_0, for_1 = packed_pair(y_left, y_right)
    mine = jnp.where(c == 0, for_0, for_1)
    other = jnp.where(c == 0, for_1, for_0)
    own[0, pl.ds(1024, 8), :] = jnp.broadcast_to(jnp.sum(mine * mine, axis=0, keepdims=True), (8, 128))
    snd[0, pl.ds(1024, 8), :] = jnp.broadcast_to(jnp.sum(other * other, axis=0, keepdims=True), (8, 128))
    for half, value in enumerate((mine, other)):
        high, low = split(value)
        yh_s[:, half * 128:(half + 1) * 128] = high
        yl_s[:, half * 128:(half + 1) * 128] = low

    def u_copy(t):
        size = 1032 if t == 0 else 1024
        return pltpu.make_async_remote_copy(
            src_ref=snd.at[t, pl.ds(0, size)], dst_ref=rcv.at[t, pl.ds(0, size)],
            send_sem=us_sem.at[t], recv_sem=ur_sem.at[t], device_id=(leaf, sib), device_id_type=MESH)

    def send_pieces(src, base, size, to_leaf, sems, recv_sem):
        for to_yh in range(2):
            to_me = (to_leaf == leaf) & (yh == to_yh)

            @pl.when(to_me)
            def _():
                ubuf[rows(base, size), :] = src[to_yh]

            @pl.when(jnp.logical_not(to_me))
            def _():
                pltpu.make_async_remote_copy(
                    src_ref=src.at[to_yh], dst_ref=ubuf.at[rows(base, size)],
                    send_sem=sems.at[to_yh], recv_sem=recv_sem,
                    device_id=(to_leaf, to_yh * 2 + c), device_id_type=MESH).start()

    def wait_pieces(src, base, size, to_leaf, sems):
        for to_yh in range(2):
            @pl.when(jnp.logical_not((to_leaf == leaf) & (yh == to_yh)))
            def _():
                pltpu.make_async_copy(src.at[to_yh], src.at[to_yh], sems.at[to_yh]).wait()

    leaf_1 = leaf - yl
    leaf_2 = (x * 4 + z - lax.rem(z, 2)) * 2 + 1
    leaf_3 = x * 8 + 3
    half_z = lax.rem(z, 2)
    piece_1 = (s1, y * 136, 136, leaf_1, ps_sem)
    piece_2 = (s2.at[0], half_z * 256 + y * 64, 64, leaf_2, p3_sem.at[0])

    def piece_3(t):
        return (s2.at[t - 1, :, pl.ds(0, 32)], (t - 2) * 512 + z * 128 + y * 32, 32, leaf_3, p3_sem.at[t - 1])

    def first_copy(k):
        q = lax.rem(y + k, 4)
        return pltpu.make_async_remote_copy(
            src_ref=pk1.at[:, q], dst_ref=yr1.at[3 - k], send_sem=y1_sem.at[0, k - 1], recv_sem=y1_sem.at[1, 3 - k],
            device_id=((x * 4 + z) * 2 + lax.rem(q, 2), lax.div(q, 2) * 2 + c), device_id_type=MESH)

    def pair_copy():
        return pltpu.make_async_remote_copy(
            src_ref=own.at[1, rows((1 - half_z) * 512, 512)], dst_ref=zpair,
            send_sem=pair_sem.at[0], recv_sem=pair_sem.at[1],
            device_id=((x * 4 + z + 1 - 2 * half_z) * 2 + yl, grid), device_id_type=MESH)

    def rs_copy(t, k):
        at = z if t < 4 else x
        q = lax.rem(at + k, 4)
        to_leaf = (x * 4 + q) * 2 + yl if t < 4 else (q * 4 + z) * 2 + yl
        return pltpu.make_async_remote_copy(
            src_ref=own.at[t, rows(q * 256, 256)], dst_ref=zrs.at[t - 2, 3 - k],
            send_sem=rs_sem.at[t - 2, k - 1], recv_sem=rr_sem.at[t - 2, 3 - k],
            device_id=(to_leaf, grid), device_id_type=MESH)

    def y_copy(t, k, size):
        q = lax.rem(y + k, 4)
        return pltpu.make_async_remote_copy(
            src_ref=pk.at[t - 1, :, rows(q * size, size)], dst_ref=yrs.at[t - 1, 3 - k, :, pl.ds(0, size)],
            send_sem=ys_sem.at[t - 1, k - 1], recv_sem=yr_sem.at[t - 1, 3 - k],
            device_id=((x * 4 + z) * 2 + lax.rem(q, 2), lax.div(q, 2) * 2 + c), device_id_type=MESH)

    def spread(t):
        u_copy(t).wait_recv()
        if t == 0:
            def body(i, carry):
                base = i * 256
                top = own[t, rows(base, 128), :] + rcv[t, rows(base, 128), :]
                bottom = own[t, rows(base + 128, 128), :] + rcv[t, rows(base + 128, 128), :]
                p0, p1 = packed_pair(top, bottom)
                pk1[0, i, pl.ds(0, 128), :] = p0
                pk1[1, i, pl.ds(0, 128), :] = p1
                pk1[0, i, pl.ds(128, 8), :] = squares_1
                pk1[1, i, pl.ds(128, 8), :] = turned(squares_1)
                return carry
            squares_1 = own[0, pl.ds(1024, 8), :] + rcv[0, pl.ds(1024, 8), :]
            lax.fori_loop(0, 4, body, 0)
            for k in range(1, 4):
                first_copy(k).start()
        else:
            def body(i, carry):
                part = rows(i * 256, 256)
                own[t, part, :] = own[t, part, :] + rcv[t, part, :]
                return carry
            lax.fori_loop(0, 4, body, 0)
            if t == 1:
                pair_copy().start()
            else:
                for k in range(1, 4):
                    rs_copy(t, k).start()

    def first_pieces():
        for k in range(3):
            pltpu.make_async_copy(yr1.at[k], yr1.at[k], y1_sem.at[1, k]).wait()
        for part in range(2):
            s1[part] = pk1[part, y] + yr1[0, part] + (yr1[1, part] + yr1[2, part])
        send_pieces(*piece_1, u_sem.at[0])

    for t in range(6):
        if t == 5:
            first_pieces()
        lp_copy(t).wait()
        masks = [jnp.full((1, 256), mask_ref[b, t].astype(F32)).astype(BF16) for b in range(4)]
        masked = lambda ref: jnp.concatenate(
            [ref[b * 128:(b + 1) * 128, :] * masks[b] for b in range(4)], axis=0)
        y_high, y_low = masked(yh_s), masked(yl_s)
        xh[...] = y_high
        xl[...] = y_low

        def body(i, carry):
            part = rows(i * 256, 256)
            product = dot3(pbuf[t % 3, part, :], xh[...], xl[...])
            own[t, part, :] = product[:, :128]
            snd[t, part, :] = product[:, 128:]
            return carry
        lax.fori_loop(0, 4, body, 0)
        if t + 3 < 6:
            lp_copy(t + 3).start()
        u_copy(t).start()
        if t > 0:
            spread(t - 1)
    spread(5)

    def ring_start(t, size):
        for k in range(1, 4):
            y_copy(t, k, size).start()

    def first_sum_2():
        pair_copy().wait_recv()
        for i in range(2):
            base = half_z * 512 + i * 256
            top = own[1, rows(base, 128), :] + zpair[pl.ds(i * 256, 128), :]
            bottom = own[1, rows(base + 128, 128), :] + zpair[pl.ds(i * 256 + 128, 128), :]
            p0, p1 = packed_pair(top, bottom)
            pk[0, 0, pl.ds(i * 128, 128), :] = p0
            pk[0, 1, pl.ds(i * 128, 128), :] = p1
        ring_start(1, 64)

    def first_sum(t):
        for k in range(3):
            pltpu.make_async_copy(zrs.at[t - 2, k], zrs.at[t - 2, k], rr_sem.at[t - 2, k]).wait()
        base = jnp.where(t < 4, z, x) * 256

        def total(start):
            value = own[t, rows(base + start, 128), :]
            for k in range(3):
                value = value + zrs[t - 2, k, pl.ds(start, 128), :]
            return value
        p0, p1 = packed_pair(total(0), total(128))
        pk[t - 1, 0, pl.ds(0, 128), :] = p0
        pk[t - 1, 1, pl.ds(0, 128), :] = p1
        ring_start(t, 32)

    def second_sum(t, size):
        for k in range(3):
            ref = yrs.at[t - 1, k, :, pl.ds(0, size)]
            pltpu.make_async_copy(ref, ref, yr_sem.at[t - 1, k]).wait()
        value = pk[t - 1, :, rows(y * size, size), :]
        for k in range(3):
            value = value + yrs[t - 1, k, :, pl.ds(0, size), :]
        s2[t - 1, :, pl.ds(0, size), :] = value
        if size == 64:
            send_pieces(*piece_2, u_sem.at[0])
        else:
            send_pieces(*piece_3(t), u_sem.at[t - 2])

    def up_copy(i, size):
        part = rows(i * 128, size)
        return pltpu.make_async_remote_copy(
            src_ref=csend.at[0, part], dst_ref=crecv.at[side, part],
            send_sem=cs_sem.at[0, i], recv_sem=cr_sem.at[side, i], device_id=(parent, grid), device_id_type=MESH)

    def wait_child(s, i, size):
        part = rows(i * 128, size)
        pltpu.make_async_copy(csend.at[0, part], crecv.at[s, part], cr_sem.at[s, i]).wait()

    def far_copy():
        return pltpu.make_async_remote_copy(
            src_ref=csend.at[1, pl.ds(0, 512)], dst_ref=grecv.at[place],
            send_sem=cs_sem.at[1, 0], recv_sem=g_sem.at[place], device_id=(above, grid), device_id_type=MESH)

    def ring_copy(m, u, k):
        over_z = u < 2
        q = lax.rem(jnp.where(over_z, z, x) + k, 4)
        return pltpu.make_async_remote_copy(
            src_ref=csend.at[m, rows(q * 128, 128)], dst_ref=xrs.at[u, 3 - k],
            send_sem=cs_sem.at[m, k], recv_sem=xr_sem.at[u, 3 - k],
            device_id=((jnp.where(over_z, x, q) * 4 + jnp.where(over_z, q, z)) * 2 + yl, grid), device_id_type=MESH)

    def side_copy(u):
        return pltpu.make_async_remote_copy(
            src_ref=qsend.at[u], dst_ref=third.at[u, rows(z * 128, 128)],
            send_sem=q_sem.at[u], recv_sem=third_sem.at[u], device_id=(leaf_3, grid), device_id_type=MESH)

    def quarter_copy(u):
        return pltpu.make_async_remote_copy(
            src_ref=qsend.at[u], dst_ref=qrecv.at[u - 2, side],
            send_sem=q_sem.at[u], recv_sem=qr_sem.at[u - 2, side], device_id=(parent, grid), device_id_type=MESH)

    def top_copy(u):
        return pltpu.make_async_remote_copy(
            src_ref=qsend.at[u], dst_ref=top.at[rows(x * 128, 128)],
            send_sem=q_sem.at[u], recv_sem=top_sem, device_id=(16 * u - 17, grid), device_id_type=MESH)

    def ring_sum(u):
        for k in range(3):
            pltpu.make_async_copy(xrs.at[u, k], xrs.at[u, k], xr_sem.at[u, k]).wait()
        m = 2 - level + u
        base = jnp.where(u < 2, z, x) * 128
        qsend[u] = csend[m, rows(base, 128), :] + xrs[u, 0] + (xrs[u, 1] + xrs[u, 2])

        @pl.when(u < 2)
        def _():
            side_copy(u).start()

        @pl.when(level > 1)
        def _():
            for s in range(2):
                pltpu.make_async_copy(qrecv.at[u - 2, s], qrecv.at[u - 2, s], qr_sem.at[u - 2, s]).wait()
            qsend[u] = qsend[u] + (qrecv[u - 2, 0] + qrecv[u - 2, 1])

        @pl.when((u > 1) & (level < 3))
        def _():
            quarter_copy(u).start()

        @pl.when(level == 3)
        def _():
            pltpu.make_async_copy(ubuf.at[pl.ds(0, 480)], ubuf.at[pl.ds(0, 480)], u_sem.at[u]).wait()
            start = u * 512
            value = qsend[u]
            for s in range(4):
                value = value + ubuf[rows(start + s * 128, 128), :]
            qsend[u] = value
            top_copy(u).start()

    def take_3(k, dst):
        pltpu.make_async_copy(ubuf.at[pl.ds(0, 480)], ubuf.at[pl.ds(0, 480)], u_sem.at[k]).wait()
        pltpu.make_async_copy(third.at[k], third.at[k], third_sem.at[k]).wait()
        dst[...] = ubuf[k * 512:(k + 1) * 512, :] + third[k]

    def take_far(slot):
        pltpu.make_async_copy(grecv.at[slot], grecv.at[slot], g_sem.at[slot]).wait()
        accp[...] = accp[...] + grecv[slot]

    def dot2(a, which, part):
        high, low = split(a)
        return dot(high, vcat[which, part, :]) + dot(low, vh0[which, part, :])

    def stacked(value, which, part):
        left = lane_left(value.shape)
        high, low = split(value)
        vcat[which, part, :] = jnp.where(left, high.astype(F32), low.astype(F32)).astype(BF16)
        vh0[which, part, :] = jnp.where(left, high.astype(F32), 0.0).astype(BF16)

    def finished(product, m, i):
        total = product + turned(product)
        part = rows(i * 128, 128)
        csend[m, part, :] = jnp.where(lane_left((128, 128)), total[:128], total[128:])

    def head():
        squares[...] = jnp.zeros_like(squares)

        @pl.when(level == 1)
        def _():
            pltpu.make_async_copy(ubuf.at[pl.ds(0, 408)], ubuf.at[pl.ds(0, 408)], u_sem.at[0]).wait()
            for q in range(4):
                accp[q * 128:(q + 1) * 128, :] = ubuf[q * 136:q * 136 + 128, :]
            squares[...] = ubuf[128:136, :]

        @pl.when(level == 2)
        def _():
            pltpu.make_async_copy(ubuf.at[pl.ds(0, 448)], ubuf.at[pl.ds(0, 448)], u_sem.at[0]).wait()
            accp[...] = ubuf[0:512, :]

        @pl.when(level == 3)
        def _():
            take_3(0, accp)

        @pl.when(level > 3)
        def _():
            accp[...] = jnp.zeros_like(accp)

        @pl.when((level == 4) | (level == 6))
        def _():
            take_far(0)
            take_far(1)

        @pl.when(level == 4)
        def _():
            take_far(2)
            take_far(3)

        @pl.when(level > 4)
        def _():
            pltpu.make_async_copy(top, top, top_sem).wait()
            accp[...] = accp[...] + top[...]

        @pl.when(n_pan > 0)
        def _():
            sp_copy(jnp.int32(0)).wait()

        for k in range(4):
            packed = pl.ds(k * 128, 128)
            size = 136 if k == 3 else 128

            @pl.when(level > 1)
            def _():
                wait_child(0, k, size)
                accp[packed, :] = accp[packed, :] + crecv[0, packed, :]

            @pl.when((level > 1) & (level < 6))
            def _():
                wait_child(1, k, size)
                accp[packed, :] = accp[packed, :] + crecv[1, packed, :]

            left = lane_left((128, 128))
            for j, value in enumerate(unpacked(accp[packed, :])):
                part = pl.ds(k * 256 + j * 128, 128)
                right_side = rhsp[part, :]
                stacked(jnp.where(left, right_side, turned(right_side)) - value, 0, part)
            part = pl.ds(k * 256, 256)
            product = dot2(invb[part, k * 256:(k + 1) * 256], 0, part)
            if k > 0:
                product = product + racc[part, :]
            s_value = product + turned(product)
            stacked(s_value, 1, part)

            @pl.when(n_pan > 0)
            def _():
                if k < 3:
                    product = dot2(spb[0, :, k * 256:(k + 1) * 256], 1, part)
                    cacc[...] = product if k == 0 else cacc[...] + product
                else:
                    squares[...] = squares[...] + jnp.sum(s_value * s_value, axis=0, keepdims=True)
                    squares[...] = squares[...] + crecv_squares()
                    csend[0, pl.ds(512, 8), :] = squares[...]

                    @pl.when(level == 3)
                    def _():
                        take_3(1, pend)
                    for i in range(4):
                        out = pl.ds(i * 256, 256)
                        finished(cacc[out, :] + dot2(spb[0, out, k * 256:(k + 1) * 256], 1, part), 0, i)

                        @pl.when(level == 3)
                        def _():
                            up = pl.ds(i * 128, 128)
                            csend[0, up, :] = csend[0, up, :] + pend[up, :]
                        up_copy(i, 136 if i == 3 else 128).start()
            solv[:, k * 256:(k + 1) * 256] = jnp.transpose(s_value)[:64]
            if k < 3:
                squares[...] = squares[...] + jnp.sum(s_value * s_value, axis=0, keepdims=True)
                rest = slice((k + 1) * 256, 1024)
                product = dot2(invb[rest, k * 256:(k + 1) * 256], 0, part)
                racc[rest, :] = product if k == 0 else racc[rest, :] + product
            else:
                @pl.when(level == 6)
                def _():
                    squares[...] = squares[...] + jnp.sum(s_value * s_value, axis=0, keepdims=True) + crecv[0, pl.ds(512, 8), :]

        @pl.when(3 < n_pan)
        def _():
            sp_copy(jnp.int32(3)).start()
        pltpu.make_async_copy(solv, sol_hbm, out_sem.at[1]).start()

    def crecv_squares():
        return jnp.where(level > 1, crecv[0, pl.ds(512, 8), :] + crecv[1, pl.ds(512, 8), :], 0.0)

    def panel(m):
        sp_copy(m).wait()
        slot = lax.rem(m, 3)
        for i in range(4):
            out = pl.ds(i * 256, 256)
            finished(dot2(spb[slot, out, :], 1, slice(None)), m, i)
        far = (m == 1) & ((level == 2) | (level == 4))

        @pl.when(far)
        def _():
            far_copy().start()

        @pl.when(jnp.logical_not(far))
        def _():
            for k in range(1, 4):
                ring_copy(m, m + level - 2, k).start()

        @pl.when(m + 3 < n_pan)
        def _():
            sp_copy(m + 3).start()

    srhs_copy.wait()
    for k in range(4):
        rhsp[k * 256:(k + 1) * 256, :64] = jnp.transpose(rhsv[:, k * 256:(k + 1) * 256])
    inv_copy.wait()

    start_at = jnp.minimum(2 * (level - 1), 5)

    def phase(p, carry):
        @pl.when(p == 0)
        def _():
            first_sum_2()

        @pl.when(p < 4)
        def _():
            first_sum(p + 2)

        @pl.when(p == 1)
        def _():
            second_sum(1, 64)

        @pl.when((p > 1) & (p < 6))
        def _():
            second_sum(p, 32)

        @pl.when(p == start_at)
        def _():
            head()

        m = p - start_at

        @pl.when((m > 0) & (m < n_pan))
        def _():
            panel(m)

        u = m + level - 3

        @pl.when((level < 4) & (u < 4) & ((u > 1) | ((level == 1) & (u >= 0))))
        def _():
            ring_sum(u)
        return carry
    lax.fori_loop(0, 8, phase, 0)

    def width_copy(d):
        return pltpu.make_async_remote_copy(
            src_ref=wsend, dst_ref=wrecv, send_sem=w_sem.at[0], recv_sem=w_sem.at[1],
            device_id=(d, grid), device_id_type=MESH)

    @pl.when(level == 6)
    def _():
        wsend[0] = jnp.sqrt(squares[...] / (32 * 3072) + 1e-06)
        for d in range(31):
            width_copy(d).start()
        width_ref[...] = wsend[0]
        pltpu.make_async_copy(abuf.at[pl.ds(0, 248)], abuf.at[pl.ds(0, 248)], w_sem.at[0]).wait()

    @pl.when(level < 6)
    def _():
        width_copy(0).wait_recv()
        width_ref[...] = wrecv[0]

    pltpu.make_async_copy(abuf.at[pl.ds(0, 1016)], abuf.at[pl.ds(0, 1016)], a2a_sem.at[0]).wait()

    @pl.when(yh == 0)
    def _():
        to_sibling(0).wait_send()
        across().wait_send()

    @pl.when(c == 0)
    def _():
        to_sibling(1).wait_send()
    y_out.wait()
    pltpu.make_async_copy(solv, sol_hbm, out_sem.at[1]).wait()
    for t in range(6):
        u_copy(t).wait_send()
    for k in range(1, 4):
        first_copy(k).wait_send()
    wait_pieces(*piece_1)
    pair_copy().wait_send()
    for k in range(1, 4):
        y_copy(1, k, 64).wait_send()
    wait_pieces(*piece_2)
    for t in range(2, 6):
        for k in range(1, 4):
            rs_copy(t, k).wait_send()
            y_copy(t, k, 32).wait_send()
        wait_pieces(*piece_3(t))

    @pl.when(n_pan > 0)
    def _():
        for i in range(4):
            up_copy(i, 136 if i == 3 else 128).wait_send()

    @pl.when((level == 2) | (level == 4))
    def _():
        far_copy().wait_send()

    def sent(u, carry):
        for k in range(1, 4):
            ring_copy(2 - level + u, u, k).wait_send()
        pltpu.make_async_copy(qsend.at[u], qsend.at[u], q_sem.at[u]).wait()
        return carry
    lax.fori_loop(jnp.where(level == 1, 0, jnp.where(level < 4, 2, 4)), 4, sent, 0)


def write_out(y_in, s_in, w_in, y_out, s_out, w_out):
    y_out[...] = y_in[...]
    s_out[...] = s_in[...]
    w_out[...] = w_in[0, :64]


def local(rhs_rows, order, leaf_inverse, leaf_panels, panel_mask, sep_rhs, sep_inverse, sep_panels):
    vmem = pl.BlockSpec(memory_space=pltpu.VMEM)
    hbm = pl.BlockSpec(memory_space=pl.ANY)
    V = pltpu.VMEM
    leaf_y, solved, width = pl.pallas_call(
        kernel,
        out_shape=(
            jax.ShapeDtypeStruct((512, 256), F32),
            jax.ShapeDtypeStruct((64, 1024), F32),
            jax.ShapeDtypeStruct((8, 128), F32),
        ),
        in_specs=[vmem, pl.BlockSpec(memory_space=pltpu.SMEM), vmem] + [hbm] * 5,
        out_specs=(hbm, hbm, vmem),
        scratch_shapes=[
            V((1024, 128), F32), V((1024, 128), F32),
            V((512, 256), BF16), V((512, 256), BF16),
            V((2048, 512), F32),
            V((3, 512, 256), F32), V((2, 512, 256), F32), V((512, 256), F32),
            V((512, 256), F32), V((512, 256), BF16), V((512, 256), BF16),
            V((3, 1024, 512), F32),
            V((6, 1032, 128), F32), V((6, 1032, 128), F32), V((6, 1032, 128), F32),
            V((4, 3, 256, 128), F32),
            V((2, 4, 136, 128), F32), V((3, 2, 136, 128), F32), V((2, 136, 128), F32),
            V((5, 2, 256, 128), F32),
            V((512, 128), F32), V((5, 3, 2, 64, 128), F32),
            V((5, 2, 64, 128), F32), V((4, 512, 128), F32),
            V((2080, 128), F32),
            V((512, 128), F32), V((512, 128), F32), V((8, 128), F32),
            V((1024, 128), F32), V((1024, 128), F32),
            V((64, 1024), F32), V((1024, 128), F32),
            V((2, 1024, 128), BF16), V((2, 1024, 128), BF16),
            V((64, 1024), F32),
            V((1024, 1024), F32), V((3, 1024, 1024), F32),
            V((5, 520, 128), F32), V((2, 520, 128), F32), V((2, 512, 128), F32),
            V((4, 3, 128, 128), F32), V((4, 128, 128), F32), V((2, 2, 128, 128), F32), V((512, 128), F32),
            V((1, 8, 128), F32), V((1, 8, 128), F32),
            DMA((3,)), DMA((3,)), DMA((3,)), DMA((2,)), DMA((3,)), DMA((2,)), DMA, DMA((6,)), DMA((6,)),
            DMA((4, 3)), DMA((4, 3)),
            DMA((2,)), DMA((4, 3)), DMA((4,)), DMA((2, 2)), DMA,
            DMA((2,)), DMA((2, 3)), DMA((5, 2)), DMA((2,)), DMA((5, 3)), DMA((5, 3)), DMA((4,)), DMA((4,)), DMA((5, 4)), DMA((2, 4)), DMA((2,)), DMA((2,)),
        ],
        compiler_params=pltpu.CompilerParams(
            collective_id=0, has_side_effects=True, vmem_limit_bytes=62 * 2 ** 20),
        cost_estimate=pl.CostEstimate(flops=7 * 10 ** 9, bytes_accessed=44 * 10 ** 6, transcendentals=0),
    )(order.reshape(4, 128), panel_mask[0].T, rhs_rows, leaf_inverse, leaf_panels[0], sep_rhs[0].T, sep_inverse[0], sep_panels[0])
    leaf_y, solved, width = pl.pallas_call(
        write_out,
        out_shape=(
            jax.ShapeDtypeStruct((512, 256), F32),
            jax.ShapeDtypeStruct((64, 1024), F32),
            jax.ShapeDtypeStruct((64,), F32),
        ),
        in_specs=[vmem] * 3,
        out_specs=(vmem,) * 3,
    )(leaf_y, solved, width)
    return leaf_y, solved.T[None], width


def solution(mesh):
    placed = (
        P(("leaf", "grid"), None),
        P(("leaf", "grid")),
        P("leaf", "grid"),
        P("leaf", None, None, "grid"),
        P("leaf", None, "grid"),
        P("leaf", None, "grid"),
        P("leaf", None, None),
        P("leaf", None, None, None),
    )
    return jax.shard_map(
        local,
        mesh=mesh,
        in_specs=placed,
        out_specs=(P(("leaf", "grid"), None), P("leaf", None, "grid"), P("grid")),
        check_vma=False,
    )
```

```python
import jax
import jax.numpy as jnp
from jax import lax
from jax.experimental import pallas as pl
from jax.experimental.pallas import tpu as pltpu
from jax.sharding import PartitionSpec as P

F32, BF16 = jnp.float32, jnp.bfloat16
MESH = pl.DeviceIdType.MESH
DMA = pltpu.SemaphoreType.DMA


def split(value):
    high = value.astype(BF16)
    return high, (value - high.astype(F32)).astype(BF16)


def dot(a, b):
    return jnp.dot(a, b, preferred_element_type=F32)


def dot3(a, b_high, b_low):
    high, low = split(a)
    return dot(high, b_high) + dot(high, b_low) + dot(low, b_high)


def lane_left(shape):
    return lax.broadcasted_iota(jnp.int32, shape, 1) < 64


def turned(value):
    return pltpu.roll(value, 64, 1)


def packed_pair(top, bottom):
    left = lane_left(top.shape)
    return jnp.where(left, top, turned(bottom)), jnp.where(left, turned(top), bottom)


def unpacked(value):
    left = lane_left(value.shape)
    other = turned(value)
    return jnp.where(left, value, other), jnp.where(left, other, value)


def rows(start, size, unit=8):
    if isinstance(start, int):
        return pl.ds(start, size)
    return pl.ds(pl.multiple_of(start, unit), size)


def kernel(order_ref, mask_ref, rhs_ref, linv_hbm, lpan_hbm, srhs_hbm, sinv_hbm, span_hbm,
           leafy_hbm, sol_hbm, width_ref,
           abuf, xbuf, xh, xl, lbuf, zs, zr, za, ybuf, yh_s, yl_s, pbuf, own, snd, rcv, zrs,
           pk1, yr1, s1, pk, zpair, yrs, s2, grecv, ubuf, accp, pend, squares, cacc, racc, rhsv, rhsp, vcat, vh0, solv, invb, spb, csend, crecv, third, peer, xrs, qsend, qrecv, top, wsend, wrecv,
           ld_sem, lp_sem, sp_sem, a2a_sem, zs_sem, zr_sem, za_sem, us_sem, ur_sem, rs_sem, rr_sem,
           third_sem, peer_sem, xr_sem, q_sem, qr_sem, top_sem, ps_sem, y1_sem, p3_sem, pair_sem, ys_sem, yr_sem, g_sem, u_sem, cs_sem, cr_sem, w_sem, out_sem):
    leaf = lax.axis_index("leaf")
    grid = lax.axis_index("grid")
    me = leaf * 4 + grid
    yl = lax.rem(leaf, 2)
    z = lax.rem(lax.div(leaf, 2), 4)
    x = lax.div(leaf, 8)
    yh = lax.div(grid, 2)
    y = yh * 2 + yl
    c = lax.rem(grid, 2)
    sib = yh * 2 + 1 - c

    level = jnp.int32(1)
    for bit in range(1, 6):
        level = level + (lax.rem(leaf + 1, 2 ** bit) == 0).astype(jnp.int32)
    parent = jnp.int32(0)
    for tier in range(1, 6):
        size = 2 ** (tier + 1)
        parent = jnp.where(level == tier, lax.div(leaf, size) * size + 2 ** tier - 1, parent)
    side = (leaf > parent).astype(jnp.int32)
    above = jnp.int32(0)
    for tier in range(1, 5):
        size = 2 ** (tier + 2)
        above = jnp.where(level == tier, lax.div(leaf, size) * size + 2 ** (tier + 1) - 1, above)
    place = (parent > above).astype(jnp.int32) * 2 + side
    n_pan = 6 - level

    l_copy = pltpu.make_async_copy(linv_hbm, lbuf, ld_sem.at[0])
    l_copy.start()
    inv_copy = pltpu.make_async_copy(sinv_hbm, invb, ld_sem.at[1])
    srhs_copy = pltpu.make_async_copy(srhs_hbm, rhsv, ld_sem.at[2])

    def lp_copy(t):
        return pltpu.make_async_copy(lpan_hbm.at[t], pbuf.at[t % 3], lp_sem.at[t % 3])

    def sp_copy(m):
        slot = lax.rem(m, 3)
        return pltpu.make_async_copy(span_hbm.at[m], spb.at[slot], sp_sem.at[slot])

    rh, rl = split(rhs_ref[...])
    index = order_ref[...].astype(F32)
    index = jnp.transpose(jnp.concatenate([index, index], axis=0)).astype(jnp.int32)
    upper = lax.broadcasted_iota(jnp.int32, (16, 8, 128), 1) < 4
    for part in range(4):
        hot = (lax.broadcasted_iota(jnp.int32, (128, 512), 1) == index[:, part:part + 1]).astype(F32).astype(BF16)
        got = dot(hot, rh) + dot(hot, rl)
        first, second = got[:, :128].reshape(16, 8, 128), got[:, 128:].reshape(16, 8, 128)
        even = jnp.where(upper, first, pltpu.roll(second, 4, 1))
        odd = jnp.where(upper, pltpu.roll(first, 4, 1), second)
        abuf[rows(part * 256, 256), :] = jnp.stack([even, odd], axis=1).reshape(256, 128)

    barrier = pltpu.get_barrier_semaphore()

    def greet(k, carry):
        d = lax.rem(me + k, 128)
        pl.semaphore_signal(barrier, inc=1, device_id=(lax.div(d, 4), lax.rem(d, 4)), device_id_type=MESH)
        return carry

    lax.fori_loop(1, 128, greet, 0)
    for t in range(3):
        lp_copy(t).start()
    srhs_copy.start()
    pl.semaphore_wait(barrier, 127)

    def a2a(k, carry):
        d = lax.rem(me + k, 128)
        pltpu.make_async_remote_copy(
            src_ref=abuf.at[rows(d * 8, 8)], dst_ref=xbuf.at[rows(me * 8, 8)],
            send_sem=a2a_sem.at[0], recv_sem=a2a_sem.at[1],
            device_id=(lax.div(d, 4), lax.rem(d, 4)), device_id_type=MESH).start()
        return carry

    lax.fori_loop(1, 128, a2a, 0)
    xbuf[rows(me * 8, 8), :] = abuf[rows(me * 8, 8), :]
    inv_copy.start()
    for m in range(3):
        @pl.when(m < n_pan)
        def _():
            sp_copy(jnp.int32(m)).start()
    pltpu.make_async_copy(xbuf.at[pl.ds(0, 1016)], xbuf.at[pl.ds(0, 1016)], a2a_sem.at[1]).wait()

    raw = xbuf[...].reshape(64, 2, 8, 128)
    first, second = raw[:, 0], raw[:, 1]
    upper = lax.broadcasted_iota(jnp.int32, (64, 8, 128), 1) < 4
    left = jnp.where(upper, first, pltpu.roll(second, 4, 1)).reshape(512, 128)
    right = jnp.where(upper, pltpu.roll(first, 4, 1), second).reshape(512, 128)
    for half, value in enumerate((left, right)):
        high, low = split(value)
        xh[:, half * 128:(half + 1) * 128] = high
        xl[:, half * 128:(half + 1) * 128] = low

    l_copy.wait()

    def leaf_block(r, dst):
        def body(i, carry):
            dst[rows(i * 256, 256), :] = dot3(lbuf[rows(r * 512 + i * 256, 256), :], xh[...], xl[...])
            return carry
        lax.fori_loop(0, 2, body, 0)

    def to_sibling(slot):
        return pltpu.make_async_remote_copy(
            src_ref=zs.at[slot], dst_ref=zr.at[slot], send_sem=zs_sem.at[slot], recv_sem=zr_sem.at[slot],
            device_id=(leaf, sib), device_id_type=MESH)

    def across():
        return pltpu.make_async_remote_copy(
            src_ref=zs.at[2], dst_ref=za, send_sem=zs_sem.at[2], recv_sem=za_sem,
            device_id=(leaf, 2 + c), device_id_type=MESH)

    @pl.when(yh == 0)
    def _():
        leaf_block(3 - c, zs.at[0])
        to_sibling(0).start()
        leaf_block(2 + c, zs.at[2])
        to_sibling(0).wait_recv()
        zs[2] = zs[2] + zr[0]
        across().start()

        @pl.when(c == 0)
        def _():
            leaf_block(1, zs.at[1])
            to_sibling(1).start()

    @pl.when((yh == 1) & (c == 0))
    def _():
        leaf_block(3, zs.at[1])
        to_sibling(1).start()

    leaf_block(grid, ybuf)

    @pl.when(c == 1)
    def _():
        to_sibling(1).wait_recv()
        ybuf[...] = ybuf[...] + zr[1]

    @pl.when(yh == 1)
    def _():
        across().wait_recv()
        ybuf[...] = ybuf[...] + za[...]

    y_out = pltpu.make_async_copy(ybuf, leafy_hbm, out_sem.at[0])
    y_out.start()

    y_left, y_right = ybuf[:, :128], ybuf[:, 128:]
    for_0, for_1 = packed_pair(y_left, y_right)
    mine = jnp.where(c == 0, for_0, for_1)
    other = jnp.where(c == 0, for_1, for_0)
    own[0, pl.ds(1024, 8), :] = jnp.broadcast_to(jnp.sum(mine * mine, axis=0, keepdims=True), (8, 128))
    snd[0, pl.ds(1024, 8), :] = jnp.broadcast_to(jnp.sum(other * other, axis=0, keepdims=True), (8, 128))
    for half, value in enumerate((mine, other)):
        high, low = split(value)
        yh_s[:, half * 128:(half + 1) * 128] = high
        yl_s[:, half * 128:(half + 1) * 128] = low

    def u_copy(t):
        size = 1032 if t == 0 else 1024
        return pltpu.make_async_remote_copy(
            src_ref=snd.at[t, pl.ds(0, size)], dst_ref=rcv.at[t, pl.ds(0, size)],
            send_sem=us_sem.at[t], recv_sem=ur_sem.at[t], device_id=(leaf, sib), device_id_type=MESH)

    def send_pieces(src, base, size, to_leaf, sems, recv_sem):
        for to_yh in range(2):
            to_me = (to_leaf == leaf) & (yh == to_yh)

            @pl.when(to_me)
            def _():
                ubuf[rows(base, size), :] = src[to_yh]

            @pl.when(jnp.logical_not(to_me))
            def _():
                pltpu.make_async_remote_copy(
                    src_ref=src.at[to_yh], dst_ref=ubuf.at[rows(base, size)],
                    send_sem=sems.at[to_yh], recv_sem=recv_sem,
                    device_id=(to_leaf, to_yh * 2 + c), device_id_type=MESH).start()

    def wait_pieces(src, base, size, to_leaf, sems):
        for to_yh in range(2):
            @pl.when(jnp.logical_not((to_leaf == leaf) & (yh == to_yh)))
            def _():
                pltpu.make_async_copy(src.at[to_yh], src.at[to_yh], sems.at[to_yh]).wait()

    leaf_1 = leaf - yl
    leaf_2 = (x * 4 + z - lax.rem(z, 2)) * 2 + 1
    leaf_3 = x * 8 + 3
    half_z = lax.rem(z, 2)
    piece_1 = (s1, y * 136, 136, leaf_1, ps_sem)
    piece_2 = (s2.at[0], half_z * 256 + y * 64, 64, leaf_2, p3_sem.at[0])

    def piece_3(t):
        return (s2.at[t - 1, :, pl.ds(0, 32)], (t - 2) * 512 + z * 128 + y * 32, 32, leaf_3, p3_sem.at[t - 1])

    def first_copy(k):
        q = lax.rem(y + k, 4)
        return pltpu.make_async_remote_copy(
            src_ref=pk1.at[:, q], dst_ref=yr1.at[3 - k], send_sem=y1_sem.at[0, k - 1], recv_sem=y1_sem.at[1, 3 - k],
            device_id=((x * 4 + z) * 2 + lax.rem(q, 2), lax.div(q, 2) * 2 + c), device_id_type=MESH)

    def pair_copy():
        return pltpu.make_async_remote_copy(
            src_ref=own.at[1, rows((1 - half_z) * 512, 512)], dst_ref=zpair,
            send_sem=pair_sem.at[0], recv_sem=pair_sem.at[1],
            device_id=((x * 4 + z + 1 - 2 * half_z) * 2 + yl, grid), device_id_type=MESH)

    def rs_copy(t, k):
        at = z if t < 4 else x
        q = lax.rem(at + k, 4)
        to_leaf = (x * 4 + q) * 2 + yl if t < 4 else (q * 4 + z) * 2 + yl
        return pltpu.make_async_remote_copy(
            src_ref=own.at[t, rows(q * 256, 256)], dst_ref=zrs.at[t - 2, 3 - k],
            send_sem=rs_sem.at[t - 2, k - 1], recv_sem=rr_sem.at[t - 2, 3 - k],
            device_id=(to_leaf, grid), device_id_type=MESH)

    def y_copy(t, k, size):
        q = lax.rem(y + k, 4)
        return pltpu.make_async_remote_copy(
            src_ref=pk.at[t - 1, :, rows(q * size, size)], dst_ref=yrs.at[t - 1, 3 - k, :, pl.ds(0, size)],
            send_sem=ys_sem.at[t - 1, k - 1], recv_sem=yr_sem.at[t - 1, 3 - k],
            device_id=((x * 4 + z) * 2 + lax.rem(q, 2), lax.div(q, 2) * 2 + c), device_id_type=MESH)

    def spread(t):
        u_copy(t).wait_recv()
        if t == 0:
            def body(i, carry):
                base = i * 256
                top = own[t, rows(base, 128), :] + rcv[t, rows(base, 128), :]
                bottom = own[t, rows(base + 128, 128), :] + rcv[t, rows(base + 128, 128), :]
                p0, p1 = packed_pair(top, bottom)
                pk1[0, i, pl.ds(0, 128), :] = p0
                pk1[1, i, pl.ds(0, 128), :] = p1
                pk1[0, i, pl.ds(128, 8), :] = squares_1
                pk1[1, i, pl.ds(128, 8), :] = turned(squares_1)
                return carry
            squares_1 = own[0, pl.ds(1024, 8), :] + rcv[0, pl.ds(1024, 8), :]
            lax.fori_loop(0, 4, body, 0)
            for k in range(1, 4):
                first_copy(k).start()
        else:
            def body(i, carry):
                part = rows(i * 256, 256)
                own[t, part, :] = own[t, part, :] + rcv[t, part, :]
                return carry
            lax.fori_loop(0, 4, body, 0)
            if t == 1:
                pair_copy().start()
            else:
                for k in range(1, 4):
                    rs_copy(t, k).start()

    for t in range(6):
        lp_copy(t).wait()
        masks = [jnp.full((1, 256), mask_ref[b, t].astype(F32)).astype(BF16) for b in range(4)]
        masked = lambda ref: jnp.concatenate(
            [ref[b * 128:(b + 1) * 128, :] * masks[b] for b in range(4)], axis=0)
        y_high, y_low = masked(yh_s), masked(yl_s)
        xh[...] = y_high
        xl[...] = y_low

        def body(i, carry):
            part = rows(i * 256, 256)
            product = dot3(pbuf[t % 3, part, :], xh[...], xl[...])
            own[t, part, :] = product[:, :128]
            snd[t, part, :] = product[:, 128:]
            return carry
        lax.fori_loop(0, 4, body, 0)
        if t + 3 < 6:
            lp_copy(t + 3).start()
        u_copy(t).start()
        if t > 0:
            spread(t - 1)
    spread(5)
    for k in range(3):
        pltpu.make_async_copy(yr1.at[k], yr1.at[k], y1_sem.at[1, k]).wait()
    for part in range(2):
        s1[part] = pk1[part, y] + yr1[0, part] + (yr1[1, part] + yr1[2, part])
    send_pieces(*piece_1, u_sem.at[0])

    def ring_start(t, size):
        for k in range(1, 4):
            y_copy(t, k, size).start()

    def first_sum_2():
        pair_copy().wait_recv()
        for i in range(2):
            base = half_z * 512 + i * 256
            top = own[1, rows(base, 128), :] + zpair[pl.ds(i * 256, 128), :]
            bottom = own[1, rows(base + 128, 128), :] + zpair[pl.ds(i * 256 + 128, 128), :]
            p0, p1 = packed_pair(top, bottom)
            pk[0, 0, pl.ds(i * 128, 128), :] = p0
            pk[0, 1, pl.ds(i * 128, 128), :] = p1
        ring_start(1, 64)

    def first_sum(t):
        for k in range(3):
            pltpu.make_async_copy(zrs.at[t - 2, k], zrs.at[t - 2, k], rr_sem.at[t - 2, k]).wait()
        base = jnp.where(t < 4, z, x) * 256

        def total(start):
            value = own[t, rows(base + start, 128), :]
            for k in range(3):
                value = value + zrs[t - 2, k, pl.ds(start, 128), :]
            return value
        p0, p1 = packed_pair(total(0), total(128))
        pk[t - 1, 0, pl.ds(0, 128), :] = p0
        pk[t - 1, 1, pl.ds(0, 128), :] = p1
        ring_start(t, 32)

    def second_sum(t, size):
        for k in range(3):
            ref = yrs.at[t - 1, k, :, pl.ds(0, size)]
            pltpu.make_async_copy(ref, ref, yr_sem.at[t - 1, k]).wait()
        value = pk[t - 1, :, rows(y * size, size), :]
        for k in range(3):
            value = value + yrs[t - 1, k, :, pl.ds(0, size), :]
        s2[t - 1, :, pl.ds(0, size), :] = value
        if size == 64:
            send_pieces(*piece_2, u_sem.at[0])
        else:
            send_pieces(*piece_3(t), u_sem.at[t - 2])

    def up_copy(i, size):
        part = rows(i * 128, size)
        return pltpu.make_async_remote_copy(
            src_ref=csend.at[0, part], dst_ref=crecv.at[side, part],
            send_sem=cs_sem.at[0, i], recv_sem=cr_sem.at[side, i], device_id=(parent, grid), device_id_type=MESH)

    def peer_copy(i, size):
        part = rows(i * 128, size)
        return pltpu.make_async_remote_copy(
            src_ref=csend.at[0, part], dst_ref=peer.at[part],
            send_sem=cs_sem.at[0, i], recv_sem=peer_sem.at[i], device_id=(jnp.maximum(leaf - 8, 0), grid), device_id_type=MESH)

    def wait_child(s, i, size):
        part = rows(i * 128, size)
        pltpu.make_async_copy(csend.at[0, part], crecv.at[s, part], cr_sem.at[s, i]).wait()

    def far_copy():
        return pltpu.make_async_remote_copy(
            src_ref=csend.at[1, pl.ds(0, 512)], dst_ref=grecv.at[place],
            send_sem=cs_sem.at[1, 0], recv_sem=g_sem.at[place], device_id=(above, grid), device_id_type=MESH)

    def ring_copy(m, u, k):
        over_z = u < 2
        q = lax.rem(jnp.where(over_z, z, x) + k, 4)
        return pltpu.make_async_remote_copy(
            src_ref=csend.at[m, rows(q * 128, 128)], dst_ref=xrs.at[u, 3 - k],
            send_sem=cs_sem.at[m, k], recv_sem=xr_sem.at[u, 3 - k],
            device_id=((jnp.where(over_z, x, q) * 4 + jnp.where(over_z, q, z)) * 2 + yl, grid), device_id_type=MESH)

    def side_copy(u):
        return pltpu.make_async_remote_copy(
            src_ref=qsend.at[u], dst_ref=third.at[u, rows(z * 128, 128)],
            send_sem=q_sem.at[u], recv_sem=third_sem.at[u], device_id=(leaf_3, grid), device_id_type=MESH)

    def quarter_copy(u):
        return pltpu.make_async_remote_copy(
            src_ref=qsend.at[u], dst_ref=qrecv.at[u - 2, side],
            send_sem=q_sem.at[u], recv_sem=qr_sem.at[u - 2, side], device_id=(parent, grid), device_id_type=MESH)

    def top_copy(u):
        return pltpu.make_async_remote_copy(
            src_ref=qsend.at[u], dst_ref=top.at[rows(x * 128, 128)],
            send_sem=q_sem.at[u], recv_sem=top_sem, device_id=(16 * u - 17, grid), device_id_type=MESH)

    def ring_sum(u):
        for k in range(3):
            pltpu.make_async_copy(xrs.at[u, k], xrs.at[u, k], xr_sem.at[u, k]).wait()
        m = 2 - level + u
        base = jnp.where(u < 2, z, x) * 128
        qsend[u] = csend[m, rows(base, 128), :] + xrs[u, 0] + (xrs[u, 1] + xrs[u, 2])

        @pl.when(u < 2)
        def _():
            side_copy(u).start()

        @pl.when(level > 1)
        def _():
            for s in range(2):
                pltpu.make_async_copy(qrecv.at[u - 2, s], qrecv.at[u - 2, s], qr_sem.at[u - 2, s]).wait()
            qsend[u] = qsend[u] + (qrecv[u - 2, 0] + qrecv[u - 2, 1])

        @pl.when((u > 1) & (level < 3))
        def _():
            quarter_copy(u).start()

        @pl.when(level == 3)
        def _():
            pltpu.make_async_copy(ubuf.at[pl.ds(0, 480)], ubuf.at[pl.ds(0, 480)], u_sem.at[u]).wait()
            start = u * 512
            value = qsend[u]
            for s in range(4):
                value = value + ubuf[rows(start + s * 128, 128), :]
            qsend[u] = value
            top_copy(u).start()

    def take_3(k, dst):
        pltpu.make_async_copy(ubuf.at[pl.ds(0, 480)], ubuf.at[pl.ds(0, 480)], u_sem.at[k]).wait()
        pltpu.make_async_copy(third.at[k], third.at[k], third_sem.at[k]).wait()
        dst[...] = ubuf[k * 512:(k + 1) * 512, :] + third[k]

    def take_far(slot):
        pltpu.make_async_copy(grecv.at[slot], grecv.at[slot], g_sem.at[slot]).wait()
        accp[...] = accp[...] + grecv[slot]

    def dot2(a, which, part):
        high, low = split(a)
        return dot(high, vcat[which, part, :]) + dot(low, vh0[which, part, :])

    def stacked(value, which, part):
        left = lane_left(value.shape)
        high, low = split(value)
        vcat[which, part, :] = jnp.where(left, high.astype(F32), low.astype(F32)).astype(BF16)
        vh0[which, part, :] = jnp.where(left, high.astype(F32), 0.0).astype(BF16)

    def finished(product, m, i):
        total = product + turned(product)
        part = rows(i * 128, 128)
        csend[m, part, :] = jnp.where(lane_left((128, 128)), total[:128], total[128:])

    def head():
        squares[...] = jnp.zeros_like(squares)

        @pl.when(level == 1)
        def _():
            pltpu.make_async_copy(ubuf.at[pl.ds(0, 408)], ubuf.at[pl.ds(0, 408)], u_sem.at[0]).wait()
            for q in range(4):
                accp[q * 128:(q + 1) * 128, :] = ubuf[q * 136:q * 136 + 128, :]
            squares[...] = ubuf[128:136, :]

        @pl.when(level == 2)
        def _():
            pltpu.make_async_copy(ubuf.at[pl.ds(0, 448)], ubuf.at[pl.ds(0, 448)], u_sem.at[0]).wait()
            accp[...] = ubuf[0:512, :]

        @pl.when(level == 3)
        def _():
            take_3(0, accp)

        @pl.when(level > 3)
        def _():
            accp[...] = jnp.zeros_like(accp)

        @pl.when((level == 4) | (level == 6))
        def _():
            take_far(0)
            take_far(1)

        @pl.when(level == 4)
        def _():
            take_far(2)
            take_far(3)

        @pl.when(level > 4)
        def _():
            pltpu.make_async_copy(top, top, top_sem).wait()
            accp[...] = accp[...] + top[...]

        @pl.when(n_pan > 0)
        def _():
            sp_copy(jnp.int32(0)).wait()

        for k in range(4):
            packed = pl.ds(k * 128, 128)
            size = 136 if k == 3 else 128

            @pl.when(level > 1)
            def _():
                wait_child(0, k, size)
                accp[packed, :] = accp[packed, :] + crecv[0, packed, :]

            @pl.when((level > 1) & (level < 6) & (level != 4))
            def _():
                wait_child(1, k, size)
                accp[packed, :] = accp[packed, :] + crecv[1, packed, :]

            left = lane_left((128, 128))
            for j, value in enumerate(unpacked(accp[packed, :])):
                part = pl.ds(k * 256 + j * 128, 128)
                right_side = rhsp[part, :]
                stacked(jnp.where(left, right_side, turned(right_side)) - value, 0, part)
            part = pl.ds(k * 256, 256)
            product = dot2(invb[part, k * 256:(k + 1) * 256], 0, part)
            if k > 0:
                product = product + racc[part, :]
            s_value = product + turned(product)
            stacked(s_value, 1, part)

            @pl.when(n_pan > 0)
            def _():
                if k < 3:
                    product = dot2(spb[0, :, k * 256:(k + 1) * 256], 1, part)
                    cacc[...] = product if k == 0 else cacc[...] + product
                else:
                    squares[...] = squares[...] + jnp.sum(s_value * s_value, axis=0, keepdims=True)
                    squares[...] = squares[...] + crecv_squares()
                    csend[0, pl.ds(512, 8), :] = squares[...]

                    @pl.when(level == 3)
                    def _():
                        take_3(1, pend)
                    for i in range(4):
                        out = pl.ds(i * 256, 256)
                        finished(cacc[out, :] + dot2(spb[0, out, k * 256:(k + 1) * 256], 1, part), 0, i)

                        @pl.when(level == 3)
                        def _():
                            up = pl.ds(i * 128, 128)
                            csend[0, up, :] = csend[0, up, :] + pend[up, :]
                        size = 136 if i == 3 else 128

                        @pl.when(level != 3)
                        def _():
                            up_copy(i, size).start()

                        @pl.when((level == 3) & (lax.rem(x, 2) == 1))
                        def _():
                            peer_copy(i, size).start()

                        @pl.when((level == 3) & (lax.rem(x, 2) == 0))
                        def _():
                            peer_copy(i, size).wait_recv()
                            both = pl.ds(i * 128, size)
                            csend[0, both, :] = csend[0, both, :] + peer[both, :]
                            up_copy(i, size).start()
            solv[:, k * 256:(k + 1) * 256] = jnp.transpose(s_value)[:64]
            if k < 3:
                squares[...] = squares[...] + jnp.sum(s_value * s_value, axis=0, keepdims=True)
                rest = slice((k + 1) * 256, 1024)
                product = dot2(invb[rest, k * 256:(k + 1) * 256], 0, part)
                racc[rest, :] = product if k == 0 else racc[rest, :] + product
            else:
                @pl.when(level == 6)
                def _():
                    squares[...] = squares[...] + jnp.sum(s_value * s_value, axis=0, keepdims=True) + crecv[0, pl.ds(512, 8), :]

        @pl.when(3 < n_pan)
        def _():
            sp_copy(jnp.int32(3)).start()
        pltpu.make_async_copy(solv, sol_hbm, out_sem.at[1]).start()

    def crecv_squares():
        second = jnp.where(level == 4, 0.0, crecv[1, pl.ds(512, 8), :])
        return jnp.where(level > 1, crecv[0, pl.ds(512, 8), :] + second, 0.0)

    def panel(m):
        sp_copy(m).wait()
        slot = lax.rem(m, 3)
        for i in range(4):
            out = pl.ds(i * 256, 256)
            finished(dot2(spb[slot, out, :], 1, slice(None)), m, i)
        far = (m == 1) & ((level == 2) | (level == 4))

        @pl.when(far)
        def _():
            far_copy().start()

        @pl.when(jnp.logical_not(far))
        def _():
            for k in range(1, 4):
                ring_copy(m, m + level - 2, k).start()

        @pl.when(m + 3 < n_pan)
        def _():
            sp_copy(m + 3).start()

    srhs_copy.wait()
    for k in range(4):
        rhsp[k * 256:(k + 1) * 256, :64] = jnp.transpose(rhsv[:, k * 256:(k + 1) * 256])
    inv_copy.wait()

    start_at = jnp.minimum(2 * (level - 1), 5)

    def phase(p, carry):
        @pl.when(p == 0)
        def _():
            first_sum_2()

        @pl.when(p < 4)
        def _():
            first_sum(p + 2)

        @pl.when(p == 1)
        def _():
            second_sum(1, 64)

        @pl.when((p > 1) & (p < 6))
        def _():
            second_sum(p, 32)

        @pl.when(p == start_at)
        def _():
            head()

        m = p - start_at

        @pl.when((m > 0) & (m < n_pan))
        def _():
            panel(m)

        u = m + level - 3

        @pl.when((level < 4) & (u < 4) & ((u > 1) | ((level == 1) & (u >= 0))))
        def _():
            ring_sum(u)
        return carry
    lax.fori_loop(0, 8, phase, 0)

    def width_copy(d):
        return pltpu.make_async_remote_copy(
            src_ref=wsend, dst_ref=wrecv, send_sem=w_sem.at[0], recv_sem=w_sem.at[1],
            device_id=(d, grid), device_id_type=MESH)

    @pl.when(level == 6)
    def _():
        wsend[0] = jnp.sqrt(squares[...] / (32 * 3072) + 1e-06)
        for d in range(31):
            width_copy(d).start()
        width_ref[...] = wsend[0]
        pltpu.make_async_copy(abuf.at[pl.ds(0, 248)], abuf.at[pl.ds(0, 248)], w_sem.at[0]).wait()

    @pl.when(level < 6)
    def _():
        width_copy(0).wait_recv()
        width_ref[...] = wrecv[0]

    pltpu.make_async_copy(abuf.at[pl.ds(0, 1016)], abuf.at[pl.ds(0, 1016)], a2a_sem.at[0]).wait()

    @pl.when(yh == 0)
    def _():
        to_sibling(0).wait_send()
        across().wait_send()

    @pl.when(c == 0)
    def _():
        to_sibling(1).wait_send()
    y_out.wait()
    pltpu.make_async_copy(solv, sol_hbm, out_sem.at[1]).wait()
    for t in range(6):
        u_copy(t).wait_send()
    for k in range(1, 4):
        first_copy(k).wait_send()
    wait_pieces(*piece_1)
    pair_copy().wait_send()
    for k in range(1, 4):
        y_copy(1, k, 64).wait_send()
    wait_pieces(*piece_2)
    for t in range(2, 6):
        for k in range(1, 4):
            rs_copy(t, k).wait_send()
            y_copy(t, k, 32).wait_send()
        wait_pieces(*piece_3(t))

    @pl.when(n_pan > 0)
    def _():
        for i in range(4):
            up_copy(i, 136 if i == 3 else 128).wait_send()

    @pl.when((level == 2) | (level == 4))
    def _():
        far_copy().wait_send()

    def sent(u, carry):
        for k in range(1, 4):
            ring_copy(2 - level + u, u, k).wait_send()
        pltpu.make_async_copy(qsend.at[u], qsend.at[u], q_sem.at[u]).wait()
        return carry
    lax.fori_loop(jnp.where(level == 1, 0, jnp.where(level < 4, 2, 4)), 4, sent, 0)


def write_out(y_in, s_in, w_in, y_out, s_out, w_out):
    y_out[...] = y_in[...]
    s_out[...] = s_in[...]
    w_out[...] = w_in[0, :64]


def local(rhs_rows, order, leaf_inverse, leaf_panels, panel_mask, sep_rhs, sep_inverse, sep_panels):
    vmem = pl.BlockSpec(memory_space=pltpu.VMEM)
    hbm = pl.BlockSpec(memory_space=pl.ANY)
    V = pltpu.VMEM
    leaf_y, solved, width = pl.pallas_call(
        kernel,
        out_shape=(
            jax.ShapeDtypeStruct((512, 256), F32),
            jax.ShapeDtypeStruct((64, 1024), F32),
            jax.ShapeDtypeStruct((8, 128), F32),
        ),
        in_specs=[vmem, pl.BlockSpec(memory_space=pltpu.SMEM), vmem] + [hbm] * 5,
        out_specs=(hbm, hbm, vmem),
        scratch_shapes=[
            V((1024, 128), F32), V((1024, 128), F32),
            V((512, 256), BF16), V((512, 256), BF16),
            V((2048, 512), F32),
            V((3, 512, 256), F32), V((2, 512, 256), F32), V((512, 256), F32),
            V((512, 256), F32), V((512, 256), BF16), V((512, 256), BF16),
            V((3, 1024, 512), F32),
            V((6, 1032, 128), F32), V((6, 1032, 128), F32), V((6, 1032, 128), F32),
            V((4, 3, 256, 128), F32),
            V((2, 4, 136, 128), F32), V((3, 2, 136, 128), F32), V((2, 136, 128), F32),
            V((5, 2, 256, 128), F32),
            V((512, 128), F32), V((5, 3, 2, 64, 128), F32),
            V((5, 2, 64, 128), F32), V((4, 512, 128), F32),
            V((2080, 128), F32),
            V((512, 128), F32), V((512, 128), F32), V((8, 128), F32),
            V((1024, 128), F32), V((1024, 128), F32),
            V((64, 1024), F32), V((1024, 128), F32),
            V((2, 1024, 128), BF16), V((2, 1024, 128), BF16),
            V((64, 1024), F32),
            V((1024, 1024), F32), V((3, 1024, 1024), F32),
            V((5, 520, 128), F32), V((2, 520, 128), F32), V((2, 512, 128), F32), V((520, 128), F32),
            V((4, 3, 128, 128), F32), V((4, 128, 128), F32), V((2, 2, 128, 128), F32), V((512, 128), F32),
            V((1, 8, 128), F32), V((1, 8, 128), F32),
            DMA((3,)), DMA((3,)), DMA((3,)), DMA((2,)), DMA((3,)), DMA((2,)), DMA, DMA((6,)), DMA((6,)),
            DMA((4, 3)), DMA((4, 3)),
            DMA((2,)), DMA((4,)), DMA((4, 3)), DMA((4,)), DMA((2, 2)), DMA,
            DMA((2,)), DMA((2, 3)), DMA((5, 2)), DMA((2,)), DMA((5, 3)), DMA((5, 3)), DMA((4,)), DMA((4,)), DMA((5, 4)), DMA((2, 4)), DMA((2,)), DMA((2,)),
        ],
        compiler_params=pltpu.CompilerParams(
            collective_id=0, has_side_effects=True, vmem_limit_bytes=62 * 2 ** 20),
        cost_estimate=pl.CostEstimate(flops=7 * 10 ** 9, bytes_accessed=44 * 10 ** 6, transcendentals=0),
    )(order.reshape(4, 128), panel_mask[0].T, rhs_rows, leaf_inverse, leaf_panels[0], sep_rhs[0].T, sep_inverse[0], sep_panels[0])
    leaf_y, solved, width = pl.pallas_call(
        write_out,
        out_shape=(
            jax.ShapeDtypeStruct((512, 256), F32),
            jax.ShapeDtypeStruct((64, 1024), F32),
            jax.ShapeDtypeStruct((64,), F32),
        ),
        in_specs=[vmem] * 3,
        out_specs=(vmem,) * 3,
    )(leaf_y, solved, width)
    return leaf_y, solved.T[None], width


def solution(mesh):
    placed = (
        P(("leaf", "grid"), None),
        P(("leaf", "grid")),
        P("leaf", "grid"),
        P("leaf", None, None, "grid"),
        P("leaf", None, "grid"),
        P("leaf", None, "grid"),
        P("leaf", None, None),
        P("leaf", None, None, None),
    )
    return jax.shard_map(
        local,
        mesh=mesh,
        in_specs=placed,
        out_specs=(P(("leaf", "grid"), None), P("leaf", None, "grid"), P("grid")),
        check_vma=False,
    )
```
